32 devices in a mesh: dp: 8 (over y, x, core), seq: 4 (over z).
Axes of the slice: x: 2, y: 2, z: 4, core: 2. Of those that a mesh axis runs over, the one named last changes fastest.
Arguments:
- patches: bfloat16 [24, 532, 768], P('dp', 'seq'), may hold values from -6 to 6
- cotangent: bfloat16 [24, 532, 768], P('dp', 'seq'), may hold values from -6 to 6
- lengths: int32 [24], P('dp'), may hold values from 66 to 529, as said below
- script_ids: int32 [24], P('dp'), may hold values from 0 to 1, as said below
- key_mask: int32 [24, 532], P('dp'), may hold values 0 or 1
- norm1_gain: bfloat16 [768], P(('dp', 'seq')), may hold values from 0.5 to 1.5
- norm1_bias: bfloat16 [768], P(('dp', 'seq')), may hold values from -1 to 1
- w_qkv: bfloat16 [768, 2304], P(('dp', 'seq')), may hold values from -0.21875 to 0.21875
- q_bias: bfloat16 [768], P(('dp', 'seq')), may hold values from -1 to 1
- v_bias: bfloat16 [768], P(('dp', 'seq')), may hold values from -1 to 1
- w_attn_out: bfloat16 [768, 768], P(('dp', 'seq')), may hold values from -2.5 to 2.5
- attn_out_bias: bfloat16 [768], P(('dp', 'seq')), may hold values from -1 to 1
- norm2_gain: bfloat16 [768], P(('dp', 'seq')), may hold values from 0.5 to 1.5
- norm2_bias: bfloat16 [768], P(('dp', 'seq')), may hold values from -1 to 1
- w_up: bfloat16 [768, 3072], P(('dp', 'seq')), may hold values from -0.21875 to 0.21875
- up_bias: bfloat16 [3072], P(('dp', 'seq')), may hold values from -1 to 1
- w_down: bfloat16 [3072, 768], P(('dp', 'seq')), may hold values from -0.109375 to 0.109375
- down_bias: bfloat16 [768], P(('dp', 'seq')), may hold values from -1 to 1
- script_table: bfloat16 [2, 768], P(None, ('dp', 'seq')), may hold values from -3 to 3
Outputs:
- block_out: bfloat16 [24, 532, 768], P('dp', 'seq')
- input_grad: bfloat16 [24, 532, 768], P('dp', 'seq')
- grad_norm1_gain: float32 [768], P(('dp', 'seq'))
- grad_norm1_bias: float32 [768], P(('dp', 'seq'))
- grad_w_qkv: float32 [768, 2304], P(('dp', 'seq'))
- grad_q_bias: float32 [768], P(('dp', 'seq'))
- grad_v_bias: float32 [768], P(('dp', 'seq'))
- grad_w_attn_out: float32 [768, 768], P(('dp', 'seq'))
- grad_attn_out_bias: float32 [768], P(('dp', 'seq'))
- grad_norm2_gain: float32 [768], P(('dp', 'seq'))
- grad_norm2_bias: float32 [768], P(('dp', 'seq'))
- grad_w_up: float32 [768, 3072], P(('dp', 'seq'))
- grad_up_bias: float32 [3072], P(('dp', 'seq'))
- grad_w_down: float32 [3072, 768], P(('dp', 'seq'))
- grad_down_bias: float32 [768], P(('dp', 'seq'))
- grad_script_table: float32 [2, 768], P(None, ('dp', 'seq'))
The draws below stay inside these ranges and needn't reach their ends.
Inputs may be any that keep to these rules, and one draw needn't show every extreme that they name: `lengths`: a strip of a dense script (script_ids 1) holds 396 to 529 patches, a strip of a sparse one (script_ids 0) * 529 // 8 to 264; some strip has exactly 529. `script_ids`: 1 marks a strip of a dense script, 0 a sparse one.
All inputs are finite; a program needn't handle non-finite values. No bound on the sum of `key_mask` on one device may be relied on, other than what follows from the above.
Results may differ from the reference program's by a relative error of at most 0.012.
Values may be sent and summed in bfloat16 or wider, within the bound.
A program may use at most 128 MiB of HBM per device.

```python
import jax
import jax.numpy as jnp
from jax import lax

D = 768
H = 12
DH = 64
FF = 3072
L = 532
MAXLEN = 529
SCRIPTS = 2
STRIPS_DEV = 3
STRIPS = 24


def script_choice(key):
    base = jax.random.fold_in(key, 7)
    level_key, pick_key = jax.random.split(base)
    level = jax.random.randint(level_key, (STRIPS // STRIPS_DEV, 1), 0, 5)
    picks = jax.random.randint(pick_key, (STRIPS // STRIPS_DEV, STRIPS_DEV), 0, 4)
    chosen = (picks < level).astype(jnp.int32).reshape(STRIPS)
    return chosen.at[0].set(1)


def draw_script_ids(key, part):
    return script_choice(key)


def draw_lengths(key, part):
    dense_script = script_choice(key)
    length_key = jax.random.fold_in(key, 8)
    dense_key, sparse_key = jax.random.split(length_key)
    dense_len = jax.random.randint(dense_key, (STRIPS,), 3 * MAXLEN // 4, MAXLEN + 1)
    sparse_len = jax.random.randint(sparse_key, (STRIPS,), MAXLEN // 8, MAXLEN // 2 + 1)
    chosen = jnp.where(dense_script == 1, dense_len, sparse_len)
    return chosen.at[0].set(MAXLEN).astype(jnp.int32)


def plant(array, stream_key, low, top_value):
    extent = array.shape
    index_at = [jax.random.randint(jax.random.fold_in(stream_key, axis), (), 0, extent[axis]) for axis in range(len(extent))]
    array = array.at[tuple(index_at)].set(low)
    longest = extent.index(max(extent))
    index_at[longest] = (index_at[longest] + 1) % extent[longest]
    return array.at[tuple(index_at)].set(top_value)


def block_scale(rng, shape, cuts, smallest, largest):
    level = 1.0
    for axis_at, shards_of in cuts:
        heights = jax.random.uniform(jax.random.fold_in(jax.random.fold_in(rng, 6), axis_at), (shards_of,), jnp.float32, smallest / len(cuts), largest / len(cuts))
        level = level * jnp.repeat(jnp.exp(heights), shape[axis_at] // shards_of).reshape((-1,) + (1,) * (len(shape) - 1 - axis_at))
    return level


def gaussian(rng, dims, scale, reach, shards=(), kind=jnp.bfloat16):
    values = jax.random.normal(rng, dims, jnp.float32) * scale
    if len(shards) > 0:
        values = block_scale(rng, dims, shards, -0.22, 0.18) * values
    return jnp.clip(values, min=-reach, max=reach).astype(kind)


def setup_inputs(seed: int = 0) -> dict:
    keys = jax.random.split(jax.random.key(seed), 20)
    patches = gaussian(keys[0], (STRIPS, L, D), 1.0, 6.0, ((0, 8), (1, 4)))
    cotangent = gaussian(keys[1], (STRIPS, L, D), 1.0, 6.0, ((0, 8), (1, 4)))
    lengths = draw_lengths(jax.random.fold_in(keys[19], 71), 0)
    script_ids = draw_script_ids(jax.random.fold_in(keys[19], 71), 0)
    key_mask = plant((jax.random.randint(keys[4], (STRIPS, L), 0, 4) < 3).astype(jnp.int32), jax.random.fold_in(keys[4], 1), 0, 1)
    norm1_gain = jnp.clip(1.0 + 0.1 * jax.random.normal(keys[5], (D,), jnp.float32), 0.5, 1.5).astype(jnp.bfloat16)
    norm1_bias = gaussian(keys[6], (D,), 0.2, 1.0, ((0, 32),))
    w_qkv = gaussian(keys[7], (D, 3 * D), D ** -0.5, 0.21875, ((0, 32),))
    q_bias = gaussian(keys[8], (D,), 0.2, 1.0, ((0, 32),))
    v_bias = gaussian(keys[9], (D,), 0.2, 1.0, ((0, 32),))
    w_attn_out = gaussian(keys[10], (D, D), (D // 128) ** -0.5, 2.5, ((0, 32),))
    attn_out_bias = gaussian(keys[11], (D,), 0.2, 1.0, ((0, 32),))
    norm2_gain = jnp.clip(1.0 + 0.1 * jax.random.normal(keys[12], (D,), jnp.float32), 0.5, 1.5).astype(jnp.bfloat16)
    norm2_bias = gaussian(keys[13], (D,), 0.2, 1.0, ((0, 32),))
    w_up = gaussian(keys[14], (D, FF), D ** -0.5, 0.21875, ((0, 32),))
    up_bias = gaussian(keys[15], (FF,), 0.2, 1.0, ((0, 32),))
    w_down = gaussian(keys[16], (FF, D), FF ** -0.5, 0.109375, ((0, 32),))
    down_bias = gaussian(keys[17], (D,), 0.2, 1.0, ((0, 32),))
    script_table = gaussian(keys[18], (SCRIPTS, D), 0.5, 3.0, ((1, 32),))
    return {"patches": patches, "cotangent": cotangent, "lengths": lengths, "script_ids": script_ids, "key_mask": key_mask, "norm1_gain": norm1_gain, "norm1_bias": norm1_bias, "w_qkv": w_qkv, "q_bias": q_bias, "v_bias": v_bias, "w_attn_out": w_attn_out, "attn_out_bias": attn_out_bias, "norm2_gain": norm2_gain, "norm2_bias": norm2_bias, "w_up": w_up, "up_bias": up_bias, "w_down": w_down, "down_bias": down_bias, "script_table": script_table}


@jax.custom_vjp
def low(v):
    return lax.optimization_barrier(v.astype(jnp.bfloat16)).astype(jnp.float32)

@jax.custom_vjp
def low_back(v):
    return v

def low_keep(v):
    return (low(v), None)

def low_pass(kept, grad):
    return (grad,)

def back_keep(v):
    return (v, None)

def back_low(kept, grad):
    return (low(grad),)
low.defvjp(low_keep, low_pass)
low_back.defvjp(back_keep, back_low)
epsilon = 1e-06
highest = lax.Precision.HIGHEST

def layer_norm(rows, gain, shift):
    row_mean = lax.optimization_barrier(jnp.mean(rows, axis=-1, keepdims=True))
    centred = rows - row_mean
    row_var = lax.optimization_barrier(jnp.mean(centred * centred, axis=-1, keepdims=True))
    return centred * lax.rsqrt(row_var + epsilon) * gain + shift

def strip_forward(params, strip_rows, script_id, key_valid):
    gain_one, shift_one, w_project, bias_query, bias_value, w_output, bias_output, gain_two, shift_two, w_expand, bias_expand, w_reduce, bias_reduce, table = params
    resid = strip_rows + table[script_id]
    hidden1 = low(layer_norm(resid, gain_one, shift_one))
    bias_all = jnp.concatenate([bias_query, jnp.zeros_like(bias_query), bias_value])
    projected = low(low_back(jnp.dot(hidden1, w_project, precision=highest) + bias_all))
    queries = projected[:, 0:D].reshape(L, H, DH)
    key_heads = projected[:, D:2 * D].reshape(L, H, DH)
    values = projected[:, 2 * D:3 * D].reshape(L, H, DH)
    scores = low_back(jnp.einsum('qhd,khd->hqk', queries, key_heads, precision=highest) * DH ** (-0.5))
    scores = jnp.where(key_valid[None, None, :], scores, -1000000000.0)
    probs = low(jax.nn.softmax(scores, axis=-1))
    context = jnp.einsum('hqk,khd->qhd', probs, values, precision=highest).reshape(L, D)
    context = low(low_back(context))
    mid = resid + low_back(jnp.dot(context, w_output, precision=highest) + bias_output)
    hidden2 = low(layer_norm(mid, gain_two, shift_two))
    pre_act = low_back(jnp.dot(hidden2, w_expand, precision=highest) + bias_expand)
    activation = low(jax.nn.gelu(pre_act, approximate=False))
    return mid + low_back(jnp.dot(activation, w_reduce, precision=highest) + bias_reduce)

def reference(patches, cotangent, lengths, script_ids, key_mask, norm1_gain, norm1_bias, w_qkv, q_bias, v_bias, w_attn_out, attn_out_bias, norm2_gain, norm2_bias, w_up, up_bias, w_down, down_bias, script_table):
    params = tuple((weight.astype(jnp.float32) for weight in (norm1_gain, norm1_bias, w_qkv, q_bias, v_bias, w_attn_out, attn_out_bias, norm2_gain, norm2_bias, w_up, up_bias, w_down, down_bias, script_table)))
    positions = jnp.arange(L, dtype=jnp.int32)
    valid = (positions[None, :] == 0) | (positions[None, :] < lengths[:, None]) & (key_mask == 1)

    def strip_step(running, strip_item):
        strip_rows, script_id, key_valid, grad_rows = strip_item

        def forward(weights, rows_in):
            return strip_forward(weights, rows_in, script_id, key_valid)
        result, pullback = jax.vjp(forward, params, strip_rows.astype(jnp.float32))
        grad_params, grad_rows_in = pullback(grad_rows.astype(jnp.float32))
        running = jax.tree.map(lambda total, term: total + term, running, grad_params)
        return (running, (result.astype(jnp.bfloat16), grad_rows_in.astype(jnp.bfloat16)))
    zero_grads = jax.tree.map(jnp.zeros_like, params)
    totals, (outputs, input_grads) = lax.scan(strip_step, zero_grads, (patches, script_ids, valid, cotangent))
    return (outputs, input_grads, totals[0], totals[1], totals[2], totals[3], totals[4], totals[5], totals[6], totals[7], totals[8], totals[9], totals[10], totals[11], totals[12], totals[13])
```

```python
import functools

import jax
import jax.numpy as jnp
from jax import lax
from jax.experimental import pallas as pl
from jax.experimental.pallas import tpu as pltpu
from jax.sharding import PartitionSpec as P

DH = 64
MESH = pl.DeviceIdType.MESH
f32 = jnp.float32
bf16 = jnp.bfloat16
epsilon = 1e-06
WIRE = 12
RS = 8


def up(n, m):
    return (n + m - 1) // m * m


def ds(start, size, align=16):
    return pl.ds(pl.multiple_of(start, align), size)


class Place:
    def __init__(self, outer, groups):
        self.dp = lax.axis_index("dp")
        self.z = lax.axis_index("seq")
        self.groups = groups
        self.b = self.dp // outer
        self.c = self.b % 2
        self.x = (self.b // 2) % 2
        self.y = self.b // 4
        self.bx = self.b + 2 - 4 * self.x
        self.by = self.b + 4 - 8 * self.y
        self.bd = self.bx + 4 - 8 * self.y
        self.bc = self.b + 1 - 2 * self.c
        self.to_c = (self.dp + outer * (1 - 2 * self.c), self.z)
        self.to_x = (self.dp + outer * (2 - 4 * self.x), self.z)
        self.to_y = (self.dp + outer * (4 - 8 * self.y), self.z)

    def ahead(self, j):
        return (self.z + j) % self.groups

    def behind(self, j):
        return (self.z + self.groups - j) % self.groups

    def to_z(self, z):
        return (self.dp, z)

    def greet(self):
        barrier = pltpu.get_barrier_semaphore()
        peers = [self.to_c, self.to_x, self.to_y]
        peers += [self.to_z(self.ahead(j)) for j in range(1, self.groups)]
        for peer in peers:
            pl.semaphore_signal(barrier, inc=1, device_id=peer, device_id_type=MESH)
        pl.semaphore_wait(barrier, len(peers))


def remote(src, dst, send, recv, to):
    return pltpu.make_async_remote_copy(
        src_ref=src, dst_ref=dst, send_sem=send, recv_sem=recv, device_id=to, device_id_type=MESH
    )


class Gather:
    def __init__(self, place, index, shard, full, stage, send, recv):
        self.p, self.i, self.shard, self.full, self.stage = place, index, shard, full, stage
        self.send, self.recv = send, recv
        self.r = shard.shape[0] if len(shard.shape) == 2 else 1
        self.slab = len(full.shape) == 3
        self.r = 1 if self.slab else shard.shape[0]
        self.u = self.r * place.groups

    def rows(self, block, part=0, parts=1):
        size = self.u // parts
        align = 1 if self.slab else 16
        return self.full.at[ds(block * self.u + part * size, size, align)]

    def copy(self, k, src, dst, to):
        return remote(src, dst, self.send.at[self.i, k], self.recv.at[self.i, k], to)

    def z_copy(self, j, owner):
        p = self.p
        if self.stage is not None:
            dst = self.stage.at[owner]
            src = self.shard
        elif self.slab:
            dst = self.full.at[p.b * p.groups + owner]
            src = self.shard
        else:
            dst = self.full.at[ds((p.b * p.groups + owner) * self.r, self.r)]
            src = self.shard
        return self.copy(j - 1, src, dst, p.to_z(p.ahead(j)))

    def z_start(self):
        p = self.p
        for j in range(1, p.groups):
            self.z_copy(j, p.z).start()
        if self.stage is not None:
            self.stage[p.z] = self.shard[...]
        elif self.slab:
            self.full[p.b * p.groups + p.z] = self.shard[...]
        else:
            self.full[ds((p.b * p.groups + p.z) * self.r, self.r), :] = self.shard[...]

    def xy(self, k):
        p = self.p
        own, bx, by, bd = p.b, p.bx, p.by, p.bd
        return {
            3: lambda: self.copy(3, self.rows(own), self.rows(own), p.to_x),
            4: lambda: self.copy(4, self.rows(own), self.rows(own), p.to_y),
            5: lambda: self.copy(5, self.rows(by, 1, 2), self.rows(by, 1, 2), p.to_x),
            6: lambda: self.copy(6, self.rows(bx, 0, 2), self.rows(bx, 0, 2), p.to_y),
            7: lambda: self.copy(7, self.rows(own), self.rows(own), p.to_c),
            8: lambda: self.copy(8, self.rows(bx), self.rows(bx), p.to_c),
            9: lambda: self.copy(9, self.rows(by), self.rows(by), p.to_c),
            10: lambda: self.copy(10, self.rows(bd, 0, 2), self.rows(bd, 0, 2), p.to_c),
            11: lambda: self.copy(11, self.rows(bd, 1, 2), self.rows(bd, 1, 2), p.to_c),
        }[k]()

    def z_finish(self):
        p = self.p
        for j in range(1, p.groups):
            self.z_copy(j, p.behind(j)).wait_recv()
        if self.stage is not None:
            width = self.full.shape[1]
            step = 768
            for at in range(0, width, step):
                block = self.stage[:, :, at : at + step].astype(f32)
                block = block.reshape(self.u, step).astype(bf16)
                self.full[ds(p.b * self.u, self.u), at : at + step] = block
        for k in (3, 4, 7):
            self.xy(k).start()

    def mid(self):
        self.xy(3).wait_recv()
        self.xy(6).start()
        self.xy(8).start()
        self.xy(4).wait_recv()
        self.xy(5).start()
        self.xy(9).start()

    def diag(self):
        self.xy(6).wait_recv()
        self.xy(10).start()
        self.xy(5).wait_recv()
        self.xy(11).start()

    def finish(self):
        p = self.p
        for k in (7, 8, 9, 10, 11):
            self.xy(k).wait_recv()
        for j in range(1, p.groups):
            self.z_copy(j, p.z).wait_send()
        for k in range(3, WIRE):
            self.xy(k).wait_send()


class Rows:
    def __init__(self, place, parts, strip, send, recv):
        self.p, self.parts, self.strip, self.send, self.recv = place, parts, strip, send, recv
        self.strips, self.rows = parts.shape[0], parts.shape[1]
        self.home = place.z - place.c
        self.is_home = (self.home >= 0) & (self.home < self.strips)

    def clip(self, s):
        return jnp.clip(s, 0, self.strips - 1)

    def at(self, z):
        return self.strip.at[ds(z * self.rows, self.rows)]

    def inward(self, j, owner, s):
        return remote(
            self.parts.at[s], self.at(owner), self.send.at[j - 1], self.recv.at[j - 1],
            self.p.to_z(self.p.ahead(j)),
        )

    def in_start(self):
        p = self.p
        for j in range(1, p.groups):
            s = p.ahead(j) - p.c

            @pl.when((s >= 0) & (s < self.strips))
            def _():
                self.inward(j, p.z, self.clip(s)).start()

        @pl.when(self.is_home)
        def _():
            self.strip[ds(p.z * self.rows, self.rows), :] = self.parts[self.clip(self.home)]

        @pl.when(jnp.logical_not(self.is_home))
        def _():
            self.strip[...] = jnp.zeros_like(self.strip)

    def in_finish(self):
        p = self.p

        @pl.when(self.is_home)
        def _():
            for j in range(1, p.groups):
                self.inward(j, p.behind(j), 0).wait_recv()

    def in_sent(self):
        p = self.p
        for j in range(1, p.groups):
            s = p.ahead(j) - p.c

            @pl.when((s >= 0) & (s < self.strips))
            def _():
                self.inward(j, p.z, self.clip(s)).wait_send()

    def outward(self, j, s):
        z = self.p.ahead(j)
        return remote(
            self.at(z), self.parts.at[s], self.send.at[j - 1], self.recv.at[j - 1], self.p.to_z(z)
        )

    def out_start(self):
        p = self.p

        @pl.when(self.is_home)
        def _():
            home = self.clip(self.home)
            for j in range(1, p.groups):
                self.outward(j, home).start()
            self.parts[home] = self.strip[ds(p.z * self.rows, self.rows), :]

    def out_finish(self):
        p = self.p
        for j in range(1, p.groups):
            s = p.behind(j) - p.c

            @pl.when((s >= 0) & (s < self.strips))
            def _():
                self.outward(j, self.clip(s)).wait_recv()

        @pl.when(self.is_home)
        def _():
            for j in range(1, p.groups):
                self.outward(j, self.clip(self.home)).wait_send()


def add_into(dst, terms, rows):
    step = 16

    def body(i, carry):
        at = ds(i * step, step)
        total = terms[0][at, :].astype(f32)
        for term in terms[1:]:
            total += term[at, :].astype(f32)
        dst[at, :] = total.astype(dst.dtype)
        return carry

    lax.fori_loop(0, rows // step, body, 0)


class Scatter:
    def __init__(self, place, index, part, core, r1, r2, q1, q2, zs, zr, out, send, recv):
        self.p, self.i = place, index
        self.part, self.core, self.r1, self.r2, self.q1, self.q2 = part, core, r1, r2, q1, q2
        self.zs, self.zr, self.out = zs, zr, out
        self.send, self.recv = send, recv
        self.u = part.shape[3]
        self.r = self.u // place.groups

    def copy(self, k, src, dst, to):
        return remote(src, dst, self.send.at[self.i, k], self.recv.at[self.i, k], to)

    def wire(self, k):
        p, u = self.p, self.u
        first, second = pl.ds(0, u // 2), pl.ds(u // 2, u // 2)
        if k == 0:
            return self.copy(0, self.part.at[:, :, 1 - p.c], self.core, p.to_c)
        if k == 1:
            return self.copy(1, self.core.at[:, 1 - p.x, first], self.r1, p.to_x)
        if k == 2:
            return self.copy(2, self.core.at[1 - p.y, :, second], self.r2, p.to_y)
        if k == 3:
            return self.copy(3, self.r1.at[1 - p.y], self.q1, p.to_y)
        if k == 4:
            return self.copy(4, self.r2.at[1 - p.x], self.q2, p.to_x)
        j = k - 4
        z = p.ahead(j)
        return self.copy(k, self.zs.at[z], self.zr.at[j - 1], p.to_z(z))

    def start(self):
        self.wire(0).start()

    def core_add(self):
        p, u = self.p, self.u
        self.wire(0).wait_recv()
        for y in range(2):
            for x in range(2):
                add_into(
                    self.core.at[y, x], (self.core.at[y, x], self.part.at[y, x, p.c]), u
                )
        self.wire(1).start()
        self.wire(2).start()

    def pass_on(self):
        p, u = self.p, self.u
        first, second = pl.ds(0, u // 2), pl.ds(u // 2, u // 2)
        self.wire(1).wait_recv()
        add_into(
            self.r1.at[1 - p.y], (self.r1.at[1 - p.y], self.core.at[1 - p.y, p.x, first]), u // 2
        )
        self.wire(3).start()
        self.wire(2).wait_recv()
        add_into(
            self.r2.at[1 - p.x], (self.r2.at[1 - p.x], self.core.at[p.y, 1 - p.x, second]), u // 2
        )
        self.wire(4).start()

    def z_start(self):
        p, u, r = self.p, self.u, self.r
        half = u // 2
        self.wire(3).wait_recv()
        self.wire(4).wait_recv()
        per = p.groups // 2
        for h, (mine, got) in enumerate(((self.r1, self.q1), (self.r2, self.q2))):
            here = p.y if h == 0 else p.x
            for at in range(0, self.out.shape[1], 768):
                cols = pl.ds(at, 768)
                total = self.core[p.y, p.x, pl.ds(h * half, half), cols].astype(f32)
                total += mine[here, :, cols].astype(f32) + got[:, cols].astype(f32)
                slabs = total.reshape(per, r, 768)
                self.zs[pl.ds(h * per, per), :, cols] = slabs.astype(bf16)
        for j in range(1, p.groups):
            self.wire(4 + j).start()

    def finish(self):
        p = self.p
        for j in range(1, p.groups):
            self.wire(4 + j).wait_recv()
        for at in range(0, self.out.shape[1], 768):
            cols = pl.ds(at, 768)
            total = self.zs[p.z, :, cols].astype(f32)
            for j in range(1, p.groups):
                total += self.zr[j - 1, :, cols].astype(f32)
            self.out[:, cols] = total
        for k in range(RS):
            self.wire(k).wait_send()


class Tally:
    def __init__(self, place, value, got, send, recv):
        self.p, self.value, self.got, self.send, self.recv = place, value, got, send, recv

    def copy(self, k):
        p = self.p
        to = (p.to_c, p.to_x, p.to_y)[k] if k < 3 else p.to_z(p.ahead(k - 2))
        return remote(
            self.value.at[min(k, 3)], self.got.at[k], self.send.at[k], self.recv.at[k], to
        )

    def start(self):
        self.copy(0).start()

    def step(self, k):
        self.copy(k).wait_recv()
        self.value[k + 1] = self.value[k] + self.got[k]
        if k < 2:
            self.copy(k + 1).start()
        else:
            for j in range(1, self.p.groups):
                self.copy(2 + j).start()

    def finish(self):
        total = self.value[3]
        for j in range(1, self.p.groups):
            self.copy(2 + j).wait_recv()
            total += self.got[2 + j]
        for k in range(2 + self.p.groups):
            self.copy(k).wait_send()
        return total


def gather_kernel(outer, groups, *refs):
    (small, s_qkv, s_out, s_up, s_down, patches, cotangent) = refs[:7]
    (f_small, f_qkv, f_out, f_up, f_down, strip, strip_cot) = refs[7:14]
    (g_qkv, g_out, g_up, xp, cp, send, recv, xsend, xrecv, csend, crecv) = refs[14:]
    p = Place(outer, groups)
    real = patches.shape[1]
    for src, dst in ((patches, xp), (cotangent, cp)):
        dst[...] = jnp.zeros_like(dst)
        for s in range(src.shape[0]):
            dst[s, :real] = src[s]
    gs = [
        Gather(p, i, shard, full, stage, send, recv)
        for i, (shard, full, stage) in enumerate(
            (
                (small, f_small, None),
                (s_qkv, f_qkv, g_qkv),
                (s_out, f_out, g_out),
                (s_up, f_up, g_up),
                (s_down, f_down, None),
            )
        )
    ]
    xs = Rows(p, xp, strip, xsend, xrecv)
    cs = Rows(p, cp, strip_cot, csend, crecv)
    p.greet()
    gs[0].z_start()
    gs[1].z_start()
    xs.in_start()
    gs[0].z_finish()
    gs[1].z_finish()
    gs[2].z_start()
    gs[3].z_start()
    gs[0].mid()
    gs[2].z_finish()
    gs[1].mid()
    gs[3].z_finish()
    gs[4].z_start()
    cs.in_start()
    gs[0].diag()
    gs[1].diag()
    gs[2].mid()
    gs[2].diag()
    gs[4].z_finish()
    gs[3].mid()
    gs[3].diag()
    gs[4].mid()
    gs[4].diag()
    for g in gs:
        g.finish()
    for m in (xs, cs):
        m.in_finish()
        m.in_sent()


def scatter_kernel(outer, groups, *refs):
    nw = 4
    grads = refs[:nw]
    tally, strip_out, strip_grad = refs[nw : nw + 3]
    outs = refs[nw + 3 : nw + 3 + nw]
    o_tally, o_out, o_grad = refs[2 * nw + 3 : 2 * nw + 6]
    scr = refs[2 * nw + 6 :]
    bufs = [scr[7 * i : 7 * i + 7] for i in range(nw)]
    (yp, gp, value, got, send, recv, tsend, trecv, ysend, yrecv, gsend, grecv) = scr[7 * nw :]
    p = Place(outer, groups)
    real = o_out.shape[1]
    ss = [
        Scatter(p, i, grads[i], *bufs[i], outs[i], send, recv) for i in range(nw)
    ]
    ys = Rows(p, yp, strip_out, ysend, yrecv)
    xs = Rows(p, gp, strip_grad, gsend, grecv)
    ts = Tally(p, value, got, tsend, trecv)
    p.greet()
    value[0] = tally[...]
    ts.start()
    for s in ss:
        s.start()
    ys.out_start()
    xs.out_start()
    ss[0].core_add()
    ts.step(0)
    ss[1].core_add()
    ts.step(1)
    ss[0].pass_on()
    ts.step(2)
    ss[2].core_add()
    ss[1].pass_on()
    ss[0].z_start()
    ss[3].core_add()
    ss[1].z_start()
    ss[2].pass_on()
    ss[3].pass_on()
    ss[2].z_start()
    ss[3].z_start()
    o_tally[...] = ts.finish()
    for s in ss:
        s.finish()
    ys.out_finish()
    xs.out_finish()
    for buf, out in ((yp, o_out), (gp, o_grad)):
        for s in range(out.shape[0]):
            out[s] = buf[s, :real]


def norm_forward(rows, gain, shift):
    row_mean = jnp.mean(rows, axis=-1, keepdims=True)
    centred = rows - row_mean
    row_var = jnp.mean(centred * centred, axis=-1, keepdims=True)
    inv_std = lax.rsqrt(row_var + epsilon)
    normal_rows = centred * inv_std
    return (normal_rows * gain + shift, normal_rows, inv_std)


def norm_backward(grad_rows, normal_rows, inv_std, gain):
    scaled = grad_rows * gain
    back = inv_std * (
        scaled
        - jnp.mean(scaled, axis=-1, keepdims=True)
        - normal_rows * jnp.mean(scaled * normal_rows, axis=-1, keepdims=True)
    )
    return (back, jnp.sum(grad_rows * normal_rows, axis=0), jnp.sum(grad_rows, axis=0))


def layer(x, cot, sid, valid, vecs, up_bias, w_qkv, w_out, w_up, w_down):
    rows, d = x.shape
    heads = d // DH
    (g1, b1, qb, vb, ob, g2, b2, db, t0, t1) = [vecs[i][None] for i in range(10)]
    resid = x.astype(f32) + jnp.where(sid == 1, t1, t0)
    n1, xh1, r1 = norm_forward(resid, g1, b1)
    h1 = n1.astype(bf16)
    bias = jnp.concatenate([qb, jnp.zeros_like(qb), vb], axis=1)
    qkv = (jnp.dot(h1, w_qkv, preferred_element_type=f32) + bias).astype(bf16)
    q, k, v = (qkv[:, i * d : (i + 1) * d].reshape(rows, heads, DH) for i in range(3))
    s = jnp.einsum("qhd,khd->hqk", q, k, preferred_element_type=f32) * DH**-0.5
    s = jnp.where(valid[None, None, :], s, -1e9)
    probs = jax.nn.softmax(s, axis=-1)
    pl_ = probs.astype(bf16)
    ctx = jnp.einsum("hqk,khd->qhd", pl_, v, preferred_element_type=f32).reshape(rows, d).astype(bf16)
    mid = resid + jnp.dot(ctx, w_out, preferred_element_type=f32) + ob
    n2, xh2, r2 = norm_forward(mid, g2, b2)
    h2 = n2.astype(bf16)
    pre = jnp.dot(h2, w_up, preferred_element_type=f32) + up_bias
    act = jax.nn.gelu(pre, approximate=False).astype(bf16)
    out = (mid + jnp.dot(act, w_down, preferred_element_type=f32) + db).astype(bf16)
    cf = cot.astype(f32)
    dw_down = jnp.dot(act.T, cot, preferred_element_type=f32)
    gact = jnp.dot(cot, w_down.T, preferred_element_type=f32)
    cum = 0.5 * (1.0 + lax.erf(pre * 2.0**-0.5))
    den = jnp.exp(-0.5 * pre * pre) * (2.0 * jnp.pi) ** -0.5
    gpre = (gact * (cum + pre * den)).astype(bf16)
    dw_up = jnp.dot(h2.T, gpre, preferred_element_type=f32)
    gh2 = jnp.dot(gpre, w_up.T, preferred_element_type=f32)
    back, dg2, db2 = norm_backward(gh2, xh2, r2, g2)
    gmid = cf + back
    gb = gmid.astype(bf16)
    dw_out = jnp.dot(ctx.T, gb, preferred_element_type=f32)
    gctx = jnp.dot(gb, w_out.T, preferred_element_type=f32).astype(bf16).reshape(rows, heads, DH)
    dv = jnp.einsum("hqk,qhd->khd", pl_, gctx, preferred_element_type=f32)
    dp = jnp.einsum("qhd,khd->hqk", gctx, v, preferred_element_type=f32)
    dsc = (probs * (dp - jnp.sum(probs * dp, axis=-1, keepdims=True))).astype(bf16)
    dq = jnp.einsum("hqk,khd->qhd", dsc, k, preferred_element_type=f32) * DH**-0.5
    dk = jnp.einsum("hqk,qhd->khd", dsc, q, preferred_element_type=f32) * DH**-0.5
    dqkv = jnp.concatenate([t.reshape(rows, d) for t in (dq, dk, dv)], axis=1).astype(bf16)
    dw_qkv = jnp.dot(h1.T, dqkv, preferred_element_type=f32)
    gh1 = jnp.dot(dqkv, w_qkv.T, preferred_element_type=f32)
    back1, dg1, db1 = norm_backward(gh1, xh1, r1, g1)
    gres = gmid + back1
    tsum = jnp.sum(gres, axis=0)
    sums = [
        dg1,
        db1,
        jnp.sum(dqkv[:, :d].astype(f32), axis=0),
        jnp.sum(dqkv[:, 2 * d :].astype(f32), axis=0),
        jnp.sum(gb.astype(f32), axis=0),
        dg2,
        db2,
        jnp.sum(cf, axis=0),
        jnp.where(sid == 1, 0.0, tsum),
        jnp.where(sid == 1, tsum, 0.0),
    ]
    tally = jnp.concatenate(
        [jnp.stack(sums), jnp.sum(gpre.astype(f32), axis=0).reshape(-1, d), jnp.zeros((2, d), f32)]
    )
    return out, gres.astype(bf16), dw_qkv, dw_out, dw_up, dw_down, tally


def on_device(outer, groups, *args):
    (patches, cotangent, lengths, script_ids, key_mask, norm1_gain, norm1_bias, w_qkv, q_bias,
     v_bias, w_attn_out, attn_out_bias, norm2_gain, norm2_bias, w_up, up_bias, w_down, down_bias,
     script_table) = args
    strips, part_rows, d = patches.shape
    hidden = w_up.shape[1]
    parts = 8 * groups
    pad_rows = up(part_rows, 16)
    rows = groups * pad_rows
    vectors = [norm1_gain, norm1_bias, q_bias, v_bias, attn_out_bias, norm2_gain, norm2_bias, down_bias, script_table[0], script_table[1]]
    weights = [w_qkv, w_attn_out, w_up, w_down]
    if outer > 1:
        dp_size = outer * 8
        mates = [[g * outer + i for i in range(outer)] for g in range(8)]
        seq = lax.axis_index("seq")

        def widen(a):
            a = lax.all_gather(a, ("seq",), axis=0, tiled=True)
            a = lax.all_gather(a, "dp", axis=0, tiled=True, axis_index_groups=mates)
            n = a.shape[0] // groups
            return lax.dynamic_slice_in_dim(a, seq * n, n, axis=0)

        vectors = [widen(a) for a in vectors]
        up_bias = widen(up_bias)
        weights = [widen(a) for a in weights]
    c = vectors[0].shape[0]
    small = jnp.concatenate(
        [
            jnp.pad(jnp.stack(vectors), ((0, 0), (0, 128 - c))),
            jnp.pad(up_bias[None], ((0, 5), (0, 128 - up_bias.shape[0]))),
        ]
    )
    vm = pl.BlockSpec(memory_space=pltpu.VMEM)
    sems = pltpu.SemaphoreType.DMA
    shapes = [(d, 3 * d), (d, d), (d, hidden), (hidden, d)]
    full = pl.pallas_call(
        functools.partial(gather_kernel, outer, groups),
        out_shape=[jax.ShapeDtypeStruct((parts, 16, 128), bf16)]
        + [jax.ShapeDtypeStruct(s, bf16) for s in shapes]
        + [jax.ShapeDtypeStruct((rows, d), bf16)] * 2,
        in_specs=[vm] * 7,
        out_specs=[vm] * 7,
        scratch_shapes=[pltpu.VMEM((groups, *w.shape), bf16) for w in weights[:3]]
        + [pltpu.VMEM((strips, pad_rows, d), bf16)] * 2
        + [sems((5, WIRE)), sems((5, WIRE))]
        + [sems((groups - 1,))] * 4,
        compiler_params=pltpu.CompilerParams(
            collective_id=0, has_side_effects=True, vmem_limit_bytes=60 * 2**20
        ),
    )(small, *weights, patches, cotangent)
    f_small, f_qkv, f_out, f_up, f_down, x, cot = full
    vecs = jnp.swapaxes(f_small[:, :10, :c], 0, 1).reshape(10, d).astype(f32)
    up_full = f_small[:, 10, : up_bias.shape[0]].reshape(1, hidden).astype(f32)
    home = jnp.clip(lax.axis_index("seq") - (lax.axis_index("dp") // outer) % 2, 0, strips - 1)
    length = lengths[home]
    mask = key_mask[home]
    pos = jnp.arange(groups * part_rows)
    valid = (pos == 0) | (pos < length) & (mask == 1)
    valid = jnp.pad(valid.reshape(groups, part_rows), ((0, 0), (0, pad_rows - part_rows))).reshape(rows)
    out, gres, dqkv, dout, dup, ddown, tally = layer(
        x, cot, script_ids[home], valid, vecs, up_full, f_qkv, f_out, f_up, f_down
    )
    grads = [
        g.astype(bf16).reshape(2, 2, 2, g.shape[0] // 8, g.shape[1]) for g in (dqkv, dout, dup, ddown)
    ]
    scratch = []
    for g in grads:
        u, w = g.shape[3:]
        scratch += [
            pltpu.VMEM((2, 2, u, w), bf16),
            pltpu.VMEM((2, u // 2, w), bf16),
            pltpu.VMEM((2, u // 2, w), bf16),
            pltpu.VMEM((u // 2, w), bf16),
            pltpu.VMEM((u // 2, w), bf16),
            pltpu.VMEM((groups, u // groups, w), bf16),
            pltpu.VMEM((groups - 1, u // groups, w), bf16),
        ]
    res = pl.pallas_call(
        functools.partial(scatter_kernel, outer, groups),
        out_shape=[jax.ShapeDtypeStruct((g.shape[3] // groups, g.shape[4]), f32) for g in grads]
        + [jax.ShapeDtypeStruct((16, d), f32)]
        + [jax.ShapeDtypeStruct(patches.shape, bf16)] * 2,
        in_specs=[vm] * 7,
        out_specs=[vm] * 7,
        scratch_shapes=scratch
        + [pltpu.VMEM((strips, pad_rows, d), bf16)] * 2
        + [pltpu.VMEM((4, 16, d), f32), pltpu.VMEM((2 + groups, 16, d), f32)]
        + [sems((4, RS)), sems((4, RS))]
        + [sems((2 + groups,))] * 2
        + [sems((groups - 1,))] * 4,
        compiler_params=pltpu.CompilerParams(
            collective_id=1, has_side_effects=True, vmem_limit_bytes=62 * 2**20
        ),
    )(*grads, tally, out, gres)
    shards = list(res[:4])
    tally = res[4]
    if outer > 1:

        def narrow(a):
            a = lax.psum(a, "dp", axis_index_groups=mates)
            a = lax.all_gather(a, ("seq",), axis=0, tiled=True)
            at = (lax.axis_index("dp") % outer) * groups + lax.axis_index("seq")
            n = a.shape[0] // groups // outer
            return lax.dynamic_slice_in_dim(a, at * n, n, axis=0)

        shards = [narrow(a) for a in shards]
        tally = lax.psum(tally, "dp", axis_index_groups=mates)
    me = lax.axis_index("dp") * groups + lax.axis_index("seq")
    n = d // (parts * outer)
    vec = lax.dynamic_slice_in_dim(tally[:10], me * n, n, axis=1)
    m = hidden // (parts * outer)
    vup = lax.dynamic_slice_in_dim(tally[10:14].reshape(hidden), me * m, m, axis=0)
    return (
        res[5], res[6], vec[0], vec[1], shards[0], vec[2], vec[3], shards[1], vec[4], vec[5],
        vec[6], shards[2], vup, shards[3], vec[7], vec[8:10],
    )


def solution(mesh):
    dp, seq = mesh.shape["dp"], mesh.shape["seq"]
    both = ("dp", "seq")
    one, two = P(both), P(both, None)
    rows = P("dp", "seq", None)
    return jax.shard_map(
        functools.partial(on_device, dp // 8, seq),
        mesh=mesh,
        in_specs=(
            rows, rows, P("dp"), P("dp"), P("dp", None), one, one, two, one, one, two, one, one,
            one, two, one, two, one, P(None, both),
        ),
        out_specs=(
            rows, rows, one, one, two, one, one, two, one, one, one, two, one, two, one,
            P(None, both),
        ),
        check_vma=False,
    )
```

```python
import functools

import jax
import jax.numpy as jnp
from jax import lax
from jax.experimental import pallas as pl
from jax.experimental.pallas import tpu as pltpu
from jax.sharding import PartitionSpec as P

DH = 64
MESH = pl.DeviceIdType.MESH
f32 = jnp.float32
bf16 = jnp.bfloat16
epsilon = 1e-06
WIRE = 12
HOPS = 8
QKV, OUT, UP = 0, 3, 4
G1, B1, QB, VB, OB, G2, B2, DB, T0, T1 = range(10)


def round_up(n, m):
    return (n + m - 1) // m * m


def ds(start, size, align=16):
    return pl.ds(pl.multiple_of(start, align), size)


def nn(a, b):
    return lax.dot_general(a, b, (((1,), (0,)), ((), ())), preferred_element_type=f32)


def nt(a, b):
    return lax.dot_general(a, b, (((1,), (1,)), ((), ())), preferred_element_type=f32)


def tn(a, b):
    return lax.dot_general(a, b, (((0,), (0,)), ((), ())), preferred_element_type=f32)


def loop(n, body):
    def step(i, carry):
        body(i)
        return carry

    lax.fori_loop(0, n, step, 0)


def total(v):
    return jnp.sum(v, axis=0, keepdims=True)


def remote(src, dst, send, recv, to):
    return pltpu.make_async_remote_copy(
        src_ref=src, dst_ref=dst, send_sem=send, recv_sem=recv, device_id=to, device_id_type=MESH
    )


class Place:
    def __init__(self, outer, groups):
        self.dp = lax.axis_index("dp")
        self.z = lax.axis_index("seq")
        self.groups = groups
        b = self.dp // outer
        self.c = b % 2
        self.x = (b // 2) % 2
        self.y = b // 4
        self.to_c = (self.dp + outer * (1 - 2 * self.c), self.z)
        self.to_x = (self.dp + outer * (2 - 4 * self.x), self.z)
        self.to_y = (self.dp + outer * (4 - 8 * self.y), self.z)

    def ahead(self, j):
        return (self.z + j) % self.groups

    def behind(self, j):
        return (self.z + self.groups - j) % self.groups

    def to_z(self, z):
        return (self.dp, z)

    def greet(self):
        barrier = pltpu.get_barrier_semaphore()
        peers = [self.to_c, self.to_x, self.to_y]
        peers += [self.to_z(self.ahead(j)) for j in range(1, self.groups)]
        for peer in peers:
            pl.semaphore_signal(barrier, inc=1, device_id=peer, device_id_type=MESH)
        pl.semaphore_wait(barrier, len(peers))


class Gather:
    def __init__(self, place, index, shard, block, part, land, send, recv, settle=None):
        self.p, self.i, self.shard = place, index, shard
        self.block, self.part, self.land, self.settle = block, part, land, settle
        self.send, self.recv = send, recv

    def copy(self, k, ref, to):
        return remote(ref, ref, self.send.at[self.i, k], self.recv.at[self.i, k], to)

    def z_copy(self, j, owner):
        return remote(
            self.shard, self.land(owner), self.send.at[self.i, j - 1], self.recv.at[self.i, j - 1],
            self.p.to_z(self.p.ahead(j)),
        )

    def z_start(self):
        p = self.p
        for j in range(1, p.groups):
            self.z_copy(j, p.z).start()
        self.land(p.z)[...] = self.shard[...]

    def xy(self, k):
        p = self.p
        mx, my = 1 - p.x, 1 - p.y
        own = lambda: self.block(p.y, p.x, p.c)
        bx = lambda: self.block(p.y, mx, p.c)
        by = lambda: self.block(my, p.x, p.c)
        bd = lambda: self.block(my, mx, p.c)
        if k == 3:
            return self.copy(3, own(), p.to_x)
        if k == 4:
            return self.copy(4, own(), p.to_y)
        if k == 5:
            return self.copy(5, self.part(by(), 1), p.to_x)
        if k == 6:
            return self.copy(6, self.part(bx(), 0), p.to_y)
        if k == 7:
            return self.copy(7, own(), p.to_c)
        if k == 8:
            return self.copy(8, bx(), p.to_c)
        if k == 9:
            return self.copy(9, by(), p.to_c)
        return self.copy(k, self.part(bd(), k - 10), p.to_c)

    def z_finish(self):
        p = self.p
        for j in range(1, p.groups):
            self.z_copy(j, p.behind(j)).wait_recv()
        if self.settle is not None:
            self.settle(self.block(p.y, p.x, p.c))
        for k in (3, 4, 7):
            self.xy(k).start()

    def mid(self):
        self.xy(3).wait_recv()
        self.xy(6).start()
        self.xy(8).start()
        self.xy(4).wait_recv()
        self.xy(5).start()
        self.xy(9).start()

    def diag(self):
        self.xy(6).wait_recv()
        self.xy(10).start()
        self.xy(5).wait_recv()
        self.xy(11).start()

    def finish(self):
        p = self.p
        for k in (7, 8, 9, 10, 11):
            self.xy(k).wait_recv()
        for j in range(1, p.groups):
            self.z_copy(j, p.z).wait_send()
        for k in range(3, WIRE):
            self.xy(k).wait_send()


class Rows:
    def __init__(self, place, parts, strip, send, recv):
        self.p, self.parts, self.strip, self.send, self.recv = place, parts, strip, send, recv
        self.strips, self.rows = parts.shape[0], parts.shape[1]
        self.home = place.z - place.c
        self.is_home = (self.home >= 0) & (self.home < self.strips)

    def clip(self, s):
        return jnp.clip(s, 0, self.strips - 1)

    def at(self, z):
        return self.strip.at[ds(z * self.rows, self.rows)]

    def inward(self, j, owner, s):
        return remote(
            self.parts.at[s], self.at(owner), self.send.at[j - 1], self.recv.at[j - 1],
            self.p.to_z(self.p.ahead(j)),
        )

    def in_start(self):
        p = self.p
        for j in range(1, p.groups):
            s = p.ahead(j) - p.c

            @pl.when((s >= 0) & (s < self.strips))
            def _():
                self.inward(j, p.z, self.clip(s)).start()

        @pl.when(self.is_home)
        def _():
            self.strip[ds(p.z * self.rows, self.rows), :] = self.parts[self.clip(self.home)]

        @pl.when(jnp.logical_not(self.is_home))
        def _():
            self.strip[...] = jnp.zeros_like(self.strip)

    def in_finish(self):
        p = self.p

        @pl.when(self.is_home)
        def _():
            for j in range(1, p.groups):
                self.inward(j, p.behind(j), 0).wait_recv()

    def in_sent(self):
        p = self.p
        for j in range(1, p.groups):
            s = p.ahead(j) - p.c

            @pl.when((s >= 0) & (s < self.strips))
            def _():
                self.inward(j, p.z, self.clip(s)).wait_send()

    def outward(self, j, s):
        z = self.p.ahead(j)
        return remote(
            self.at(z), self.parts.at[s], self.send.at[j - 1], self.recv.at[j - 1], self.p.to_z(z)
        )

    def out_start(self):
        p = self.p

        @pl.when(self.is_home)
        def _():
            home = self.clip(self.home)
            for j in range(1, p.groups):
                self.outward(j, home).start()
            self.parts[home] = self.strip[ds(p.z * self.rows, self.rows), :]

    def out_finish(self):
        p = self.p
        for j in range(1, p.groups):
            s = p.behind(j) - p.c

            @pl.when((s >= 0) & (s < self.strips))
            def _():
                self.outward(j, self.clip(s)).wait_recv()

        @pl.when(self.is_home)
        def _():
            for j in range(1, p.groups):
                self.outward(j, self.clip(self.home)).wait_send()


def add_into(dst, terms, rows, step=48):
    def body(i):
        at = ds(i * step, step)
        value = terms[0][at, :]
        for term in terms[1:]:
            value = value + term[at, :]
        dst[at, :] = value

    loop(rows // step, body)


class Scatter:
    def __init__(self, place, index, part, bufs, out, send, recv):
        self.p, self.i, self.part = place, index, part
        self.core, self.r1, self.r2, self.q1, self.q2, self.zs, self.zr = bufs
        self.out, self.send, self.recv = out, send, recv
        self.k, self.u, self.n = self.q1.shape[0], self.core.shape[3], self.q1.shape[2]
        self.r = self.u // place.groups
        self.first, self.second = pl.ds(0, self.u // 2), pl.ds(self.u // 2, self.u // 2)

    def wire(self, k):
        p, i = self.p, self.i
        if k == 0:
            src, dst, to = self.part.at[:, :, :, 1 - p.c], self.core, p.to_c
        elif k == 1:
            src, dst, to = self.core.at[:, :, 1 - p.x, self.first], self.r1, p.to_x
        elif k == 2:
            src, dst, to = self.core.at[:, 1 - p.y, :, self.second], self.r2, p.to_y
        elif k == 3:
            src, dst, to = self.r1.at[:, 1 - p.y], self.q1, p.to_y
        elif k == 4:
            src, dst, to = self.r2.at[:, 1 - p.x], self.q2, p.to_x
        else:
            z = p.ahead(k - 4)
            src, dst, to = self.zs.at[:, z], self.zr.at[k - 5], p.to_z(z)
        return remote(src, dst, self.send.at[i, k], self.recv.at[i, k], to)

    def start(self):
        self.wire(0).start()

    def core_add(self):
        p = self.p
        self.wire(0).wait_recv()
        for k in range(self.k):
            for y in range(2):
                for x in range(2):
                    here = self.core.at[k, y, x]
                    add_into(here, (here, self.part.at[k, y, x, p.c]), self.u)
        self.wire(1).start()
        self.wire(2).start()

    def pass_on(self):
        p = self.p
        self.wire(1).wait_recv()
        for k in range(self.k):
            here = self.r1.at[k, 1 - p.y]
            add_into(here, (here, self.core.at[k, 1 - p.y, p.x, self.first]), self.u // 2)
        self.wire(3).start()
        self.wire(2).wait_recv()
        for k in range(self.k):
            here = self.r2.at[k, 1 - p.x]
            add_into(here, (here, self.core.at[k, p.y, 1 - p.x, self.second]), self.u // 2)
        self.wire(4).start()

    def z_start(self):
        p, r = self.p, self.r
        half = self.u // 2
        self.wire(3).wait_recv()
        self.wire(4).wait_recv()
        per = p.groups // 2
        for k in range(self.k):
            for h in range(2):
                mine = self.r1.at[k, p.y] if h == 0 else self.r2.at[k, p.x]
                got = self.q1.at[k] if h == 0 else self.q2.at[k]
                value = self.core[k, p.y, p.x, pl.ds(h * half, half), :].astype(f32)
                value += mine[...].astype(f32) + got[...].astype(f32)
                slabs = value.reshape(per, r, self.n)
                self.zs[k, pl.ds(h * per, per)] = slabs.astype(bf16)
        for j in range(1, p.groups):
            self.wire(4 + j).start()

    def finish(self):
        p = self.p
        for j in range(1, p.groups):
            self.wire(4 + j).wait_recv()
        for k in range(self.k):
            value = self.zs[k, p.z].astype(f32)
            for j in range(1, p.groups):
                value += self.zr[j - 1, k].astype(f32)
            self.out[k][...] = value

    def drain(self):
        for k in range(HOPS):
            self.wire(k).wait_send()


class Tally:
    def __init__(self, place, value, got, send, recv):
        self.p, self.value, self.got, self.send, self.recv = place, value, got, send, recv

    def copy(self, k):
        p = self.p
        to = (p.to_c, p.to_x, p.to_y)[k] if k < 3 else p.to_z(p.ahead(k - 2))
        return remote(
            self.value.at[min(k, 3)], self.got.at[k], self.send.at[k], self.recv.at[k], to
        )

    def start(self):
        self.copy(0).start()

    def step(self, k):
        self.copy(k).wait_recv()
        self.value[k + 1] = self.value[k] + self.got[k]
        if k < 2:
            self.copy(k + 1).start()
        else:
            for j in range(1, self.p.groups):
                self.copy(2 + j).start()

    def finish(self):
        value = self.value[3]
        for j in range(1, self.p.groups):
            self.copy(2 + j).wait_recv()
            value += self.got[2 + j]
        for k in range(2 + self.p.groups):
            self.copy(k).wait_send()
        return value


def normalize(v):
    mean = jnp.mean(v, axis=1, keepdims=True)
    centred = v - mean
    inv = lax.rsqrt(jnp.mean(centred * centred, axis=1, keepdims=True) + epsilon)
    return centred * inv, mean, inv


def norm_backward(grad, hat, inv, gain):
    t = grad * gain
    mean_t = jnp.mean(t, axis=1, keepdims=True)
    mean_th = jnp.mean(t * hat, axis=1, keepdims=True)
    return inv * (t - mean_t - hat * mean_th)


class Layer:
    def __init__(self, place, refs):
        self.__dict__.update(refs)
        self.p = place
        self.rows, self.d = self.x.shape
        self.hidden = self.act.shape[1]
        self.step = 96

    def vec(self, i):
        return self.vecs[i : i + 1, :]

    def weight(self, i, cols=slice(None)):
        value = self.w[i, :, :, :, :, cols]
        return value.reshape(self.d, value.shape[-1])

    def eighths(self, value):
        return value.reshape(2, 2, 2, value.shape[0] // 8, value.shape[1])

    def vectors(self):
        d, groups = self.d, self.p.groups
        per = d // (8 * groups)
        wide = self.hidden // (8 * groups)

        def spread(lanes, cols, width):
            lane = lax.broadcasted_iota(jnp.int32, (lanes, cols), 0)
            col = lax.broadcasted_iota(jnp.int32, (lanes, cols), 1)
            hit = (col == lane // 128 * width + lane % 128) & (lane % 128 < width)
            return jnp.where(hit, 1.0, 0.0).astype(bf16)

        half = spread(4 * groups * 128, d // 2, per)
        for h in range(2):
            slabs = [self.small[4 * h + b, z] for b in range(4) for z in range(groups)]
            self.vecs[:, h * (d // 2) : (h + 1) * (d // 2)] = nn(jnp.concatenate(slabs, 1), half)
        one = spread(groups * 128, groups * wide, wide)
        for b in range(8):
            slabs = [self.small[b, z] for z in range(groups)]
            row = nn(jnp.concatenate(slabs, 1), one)[10:11, :]
            self.b_up[:, b * groups * wide : (b + 1) * groups * wide] = row

    def mask(self, lengths, script_ids, key_mask):
        strips, length = key_mask.shape
        home = jnp.clip(self.p.z - self.p.c, 0, strips - 1)
        keys = jnp.zeros((1, length), jnp.int32)
        for s in range(strips):
            keys = jnp.where(home == s, key_mask[s : s + 1, :], keys)
        pos = lax.broadcasted_iota(jnp.int32, (1, length), 1)
        good = (pos == 0) | ((pos < lengths[home]) & (keys == 1))
        good = jnp.broadcast_to(jnp.where(good, 1.0, 0.0), (8, length)).astype(bf16)
        real = length // self.p.groups
        padded = self.rows // self.p.groups
        row = lax.broadcasted_iota(jnp.int32, (self.rows, length), 0)
        col = lax.broadcasted_iota(jnp.int32, (self.rows, length), 1)
        hit = (col == row // padded * real + row % padded) & (row % padded < real)
        self.valid[...] = nt(jnp.where(hit, 1.0, 0.0).astype(bf16), good)[:, 0:1]
        self.sid = script_ids[home]

    def norm1(self):
        self.emb[...] = jnp.where(self.sid == 1, self.vec(T1), self.vec(T0))

        def body(i):
            at = ds(i * self.step, self.step)
            hat, mean, inv = normalize(self.x[at, :].astype(f32) + self.emb[...])
            self.stats[at, 0:1] = mean
            self.stats[at, 1:2] = inv
            self.h1[at, :] = (hat * self.vec(G1) + self.vec(B1)).astype(bf16)

        loop(self.rows // self.step, body)

    def project(self, i, n=256):
        d = self.d

        def body(k):
            at = ds(k * n, n, 128)
            value = nn(self.h1[...], self.weight(QKV + i, at))
            if i != 1:
                value = value + self.vecs[QB if i == 0 else VB : (QB if i == 0 else VB) + 1, at]
            self.qkv[:, ds(i * d + k * n, n, 128)] = value.astype(bf16)

        loop(d // n, body)

    def half(self, h, value):
        lane = lax.broadcasted_iota(jnp.int32, value.shape, 1)
        return jnp.where(lane // DH == h, value, jnp.zeros_like(value))

    def pick(self, a, b):
        lane = lax.broadcasted_iota(jnp.int32, a.shape, 1)
        return jnp.where(lane < DH, a, b)

    def lanes(self, p):
        return [ds(i * self.d + p * 128, 128, 128) for i in range(3)]

    def probs_out(self, p):
        slot = p % 2
        return pltpu.make_async_copy(self.probs.at[slot], self.kept.at[p], self.out_sem.at[slot])

    def probs_in(self, p):
        slot = p % 2
        return pltpu.make_async_copy(self.kept.at[p], self.probs.at[slot], self.in_sem.at[slot])

    def attend(self, p):
        aq, ak, av = self.lanes(p)
        q = self.qkv[:, aq] * jnp.asarray(DH**-0.5, bf16)
        k, v = self.qkv[:, ak], self.qkv[:, av]
        valid = self.valid[...] > 0

        @pl.when(p >= 2)
        def _():
            self.probs_out(p - 2).wait()

        contexts = []
        for h in range(2):
            s = nt(k, self.half(h, q))
            s = jnp.where(valid, s, -1e9)
            e = jnp.exp(s - jnp.max(s, axis=0, keepdims=True))
            probs = (e * (1.0 / total(e))).astype(bf16)
            self.probs[p % 2, h] = probs
            contexts.append(tn(probs, v))
        self.ctx[:, ds(p * 128, 128, 128)] = self.pick(*contexts).astype(bf16)
        self.probs_out(p).start()

    def mid_norm(self, n=256):
        def body(k):
            at = ds(k * n, n, 128)
            self.mid[:, at] = nn(self.ctx[...], self.weight(OUT, at))

        loop(self.d // n, body)

        def norm(i):
            at = ds(i * self.step, self.step)
            v = self.x[at, :].astype(f32) + self.emb[...] + (self.mid[at, :] + self.vec(OB))
            self.mid[at, :] = v
            hat, mean, inv = normalize(v)
            self.stats[at, 2:3] = mean
            self.stats[at, 3:4] = inv
            self.h2[at, :] = (hat * self.vec(G2) + self.vec(B2)).astype(bf16)

        loop(self.rows // self.step, norm)

    def mlp_up(self, j, n=256):
        def body(k):
            at = ds(j * self.d + k * n, n, 128)
            pre = nn(self.h2[...], self.weight(UP + j, ds(k * n, n, 128))) + self.b_up[:, at]
            cum = 0.5 * (1.0 + lax.erf(pre * 2.0**-0.5))
            den = jnp.exp(-0.5 * pre * pre) * (2.0 * jnp.pi) ** -0.5
            self.act[:, at] = (pre * cum).astype(bf16)
            self.slope[:, at] = (cum + pre * den).astype(bf16)

        loop(self.d // n, body)

    def down(self, b):
        return self.w_down.at[b // 4, (b // 2) % 2, b % 2]

    def dw_down(self, b):
        u = self.hidden // 8
        grad = tn(self.act[:, ds(b * u, u, 128)], self.cot[...])
        self.p_down[0, b // 4, (b // 2) % 2, b % 2] = grad.astype(bf16)

    def grad_pre(self, b):
        u = self.hidden // 8
        at = ds(b * u, u, 128)
        g = (nt(self.cot[...], self.down(b)[...]) * self.slope[:, at].astype(f32)).astype(bf16)
        self.slope[:, at] = g
        self.up_sums[:, at] = total(g.astype(f32))

    def mlp_down(self, n=256):
        def body(k):
            at = ds(k * n, n, 128)
            w = self.w_down[:, :, :, :, at].reshape(self.hidden, n)
            value = self.mid[:, at] + (nn(self.act[...], w) + self.vecs[DB : DB + 1, at])
            self.out[:, at] = value.astype(bf16)

        loop(self.d // n, body)

    def grad_h2(self, j):
        m = self.rows // 2

        def body(i):
            at = ds(i * m, m)
            value = nt(self.slope[at, ds(j * self.d, self.d, 128)], self.weight(UP + j))
            if j == 0:
                self.wide[at, :] = value
            else:
                self.wide[at, :] += value

        loop(2, body)

    def dw_up(self, j, n=256):
        def body(k):
            grad = tn(self.h2[...], self.slope[:, ds(j * self.d + k * n, n, 128)])
            self.w[UP + j, :, :, :, :, ds(k * n, n, 128)] = self.eighths(grad).astype(bf16)

        loop(self.d // n, body)

    def back2(self):
        zero = jnp.zeros((1, self.d), f32)

        def body(i, sums):
            at = ds(i * self.step, self.step)
            inv = self.stats[at, 3:4]
            hat = (self.mid[at, :] - self.stats[at, 2:3]) * inv
            g = self.wide[at, :]
            cot = self.cot[at, :].astype(f32)
            value = cot + norm_backward(g, hat, inv, self.vec(G2))
            self.mid[at, :] = value
            low = value.astype(bf16)
            self.gb[at, :] = low
            terms = (g * hat, g, cot, low.astype(f32))
            return tuple(s + total(t) for s, t in zip(sums, terms))

        sums = lax.fori_loop(0, self.rows // self.step, body, (zero,) * 4)
        for row, s in zip((G2, B2, DB, OB), sums):
            self.sums[row : row + 1, :] = s

    def grad_ctx(self):
        m = self.rows // 2

        def body(i):
            at = ds(i * m, m)
            self.gctx[at, :] = nt(self.gb[at, :], self.weight(OUT)).astype(bf16)

        loop(2, body)

    def dw_out(self, n=256):
        def body(k):
            at = ds(k * n, n, 128)
            grad = tn(self.ctx[...], self.gb[:, at])
            self.w[OUT, :, :, :, :, at] = self.eighths(grad).astype(bf16)

        loop(self.d // n, body)

    def attend_back(self, p, last):
        aq, ak, av = self.lanes(p)
        q, k, v = self.qkv[:, aq], self.qkv[:, ak], self.qkv[:, av]
        g = self.gctx[:, aq]

        @pl.when(p + 1 < last)
        def _():
            self.probs_in(p + 1).start()

        self.probs_in(p).wait()
        dq, dk, dv = [], [], []
        for h in range(2):
            probs = self.probs[p % 2, h]
            dv.append(nn(probs, g))
            grad = nt(v, self.half(h, g))
            wide = probs.astype(f32)
            grad = (wide * (grad - total(wide * grad))).astype(bf16)
            dk.append(nn(grad, q))
            dq.append(tn(grad, k))
        dq = (self.pick(*dq) * DH**-0.5).astype(bf16)
        dv = self.pick(*dv).astype(bf16)
        self.qkv[:, aq] = dq
        self.qkv[:, ak] = (self.pick(*dk) * DH**-0.5).astype(bf16)
        self.qkv[:, av] = dv
        self.sums[QB : QB + 1, aq] = total(dq.astype(f32))
        self.sums[VB : VB + 1, aq] = total(dv.astype(f32))

    def grad_h1(self, g, n=256):
        m = self.rows // 2

        def body(i):
            at = ds(i * m, m)
            value = None
            for k in range(3):
                w = self.weight(QKV + k, pl.ds(g * n, n))
                term = nt(self.qkv[at, pl.ds(k * self.d + g * n, n)], w)
                value = term if value is None else value + term
            if g == 0:
                self.wide[at, :] = value
            else:
                self.wide[at, :] += value

        loop(2, body)

    def dw_qkv(self, g, n=256):
        for k in range(3):
            grad = tn(self.h1[...], self.qkv[:, pl.ds(k * self.d + g * n, n)])
            self.w[QKV + k, :, :, :, :, pl.ds(g * n, n)] = self.eighths(grad).astype(bf16)

    def back1(self):
        zero = jnp.zeros((1, self.d), f32)

        def body(i, sums):
            at = ds(i * self.step, self.step)
            inv = self.stats[at, 1:2]
            hat = (self.x[at, :].astype(f32) + self.emb[...] - self.stats[at, 0:1]) * inv
            g = self.wide[at, :]
            value = self.mid[at, :] + norm_backward(g, hat, inv, self.vec(G1))
            self.gx[at, :] = value.astype(bf16)
            return tuple(s + total(t) for s, t in zip(sums, (g * hat, g, value)))

        sums = lax.fori_loop(0, self.rows // self.step, body, (zero,) * 3)
        self.sums[G1 : G1 + 1, :] = sums[0]
        self.sums[B1 : B1 + 1, :] = sums[1]
        self.sums[T0 : T0 + 1, :] = jnp.where(self.sid == 1, 0.0, sums[2])
        self.sums[T1 : T1 + 1, :] = jnp.where(self.sid == 1, sums[2], 0.0)


def kernel(outer, groups, names, *refs):
    r = dict(zip(names, refs, strict=True))
    p = Place(outer, groups)
    L = Layer(p, r)
    d, hidden = L.d, L.hidden
    nh = hidden // d
    real = r["patches"].shape[1]
    strips = r["patches"].shape[0]
    per = d // (8 * groups)
    u = d // 8
    n_down = d // 256
    w, w_down, stage = r["w"], r["w_down"], r["stage"]

    gs = []

    def add(shard, block, part, land, settle=None):
        gs.append(
            Gather(p, len(gs), shard, block, part, land, r["g_send"], r["g_recv"], settle)
        )

    add(
        r["s_small"],
        lambda y, x, c: r["small"].at[y * 4 + x * 2 + c],
        lambda ref, h: ref.at[pl.ds(h * (groups // 2), groups // 2)],
        lambda z: r["small"].at[p.y * 4 + p.x * 2 + p.c, z],
    )

    def add_square(i, shard):
        def settle(block):
            block[...] = stage[i].astype(f32).reshape(u, d).astype(bf16)

        add(
            shard,
            lambda y, x, c: w.at[i, y, x, c],
            lambda ref, h: ref.at[pl.ds(h * (u // 2), u // 2)],
            lambda z: stage.at[i, z],
            settle,
        )

    for i in range(3):
        add_square(QKV + i, r["s_qkv"].at[:, pl.ds(i * d, d)])
    add_square(OUT, r["s_out"])
    for i in range(nh):
        add_square(UP + i, r["s_up"].at[:, pl.ds(i * d, d)])
    hu = hidden // 8
    hr = hu // groups
    for i in range(n_down):
        cols = pl.ds(i * 256, 256)
        add(
            r["s_down"].at[:, cols],
            lambda y, x, c, cols=cols: w_down.at[y, x, c, :, cols],
            lambda ref, h: ref.at[pl.ds(h * (hu // 2), hu // 2)],
            lambda z, cols=cols: w_down.at[p.y, p.x, p.c, ds(z * hr, hr), cols],
        )
    xs = Rows(p, r["xp"], r["x"], r["x_send"], r["x_recv"])
    cs = Rows(p, r["cp"], r["cot"], r["c_send"], r["c_recv"])
    last = len(gs)

    def gather_tick(t):
        for lag, act in enumerate(("z_start", "z_finish", "mid", "diag", "finish")):
            if 0 <= t - lag < last:
                getattr(gs[t - lag], act)()

    ss = []

    def give(part, bufs, out):
        ss.append(Scatter(p, len(ss), part, bufs, out, r["s_send"], r["s_recv"]))

    def bufs(kind, i):
        flat = kind == "flat"
        found = [r[f"{kind}_{name}"].at[i] for name in ("core", "r1", "r2", "q1", "q2")]
        slot = stage.at[pl.ds(UP + i if i < nh else OUT, 1)] if flat else r[f"{kind}_zs"].at[i]
        return found + [slot, r[f"{kind}_zr"].at[i]]

    for i in range(n_down):
        cols = pl.ds(i * 256, 256)
        give(r["p_down"].at[:, :, :, :, :, cols], bufs("tall", i), [r["o_down"].at[:, cols]])
    for i in range(nh):
        give(w.at[pl.ds(UP + i, 1)], bufs("flat", i), [r["o_up"].at[:, pl.ds(i * d, d)]])
    give(w.at[pl.ds(OUT, 1)], bufs("flat", nh), [r["o_out"]])
    for g in range(d // 256):
        cols = pl.ds(g * 256, 256)
        outs = [r["o_qkv"].at[:, pl.ds(k * d + g * 256, 256)] for k in range(3)]
        give(w.at[pl.ds(QKV, 3), :, :, :, :, cols], bufs("head", g), outs)

    def scatter_tick(t):
        for lag, act in enumerate(("core_add", "pass_on", "z_start", "finish")):
            if 0 <= t - lag < len(ss):
                getattr(ss[t - lag], act)()

    ys = Rows(p, r["xp"], r["out"], r["y_send"], r["y_recv"])
    ds_ = Rows(p, r["cp"], L.gx, r["d_send"], r["d_recv"])
    ts = Tally(p, r["value"], r["got"], r["t_send"], r["t_recv"])

    p.greet()
    gather_tick(0)
    gather_tick(1)
    for src, dst in ((r["patches"], r["xp"]), (r["cotangent"], r["cp"])):
        dst[...] = jnp.zeros_like(dst)
        for s in range(strips):
            dst[s, :real] = src[s]
    gather_tick(2)
    xs.in_start()
    L.mask(r["lengths"], r["script_ids"], r["key_mask"])
    gather_tick(3)
    gather_tick(4)
    L.vectors()
    xs.in_finish()
    L.norm1()
    gather_tick(5)
    L.project(0)
    gather_tick(6)
    cs.in_start()
    L.project(1)
    gather_tick(7)
    L.project(2)
    gather_tick(8)
    pairs = d // 128

    def attend(i):
        L.attend(i)
        for k, t in ((1, 9), (3, 10)):

            @pl.when(i == k)
            def _():
                gather_tick(t)

    loop(pairs, attend)
    for i in (pairs - 2, pairs - 1):
        L.probs_out(i).wait()
    L.mid_norm()
    gather_tick(11)
    for j in range(nh - 1):
        L.mlp_up(j)
    gather_tick(12)
    L.mlp_up(nh - 1)
    cs.in_finish()
    xs.in_sent()
    cs.in_sent()

    def down(i):
        L.dw_down(i)

        @pl.when(i == 3)
        def _():
            gather_tick(13)

    loop(8, down)
    for i in range(n_down):
        ss[i].start()
    for t in range(14, last + 4):
        gather_tick(t)
    scatter_tick(0)

    def grad_pre(i):
        L.grad_pre(i)

        @pl.when(i == 3)
        def _():
            scatter_tick(1)

    loop(8, grad_pre)
    scatter_tick(2)
    for j in range(nh):
        L.grad_h2(j)
    for j in range(nh):
        L.dw_up(j)
        ss[n_down + j].start()
        scatter_tick(n_down + j)
    L.mlp_down()
    ys.out_start()
    L.back2()
    L.grad_ctx()
    L.dw_out()
    at = n_down + nh
    ss[at].start()
    scatter_tick(at)
    L.probs_in(0).start()
    for g in range(d // 256):
        loop(2, lambda i: L.attend_back(2 * g + i, pairs))
        L.grad_h1(g)
        L.dw_qkv(g)
        at += 1
        ss[at].start()
        if g < d // 256 - 1:
            scatter_tick(at)
    L.back1()
    ds_.out_start()
    r["value"][0] = jnp.concatenate(
        [r["sums"][0:10, :]]
        + [L.up_sums[:, j * d : (j + 1) * d] for j in range(nh)]
        + [jnp.zeros((6 - nh, d), f32)]
    )
    ts.start()
    scatter_tick(at)
    ts.step(0)
    scatter_tick(at + 1)
    ts.step(1)
    scatter_tick(at + 2)
    ts.step(2)
    ys.out_finish()
    for s in range(strips):
        r["o_out_rows"][s] = r["xp"][s, :real]
    r["o_tally"][...] = ts.finish()
    scatter_tick(at + 3)
    ds_.out_finish()
    for s in range(strips):
        r["o_grad_rows"][s] = r["cp"][s, :real]
    for s in ss:
        s.drain()


def on_device(outer, groups, *args):
    (patches, cotangent, lengths, script_ids, key_mask, norm1_gain, norm1_bias, w_qkv, q_bias,
     v_bias, w_attn_out, attn_out_bias, norm2_gain, norm2_bias, w_up, up_bias, w_down, down_bias,
     script_table) = args
    strips, part_rows, d = patches.shape
    hidden = w_up.shape[1]
    parts = 8 * groups
    pad_rows = round_up(part_rows, 16)
    rows = groups * pad_rows
    vectors = [norm1_gain, norm1_bias, q_bias, v_bias, attn_out_bias, norm2_gain, norm2_bias,
               down_bias, script_table[0], script_table[1]]
    weights = [w_qkv, w_attn_out, w_up, w_down]
    if outer > 1:
        mates = [[g * outer + i for i in range(outer)] for g in range(8)]
        seq = lax.axis_index("seq")

        def widen(a):
            a = lax.all_gather(a, ("seq",), axis=0, tiled=True)
            a = lax.all_gather(a, "dp", axis=0, tiled=True, axis_index_groups=mates)
            n = a.shape[0] // groups
            return lax.dynamic_slice_in_dim(a, seq * n, n, axis=0)

        vectors = [widen(a) for a in vectors]
        up_bias = widen(up_bias)
        weights = [widen(a) for a in weights]
    c = vectors[0].shape[0]
    small = jnp.concatenate(
        [
            jnp.pad(jnp.stack(vectors), ((0, 0), (0, 128 - c))),
            jnp.pad(up_bias[None], ((0, 5), (0, 128 - up_bias.shape[0]))),
        ]
    )
    vm = pl.BlockSpec(memory_space=pltpu.VMEM)
    sm = pl.BlockSpec(memory_space=pltpu.SMEM)
    anywhere = pl.BlockSpec(memory_space=pl.ANY)
    sems = pltpu.SemaphoreType.DMA
    nh = hidden // d
    u, r, nd, ng = d // 8, d // parts, d // 256, d // 256
    ins = ["s_small", "s_qkv", "s_out", "s_up", "s_down", "patches", "cotangent", "key_mask",
           "lengths", "script_ids"]
    outs = {
        "o_qkv": ((r, 3 * d), f32),
        "o_out": ((r, d), f32),
        "o_up": ((r, hidden), f32),
        "o_down": ((hidden // parts, d), f32),
        "o_tally": ((16, d), f32),
        "o_out_rows": (patches.shape, bf16),
        "o_grad_rows": (patches.shape, bf16),
        "kept": ((d // 128, 2, rows, rows), bf16),
    }
    scratch = {
        "small": ((8, groups, 16, 128), bf16),
        "stage": ((4 + nh, groups, r, d), bf16),
        "w": ((4 + nh, 2, 2, 2, u, d), bf16),
        "w_down": ((2, 2, 2, hidden // 8, d), bf16),
        "p_down": ((1, 2, 2, 2, hidden // 8, d), bf16),
        "xp": ((strips, pad_rows, d), bf16),
        "cp": ((strips, pad_rows, d), bf16),
        "x": ((rows, d), bf16),
        "cot": ((rows, d), bf16),
        "valid": ((rows, 1), f32),
        "vecs": ((16, d), f32),
        "b_up": ((1, hidden), f32),
        "up_sums": ((1, hidden), f32),
        "sums": ((16, d), f32),
        "emb": ((1, d), f32),
        "stats": ((rows, 4), f32),
        "h1": ((rows, d), bf16),
        "qkv": ((rows, 3 * d), bf16),
        "probs": ((2, 2, rows, rows), bf16),
        "ctx": ((rows, d), bf16),
        "mid": ((rows, d), f32),
        "wide": ((rows, d), f32),
        "h2": ((rows, d), bf16),
        "act": ((rows, hidden), bf16),
        "slope": ((rows, hidden), bf16),
        "value": ((4, 16, d), f32),
        "got": ((2 + groups, 16, d), f32),
    }
    for kind, count, k, uu, n in (
        ("tall", nd, 1, hidden // 8, 256),
        ("flat", nh + 1, 1, u, d),
        ("head", ng, 3, u, 256),
    ):
        rr = uu // groups
        scratch[f"{kind}_core"] = ((count, k, 2, 2, uu, n), bf16)
        scratch[f"{kind}_r1"] = ((count, k, 2, uu // 2, n), bf16)
        scratch[f"{kind}_r2"] = ((count, k, 2, uu // 2, n), bf16)
        scratch[f"{kind}_q1"] = ((count, k, uu // 2, n), bf16)
        scratch[f"{kind}_q2"] = ((count, k, uu // 2, n), bf16)
        if kind != "flat":
            scratch[f"{kind}_zs"] = ((count, k, groups, rr, n), bf16)
        scratch[f"{kind}_zr"] = ((count, groups - 1, k, rr, n), bf16)
    n_gather = 5 + nh + nd
    n_scatter = nd + nh + 1 + ng
    semaphores = {
        "g_send": (n_gather, WIRE), "g_recv": (n_gather, WIRE),
        "s_send": (n_scatter, HOPS), "s_recv": (n_scatter, HOPS),
        "t_send": (2 + groups,), "t_recv": (2 + groups,),
        "out_sem": (2,), "in_sem": (2,),
    }
    for name in "xcyd":
        semaphores[f"{name}_send"] = (groups - 1,)
        semaphores[f"{name}_recv"] = (groups - 1,)
    names = ins + list(outs) + list(scratch) + list(semaphores)

    def body(*refs):
        refs = dict(zip(names, refs, strict=True))
        act = refs["act"]
        refs["out"] = refs["h2"]
        refs["gb"] = act.at[:, pl.ds(0, d)]
        refs["gctx"] = act.at[:, pl.ds(d, d)]
        refs["gx"] = act.at[:, pl.ds(2 * d, d)]
        kernel(outer, groups, list(refs), *refs.values())

    res = pl.pallas_call(
        body,
        out_shape=[jax.ShapeDtypeStruct(*s) for s in outs.values()],
        in_specs=[vm] * 8 + [sm] * 2,
        out_specs=[vm] * 7 + [anywhere],
        scratch_shapes=[pltpu.VMEM(*s) for s in scratch.values()]
        + [sems(s) for s in semaphores.values()],
        compiler_params=pltpu.CompilerParams(
            collective_id=0, has_side_effects=True, vmem_limit_bytes=63 * 2**20
        ),
    )(small, *weights, patches, cotangent, key_mask, lengths, script_ids)
    shards = list(res[:4])
    tally = res[4]
    if outer > 1:

        def narrow(a):
            a = lax.psum(a, "dp", axis_index_groups=mates)
            a = lax.all_gather(a, ("seq",), axis=0, tiled=True)
            at = (lax.axis_index("dp") % outer) * groups + lax.axis_index("seq")
            n = a.shape[0] // groups // outer
            return lax.dynamic_slice_in_dim(a, at * n, n, axis=0)

        shards = [narrow(a) for a in shards]
        tally = lax.psum(tally, "dp", axis_index_groups=mates)
    me = lax.axis_index("dp") * groups + lax.axis_index("seq")
    n = d // (parts * outer)
    vec = lax.dynamic_slice_in_dim(tally[:10], me * n, n, axis=1)
    m = hidden // (parts * outer)
    vup = lax.dynamic_slice_in_dim(tally[10 : 10 + nh].reshape(hidden), me * m, m, axis=0)
    return (
        res[5], res[6], vec[G1], vec[B1], shards[0], vec[QB], vec[VB], shards[1], vec[OB], vec[G2],
        vec[B2], shards[2], vup, shards[3], vec[DB], vec[T0 : T1 + 1],
    )


def solution(mesh):
    dp, seq = mesh.shape["dp"], mesh.shape["seq"]
    both = ("dp", "seq")
    one, two = P(both), P(both, None)
    rows = P("dp", "seq", None)
    return jax.shard_map(
        functools.partial(on_device, dp // 8, seq),
        mesh=mesh,
        in_specs=(
            rows, rows, P("dp"), P("dp"), P("dp", None), one, one, two, one, one, two, one, one,
            one, two, one, two, one, P(None, both),
        ),
        out_specs=(
            rows, rows, one, one, two, one, one, two, one, one, one, two, one, two, one,
            P(None, both),
        ),
        check_vma=False,
    )
```

```python
import functools

import jax
import jax.numpy as jnp
from jax import lax
from jax.experimental import pallas as pl
from jax.experimental.pallas import tpu as pltpu
from jax.sharding import PartitionSpec as P

DH = 64
MESH = pl.DeviceIdType.MESH
f32 = jnp.float32
bf16 = jnp.bfloat16
epsilon = 1e-06
WIRE = 13
FAR = 12
DIRECT = 1
HOPS = 9
QKV, OUT, UP = 0, 3, 4
G1, B1, QB, VB, OB, G2, B2, DB, T0, T1 = range(10)


def round_up(n, m):
    return (n + m - 1) // m * m


def ds(start, size, align=16):
    return pl.ds(pl.multiple_of(start, align), size)


def nn(a, b):
    return lax.dot_general(a, b, (((1,), (0,)), ((), ())), preferred_element_type=f32)


def nt(a, b):
    return lax.dot_general(a, b, (((1,), (1,)), ((), ())), preferred_element_type=f32)


def tn(a, b):
    return lax.dot_general(a, b, (((0,), (0,)), ((), ())), preferred_element_type=f32)


def loop(n, body):
    def step(i, carry):
        body(i)
        return carry

    lax.fori_loop(0, n, step, 0)


def total(v):
    return jnp.sum(v, axis=0, keepdims=True)


def remote(src, dst, send, recv, to):
    return pltpu.make_async_remote_copy(
        src_ref=src, dst_ref=dst, send_sem=send, recv_sem=recv, device_id=to, device_id_type=MESH
    )


(ZS, ZE, MX, MY, DX, DY, FIN, ST, CA, PX, PY, ZT, FI, ROW, IN, OUT_, ZF, ZP) = range(18)
(SMALL, WQ, WK, WV, WO, WU, WD, GD, GU, GO, GQ, X_IN, C_IN, Y_OUT, R_OUT) = range(1, 16)
(PREP, MASK, VEC, NORM1, PROJ, ATT, MID, UP_, DWDOWN, GPRE, DOWN, GU_, BACK2, GCTX, DWUP, ATTB,
 GQ_, DWQKV, BACK1, DWOUT, SENT, SENTX, T) = range(100, 123)
SCHEDULE = (
    (ZS, SMALL, 0), (ZS, WQ, 0), (ZS, WK, 0), (PREP, 0, 0), (ZS, WV, 0), (MASK, 0, 0),
    (ZS, WO, 0), (ZE, SMALL, 0), (ZF, WQ, 0), (ROW, X_IN, 0), (MX, SMALL, 0), (MY, SMALL, 0),
    (ZF, WK, 0), (DX, SMALL, 0), (DY, SMALL, 0), (ZF, WV, 0), (FIN, SMALL, 0), (VEC, 0, 0),
    (ZF, WO, 0), (ZE, WQ, 0), (ZS, WU, 0), (ROW, X_IN, 1), (ZE, WK, 0), (ZE, WV, 0), (MX, WQ, 0),
    (MY, WQ, 0), (ZE, WO, 0), (ZS, WU, 1), (ZF, WU, 0), (ROW, X_IN, 2), (MX, WK, 0), (MY, WK, 0),
    (MX, WV, 0), (ZS, WU, 2), (MY, WV, 0), (ZF, WU, 1), (ZE, WU, 0), (DX, WQ, 0), (DY, WQ, 0),
    (ZS, WU, 3), (ZS, WD, 0), (MX, WO, 0), (MY, WO, 0), (IN, X_IN, 0), (NORM1, 0, 0),
    (ROW, C_IN, 0), (DX, WK, 0), (DY, WK, 0), (FIN, WQ, 0), (PROJ, 0, 0), (DX, WV, 0),
    (DY, WV, 0), (ZE, WU, 1), (ZF, WU, 2), (FIN, WK, 0), (PROJ, 0, 1), (ZF, WU, 3), (FIN, WV, 0),
    (PROJ, 0, 2), (MX, WU, 0), (MY, WU, 0), (ATT, 0, 0), (ZS, WD, 1), (DX, WO, 0), (DY, WO, 0),
    (ZF, WD, 0), (ATT, 0, 1), (ROW, C_IN, 1), (MX, WU, 1), (MY, WU, 1), (ATT, 0, 2), (DX, WU, 0),
    (DY, WU, 0), (ZE, WU, 2), (ZE, WU, 3), (ATT, 0, 3), (ZS, WD, 2), (DX, WU, 1), (DY, WU, 1),
    (ZF, WD, 1), (ATT, 0, 4), (ZE, WD, 0), (ATT, 0, 5), (SENTX, 0, 0), (ROW, C_IN, 2),
    (MX, WU, 2), (MY, WU, 2), (FIN, WO, 0), (MID, 0, 0), (MX, WU, 3), (MY, WU, 3), (FIN, WU, 0),
    (UP_, 0, 0), (ZE, WD, 1), (ZF, WD, 2), (FIN, WU, 1), (UP_, 0, 1), (MX, WD, 0), (MY, WD, 0),
    (DX, WU, 2), (DY, WU, 2), (FIN, WU, 2), (UP_, 0, 2), (DX, WU, 3), (DY, WU, 3), (ZE, WD, 2),
    (FIN, WU, 3), (UP_, 0, 3), (IN, C_IN, 0), (DWDOWN, 0, 0), (MX, WD, 1), (MY, WD, 1),
    (DWDOWN, 0, 1), (DWDOWN, 0, 2), (DWDOWN, 0, 3), (DX, WD, 0), (DY, WD, 0), (DWDOWN, 0, 4),
    (DWDOWN, 0, 5), (DWDOWN, 0, 6), (DWDOWN, 0, 7), (ST, GD, 0), (ST, GD, 1), (ST, GD, 2),
    (MX, WD, 2), (MY, WD, 2), (CA, GD, 0), (DX, WD, 1), (DY, WD, 1), (CA, GD, 1), (DX, WD, 2),
    (DY, WD, 2), (CA, GD, 2), (FIN, WD, 0), (FIN, WD, 1), (FIN, WD, 2), (GPRE, 0, 0),
    (GPRE, 0, 1), (GPRE, 0, 2), (GPRE, 0, 3), (PX, GD, 0), (PY, GD, 0), (GPRE, 0, 4),
    (GPRE, 0, 5), (GPRE, 0, 6), (GPRE, 0, 7), (DOWN, 0, 0), (OUT_, Y_OUT, 0), (PX, GD, 1),
    (PY, GD, 1), (GU_, 0, 0), (GU_, 0, 1), (PY, GD, 2), (PX, GD, 2), (GU_, 0, 2), (GU_, 0, 3),
    (SENT, 0, 0), (DWUP, 0, 0), (ST, GU, 0), (ZT, GD, 0), (DWUP, 0, 1), (ST, GU, 1), (ZT, GD, 1),
    (CA, GU, 0), (DWUP, 0, 2), (ST, GU, 2), (ZT, GD, 2), (CA, GU, 1), (DWUP, 0, 3), (ST, GU, 3),
    (CA, GU, 2), (BACK2, 0, 0), (PX, GU, 0), (PY, GU, 0), (CA, GU, 3), (GCTX, 0, 0), (ATTB, 0, 0),
    (PX, GU, 1), (PY, GU, 1), (ATTB, 0, 1), (ZP, GD, 0), (GQ_, 0, 0), (PX, GU, 2), (PY, GU, 2),
    (DWQKV, 0, 0), (ST, GQ, 0), (ZP, GD, 1), (ZT, GU, 0), (ZP, GD, 2), (ATTB, 0, 2), (FI, GD, 0),
    (PX, GU, 3), (PY, GU, 3), (CA, GQ, 0), (ATTB, 0, 3), (FI, GD, 1), (ZT, GU, 1), (GQ_, 0, 1),
    (ZP, GU, 0), (ZT, GU, 2), (DWQKV, 0, 1), (ST, GQ, 1), (FI, GD, 2), (ZT, GU, 3), (ATTB, 0, 4),
    (ZP, GU, 1), (FI, GU, 0), (PX, GQ, 0), (PY, GQ, 0), (CA, GQ, 1), (ATTB, 0, 5), (ZP, GU, 2),
    (ZP, GU, 3), (GQ_, 0, 2), (BACK1, 0, 0), (OUT_, R_OUT, 0), (FI, GU, 1), (ZT, GQ, 0), (T, 0, 0),
    (DWQKV, 0, 2), (ST, GQ, 2), (FI, GU, 2), (DWOUT, 0, 0), (ST, GO, 0), (T, 0, 1), (FI, GU, 3),
    (PX, GQ, 1), (PY, GQ, 1), (CA, GQ, 2), (CA, GO, 0), (ZT, GQ, 1), (PY, GQ, 2), (T, 0, 2),
    (PX, GQ, 2), (PY, GO, 0), (PX, GO, 0), (ZT, GQ, 2), (ZT, GO, 0), (ZP, GQ, 0), (ZP, GQ, 1),
    (ZP, GQ, 2), (ZP, GO, 0), (FI, GQ, 0), (FI, GQ, 1), (FI, GQ, 2), (FI, GO, 0),
)


class Place:
    def __init__(self, outer, groups):
        self.dp = lax.axis_index("dp")
        self.z = lax.axis_index("seq")
        assert groups == 4
        self.groups = groups
        b = self.dp // outer
        self.c = b % 2
        self.x = (b // 2) % 2
        self.y = b // 4
        self.inner = (self.z == 1) | (self.z == 2)
        self.to_c = (self.dp + outer * (1 - 2 * self.c), self.z)
        self.to_x = (self.dp + outer * (2 - 4 * self.x), self.z)
        self.to_y = (self.dp + outer * (4 - 8 * self.y), self.z)

    def ahead(self, j):
        return (self.z + j) % self.groups

    def behind(self, j):
        return (self.z + self.groups - j) % self.groups

    def to_z(self, z):
        return (self.dp, z)

    def greet(self):
        barrier = pltpu.get_barrier_semaphore()
        peers = [self.to_c, self.to_x, self.to_y]
        peers += [self.to_z(self.ahead(j)) for j in range(1, self.groups)]
        for peer in peers:
            pl.semaphore_signal(barrier, inc=1, device_id=peer, device_id_type=MESH)
        pl.semaphore_wait(barrier, len(peers))


class Gather:
    def __init__(self, place, index, shard, block, part, land, send, recv, settle=None):
        self.p, self.i, self.shard = place, index, shard
        self.block, self.part, self.land, self.settle = block, part, land, settle
        self.send, self.recv = send, recv

    def copy(self, k, ref, to):
        return remote(ref, ref, self.send.at[self.i, k], self.recv.at[self.i, k], to)

    def z_wire(self, k):
        p, z = self.p, self.p.z
        if k < 3:
            src, owner, to = self.shard, z, ((z + 1) % 4, (z + 2) % 4, (z + 3) % 4)[k]
        elif self.i < DIRECT:
            src, owner, to = self.shard, z, 3 - z
        else:
            owner = (z + 2) % 4
            src, to = self.land(owner), (z + 1) % 4 * (z // 2)
        return remote(
            src, self.land(owner), self.send.at[self.i, k], self.recv.at[self.i, k], p.to_z(to)
        )

    def z_got(self, k):
        z = self.p.z
        owner = ((z + 3) % 4, (z + 2) % 4, (z + 1) % 4)[k] if k < 3 else 3 - z
        ref = self.land(owner)
        remote(
            ref, ref, self.send.at[self.i, k], self.recv.at[self.i, k], self.p.to_z((z + 1) % 4)
        ).wait_recv()

    def z_start(self):
        p = self.p
        pl.when(p.z < 3)(lambda: self.z_wire(0).start())
        self.z_wire(1).start()
        pl.when(p.z > 0)(lambda: self.z_wire(2).start())
        if self.i < DIRECT:
            pl.when(jnp.logical_not(p.inner))(lambda: self.z_wire(FAR).start())
        self.land(p.z)[...] = self.shard[...]

    def z_far(self):
        if self.i < DIRECT:
            return

        @pl.when(self.p.inner)
        def _():
            self.z_got(1)
            self.z_wire(FAR).start()

    def xy(self, k):
        p = self.p
        mx, my = 1 - p.x, 1 - p.y
        own = lambda: self.block(p.y, p.x, p.c)
        bx = lambda: self.block(p.y, mx, p.c)
        by = lambda: self.block(my, p.x, p.c)
        bd = lambda: self.block(my, mx, p.c)
        if k == 3:
            return self.copy(3, own(), p.to_x)
        if k == 4:
            return self.copy(4, own(), p.to_y)
        if k == 5:
            return self.copy(5, self.part(by(), 1), p.to_x)
        if k == 6:
            return self.copy(6, self.part(bx(), 0), p.to_y)
        if k == 7:
            return self.copy(7, own(), p.to_c)
        if k == 8:
            return self.copy(8, bx(), p.to_c)
        if k == 9:
            return self.copy(9, by(), p.to_c)
        return self.copy(k, self.part(bd(), k - 10), p.to_c)

    def z_end(self):
        p = self.p
        pl.when(p.z > 0)(lambda: self.z_got(0))
        pl.when(p.z < 3)(lambda: self.z_got(2))

        @pl.when(jnp.logical_not(p.inner))
        def _():
            self.z_got(1)
            self.z_got(FAR)

        if self.i < DIRECT:
            pl.when(p.inner)(lambda: self.z_got(1))
        if self.settle is not None:
            self.settle(self.block(p.y, p.x, p.c))
        for k in (3, 4, 7):
            self.xy(k).start()

    def pass_on(self, came, on, core):
        self.xy(came).wait_recv()
        for k in (on, core):
            if k is not None:
                self.xy(k).start()

    def finish(self):
        for k in (7, 8, 9, 10, 11):
            self.xy(k).wait_recv()

    def sent(self):
        p = self.p
        pl.when(p.z < 3)(lambda: self.z_wire(0).wait_send())
        self.z_wire(1).wait_send()
        pl.when(p.z > 0)(lambda: self.z_wire(2).wait_send())
        far = jnp.logical_not(p.inner) if self.i < DIRECT else p.inner
        pl.when(far)(lambda: self.z_wire(FAR).wait_send())
        for k in range(3, FAR):
            self.xy(k).wait_send()


class Rows:
    def __init__(self, place, parts, strip, send, recv):
        self.p, self.parts, self.strip, self.send, self.recv = place, parts, strip, send, recv
        self.strips, self.rows = parts.shape[0], parts.shape[1]
        self.pieces = parts.shape[2] // 256
        self.home = place.z - place.c
        self.is_home = (self.home >= 0) & (self.home < self.strips)

    def clip(self, s):
        return jnp.clip(s, 0, self.strips - 1)

    def at(self, z):
        return self.strip.at[ds(z * self.rows, self.rows)]

    def inward(self, k, j, owner, s):
        cols = pl.ds(k * 256, 256)
        return remote(
            self.parts.at[s, :, cols], self.strip.at[ds(owner * self.rows, self.rows), cols],
            self.send.at[k, j - 1], self.recv.at[k, j - 1], self.p.to_z(self.p.ahead(j)),
        )

    def in_start(self, k):
        p = self.p
        for j in range(1, p.groups):
            s = p.ahead(j) - p.c

            @pl.when((s >= 0) & (s < self.strips))
            def _():
                self.inward(k, j, p.z, self.clip(s)).start()

    def in_local(self):
        p = self.p

        @pl.when(self.is_home)
        def _():
            self.strip[ds(p.z * self.rows, self.rows), :] = self.parts[self.clip(self.home)]

        @pl.when(jnp.logical_not(self.is_home))
        def _():
            self.strip[...] = jnp.zeros_like(self.strip)

    def in_finish(self):
        p = self.p

        @pl.when(self.is_home)
        def _():
            for k in range(self.pieces):
                for j in range(1, p.groups):
                    self.inward(k, j, p.behind(j), 0).wait_recv()

    def in_sent(self):
        p = self.p
        for j in range(1, p.groups):
            s = p.ahead(j) - p.c

            @pl.when((s >= 0) & (s < self.strips))
            def _():
                for k in range(self.pieces):
                    self.inward(k, j, p.z, self.clip(s)).wait_send()

    def outward(self, j, s):
        z = self.p.ahead(j)
        return remote(
            self.at(z), self.parts.at[s], self.send.at[j - 1], self.recv.at[j - 1], self.p.to_z(z)
        )

    def out_start(self):
        p = self.p

        @pl.when(self.is_home)
        def _():
            home = self.clip(self.home)
            for j in range(1, p.groups):
                self.outward(j, home).start()
            self.parts[home] = self.strip[ds(p.z * self.rows, self.rows), :]

    def out_finish(self):
        p = self.p
        for j in range(1, p.groups):
            s = p.behind(j) - p.c

            @pl.when((s >= 0) & (s < self.strips))
            def _():
                self.outward(j, self.clip(s)).wait_recv()

        @pl.when(self.is_home)
        def _():
            for j in range(1, p.groups):
                self.outward(j, self.clip(self.home)).wait_send()


class Scatter:
    def __init__(self, place, index, part, bufs, out, send, recv):
        self.p, self.i, self.part = place, index, part
        self.core, self.r1, self.r2, self.q1, self.q2, self.zs, self.zr = bufs
        self.out, self.send, self.recv = out, send, recv
        self.k, self.u, self.n = self.q1.shape[0], self.core.shape[3], self.q1.shape[2]
        self.r = self.u // place.groups
        self.first, self.second = pl.ds(0, self.u // 2), pl.ds(self.u // 2, self.u // 2)

    def wire(self, k):
        p, i = self.p, self.i
        if k == 0:
            src, dst, to = self.part.at[:, :, :, 1 - p.c], self.core, p.to_c
        elif k == 1:
            src, dst, to = self.core.at[:, :, 1 - p.x, self.first], self.r1, p.to_x
        elif k == 2:
            src, dst, to = self.core.at[:, 1 - p.y, :, self.second], self.r2, p.to_y
        elif k == 3:
            src, dst, to = self.r1.at[:, 1 - p.y], self.q1, p.to_y
        elif k == 4:
            src, dst, to = self.r2.at[:, 1 - p.x], self.q2, p.to_x
        elif k < 8:
            z = (p.z + k - 4) % 4
            src, dst, to = self.zs.at[:, z], self.zr.at[k - 5], p.to_z(z)
        else:
            z = 1 + p.z // 3
            src, dst, to = self.zs.at[:, 3 - p.z], self.zr.at[3], p.to_z(z)
        return remote(src, dst, self.send.at[i, k], self.recv.at[i, k], to)

    def start(self):
        self.wire(0).start()

    def core_add(self):
        p = self.p
        self.wire(0).wait_recv()
        for k in range(self.k):
            for y in range(2):
                for x in range(2):
                    here = self.core.at[k, y, x]
                    here[...] = here[...] + self.part[k, y, x, p.c]
        self.wire(1).start()
        self.wire(2).start()

    def pass_x(self):
        p = self.p
        self.wire(1).wait_recv()
        for k in range(self.k):
            here = self.r1.at[k, 1 - p.y]
            here[...] = here[...] + self.core[k, 1 - p.y, p.x, self.first, :]
        self.wire(3).start()

    def pass_y(self):
        p = self.p
        self.wire(2).wait_recv()
        for k in range(self.k):
            here = self.r2.at[k, 1 - p.x]
            here[...] = here[...] + self.core[k, p.y, 1 - p.x, self.second, :]
        self.wire(4).start()

    def z_start(self):
        p, r = self.p, self.r
        half = self.u // 2
        self.wire(3).wait_recv()
        self.wire(4).wait_recv()
        per = p.groups // 2
        for k in range(self.k):
            for h in range(2):
                mine = self.r1.at[k, p.y] if h == 0 else self.r2.at[k, p.x]
                got = self.q1.at[k] if h == 0 else self.q2.at[k]
                value = self.core[k, p.y, p.x, pl.ds(h * half, half), :].astype(f32)
                value += mine[...].astype(f32) + got[...].astype(f32)
                slabs = value.reshape(per, r, self.n)
                self.zs[k, pl.ds(h * per, per)] = slabs.astype(bf16)
        pl.when(p.z < 3)(lambda: self.wire(5).start())
        pl.when(p.z > 0)(lambda: self.wire(7).start())

        @pl.when(jnp.logical_not(p.inner))
        def _():
            self.wire(6).start()
            self.wire(8).start()

    def z_pass(self):
        @pl.when(self.p.inner)
        def _():
            self.wire(8).wait_recv()
            z = (self.p.z + 2) % 4
            for k in range(self.k):
                self.zs[k, z] = self.zs[k, z] + self.zr[3, k]
            self.wire(6).start()

    def finish(self):
        p = self.p
        self.wire(6).wait_recv()
        for k in range(self.k):
            self.out[k][...] = self.zs[k, p.z].astype(f32) + self.zr[1, k].astype(f32)

        def more(wire, slot):
            self.wire(wire).wait_recv()
            for k in range(self.k):
                self.out[k][...] += self.zr[slot, k].astype(f32)

        pl.when(p.z > 0)(lambda: more(5, 0))
        pl.when(p.z < 3)(lambda: more(7, 2))

    def drain(self):
        p = self.p
        for k in (0, 1, 2, 3, 4, 6):
            self.wire(k).wait_send()
        pl.when(p.z < 3)(lambda: self.wire(5).wait_send())
        pl.when(p.z > 0)(lambda: self.wire(7).wait_send())
        pl.when(jnp.logical_not(p.inner))(lambda: self.wire(8).wait_send())


class Tally:
    def __init__(self, place, value, got, send, recv):
        self.p, self.value, self.got, self.send, self.recv = place, value, got, send, recv

    def copy(self, k):
        p = self.p
        to = (p.to_c, p.to_x, p.to_y)[k] if k < 3 else p.to_z(p.ahead(k - 2))
        return remote(
            self.value.at[min(k, 3)], self.got.at[k], self.send.at[k], self.recv.at[k], to
        )

    def start(self):
        self.copy(0).start()

    def step(self, k):
        self.copy(k).wait_recv()
        self.value[k + 1] = self.value[k] + self.got[k]
        if k < 2:
            self.copy(k + 1).start()
        else:
            for j in range(1, self.p.groups):
                self.copy(2 + j).start()

    def finish(self):
        value = self.value[3]
        for j in range(1, self.p.groups):
            self.copy(2 + j).wait_recv()
            value += self.got[2 + j]
        for k in range(2 + self.p.groups):
            self.copy(k).wait_send()
        return value


def normalize(v):
    mean = jnp.mean(v, axis=1, keepdims=True)
    centred = v - mean
    inv = lax.rsqrt(jnp.mean(centred * centred, axis=1, keepdims=True) + epsilon)
    return centred * inv, mean, inv


def norm_backward(grad, hat, inv, gain):
    t = grad * gain
    mean_t = jnp.mean(t, axis=1, keepdims=True)
    mean_th = jnp.mean(t * hat, axis=1, keepdims=True)
    return inv * (t - mean_t - hat * mean_th)


class Layer:
    def __init__(self, place, refs):
        self.__dict__.update(refs)
        self.p = place
        self.rows, self.d = self.x.shape
        self.hidden = self.act.shape[1]
        self.step = 96

    def vec(self, i):
        return self.vecs[i : i + 1, :]

    def weight(self, i, cols=slice(None)):
        value = self.w[i, :, :, :, :, cols]
        return value.reshape(self.d, value.shape[-1])

    def eighths(self, value):
        return value.reshape(2, 2, 2, value.shape[0] // 8, value.shape[1])

    def vectors(self):
        d, groups = self.d, self.p.groups
        per = d // (8 * groups)
        wide = self.hidden // (8 * groups)

        def spread(lanes, cols, width):
            lane = lax.broadcasted_iota(jnp.int32, (lanes, cols), 0)
            col = lax.broadcasted_iota(jnp.int32, (lanes, cols), 1)
            hit = (col == lane // 128 * width + lane % 128) & (lane % 128 < width)
            return jnp.where(hit, 1.0, 0.0).astype(bf16)

        half = spread(4 * groups * 128, d // 2, per)
        for h in range(2):
            slabs = [self.small[4 * h + b, z] for b in range(4) for z in range(groups)]
            self.vecs[:, h * (d // 2) : (h + 1) * (d // 2)] = nn(jnp.concatenate(slabs, 1), half)
        one = spread(groups * 128, groups * wide, wide)
        for b in range(8):
            slabs = [self.small[b, z] for z in range(groups)]
            row = nn(jnp.concatenate(slabs, 1), one)[10:11, :]
            self.b_up[:, b * groups * wide : (b + 1) * groups * wide] = row

    def mask(self, lengths, script_ids, key_mask):
        strips, length = key_mask.shape
        home = jnp.clip(self.p.z - self.p.c, 0, strips - 1)
        keys = jnp.zeros((1, length), jnp.int32)
        for s in range(strips):
            keys = jnp.where(home == s, key_mask[s : s + 1, :], keys)
        pos = lax.broadcasted_iota(jnp.int32, (1, length), 1)
        good = (pos == 0) | ((pos < lengths[home]) & (keys == 1))
        good = jnp.broadcast_to(jnp.where(good, 1.0, 0.0), (8, length)).astype(bf16)
        real = length // self.p.groups
        padded = self.rows // self.p.groups
        row = lax.broadcasted_iota(jnp.int32, (self.rows, length), 0)
        col = lax.broadcasted_iota(jnp.int32, (self.rows, length), 1)
        hit = (col == row // padded * real + row % padded) & (row % padded < real)
        self.valid[...] = nt(jnp.where(hit, 1.0, 0.0).astype(bf16), good)[:, 0:1]
        self.sid = script_ids[home]

    def norm1(self):
        self.emb[...] = jnp.where(self.sid == 1, self.vec(T1), self.vec(T0))

        def body(i):
            at = ds(i * self.step, self.step)
            hat, mean, inv = normalize(self.x[at, :].astype(f32) + self.emb[...])
            self.stats[at, 0:1] = mean
            self.stats[at, 1:2] = inv
            self.h1[at, :] = (hat * self.vec(G1) + self.vec(B1)).astype(bf16)

        loop(self.rows // self.step, body)

    def project(self, i, n=256):
        d = self.d

        def body(k):
            at = ds(k * n, n, 128)
            value = nn(self.h1[...], self.weight(QKV + i, at))
            if i != 1:
                value = value + self.vecs[QB if i == 0 else VB : (QB if i == 0 else VB) + 1, at]
            self.qkv[:, ds(i * d + k * n, n, 128)] = value.astype(bf16)

        loop(d // n, body)

    def half(self, h, value):
        lane = lax.broadcasted_iota(jnp.int32, value.shape, 1)
        return jnp.where(lane // DH == h, value, jnp.zeros_like(value))

    def pick(self, a, b):
        lane = lax.broadcasted_iota(jnp.int32, a.shape, 1)
        return jnp.where(lane < DH, a, b)

    def lanes(self, p):
        return [ds(i * self.d + p * 128, 128, 128) for i in range(3)]

    def probs_out(self, p):
        slot = p % 2
        return pltpu.make_async_copy(self.probs.at[slot], self.kept.at[p], self.out_sem.at[slot])

    def probs_in(self, p):
        slot = p % 2
        return pltpu.make_async_copy(self.kept.at[p], self.probs.at[slot], self.in_sem.at[slot])

    def attend(self, p):
        aq, ak, av = self.lanes(p)
        q = self.qkv[:, aq] * jnp.asarray(DH**-0.5, bf16)
        k, v = self.qkv[:, ak], self.qkv[:, av]
        valid = self.valid[...] > 0

        @pl.when(p >= 2)
        def _():
            self.probs_out(p - 2).wait()

        contexts = []
        for h in range(2):
            s = nt(k, self.half(h, q))
            s = jnp.where(valid, s, -1e9)
            e = jnp.exp(s - jnp.max(s, axis=0, keepdims=True))
            probs = (e * (1.0 / total(e))).astype(bf16)
            self.probs[p % 2, h] = probs
            contexts.append(tn(probs, v))
        self.ctx[:, ds(p * 128, 128, 128)] = self.pick(*contexts).astype(bf16)
        self.probs_out(p).start()

    def mid_norm(self, n=256):
        def body(k):
            at = ds(k * n, n, 128)
            self.mid[:, at] = nn(self.ctx[...], self.weight(OUT, at))

        loop(self.d // n, body)

        def norm(i):
            at = ds(i * self.step, self.step)
            v = self.x[at, :].astype(f32) + self.emb[...] + (self.mid[at, :] + self.vec(OB))
            self.mid[at, :] = v
            hat, mean, inv = normalize(v)
            self.stats[at, 2:3] = mean
            self.stats[at, 3:4] = inv
            self.h2[at, :] = (hat * self.vec(G2) + self.vec(B2)).astype(bf16)

        loop(self.rows // self.step, norm)

    def mlp_up(self, j, n=256):
        def body(k):
            at = ds(j * self.d + k * n, n, 128)
            pre = nn(self.h2[...], self.weight(UP + j, ds(k * n, n, 128))) + self.b_up[:, at]
            cum = 0.5 * (1.0 + lax.erf(pre * 2.0**-0.5))
            den = jnp.exp(-0.5 * pre * pre) * (2.0 * jnp.pi) ** -0.5
            self.act[:, at] = (pre * cum).astype(bf16)
            self.slope[:, at] = (cum + pre * den).astype(bf16)

        loop(self.d // n, body)

    def down(self, b):
        return self.w_down.at[b // 4, (b // 2) % 2, b % 2]

    def dw_down(self, b):
        u = self.hidden // 8
        grad = tn(self.act[:, ds(b * u, u, 128)], self.cot[...])
        self.p_down[0, b // 4, (b // 2) % 2, b % 2] = grad.astype(bf16)

    def grad_pre(self, b):
        u = self.hidden // 8
        at = ds(b * u, u, 128)
        g = (nt(self.cot[...], self.down(b)[...]) * self.slope[:, at].astype(f32)).astype(bf16)
        self.slope[:, at] = g
        self.up_sums[:, at] = total(g.astype(f32))

    def mlp_down(self):
        m = self.rows // 2

        def body(i):
            at = ds(i * m, m)
            value = self.mid[at, :] + self.vec(DB)
            for k in range(self.hidden // self.d):
                w = self.w_down[k // 2, k % 2].reshape(self.d, self.d)
                value = value + nn(self.act[at, pl.ds(k * self.d, self.d)], w)
            self.out[at, :] = value.astype(bf16)

        loop(2, body)

    def grad_h2(self, j):
        m = self.rows // 2

        def body(i):
            at = ds(i * m, m)
            value = nt(self.slope[at, ds(j * self.d, self.d, 128)], self.weight(UP + j))
            if j == 0:
                self.wide[at, :] = value
            else:
                self.wide[at, :] += value

        loop(2, body)

    def dw_up(self, j, n=256):
        def body(k):
            grad = tn(self.h2[...], self.slope[:, ds(j * self.d + k * n, n, 128)])
            self.w[UP + j, :, :, :, :, ds(k * n, n, 128)] = self.eighths(grad).astype(bf16)

        loop(self.d // n, body)

    def back2(self):
        zero = jnp.zeros((1, self.d), f32)

        def body(i, sums):
            at = ds(i * self.step, self.step)
            inv = self.stats[at, 3:4]
            hat = (self.mid[at, :] - self.stats[at, 2:3]) * inv
            g = self.wide[at, :]
            cot = self.cot[at, :].astype(f32)
            value = cot + norm_backward(g, hat, inv, self.vec(G2))
            self.mid[at, :] = value
            low = value.astype(bf16)
            self.gb[at, :] = low
            terms = (g * hat, g, cot, low.astype(f32))
            return tuple(s + total(t) for s, t in zip(sums, terms))

        sums = lax.fori_loop(0, self.rows // self.step, body, (zero,) * 4)
        for row, s in zip((G2, B2, DB, OB), sums):
            self.sums[row : row + 1, :] = s

    def grad_ctx(self):
        m = self.rows // 2

        def body(i):
            at = ds(i * m, m)
            self.gctx[at, :] = nt(self.gb[at, :], self.weight(OUT)).astype(bf16)

        loop(2, body)

    def dw_out(self, n=256):
        def body(k):
            at = ds(k * n, n, 128)
            grad = tn(self.ctx[...], self.gb[:, at])
            self.w[OUT, :, :, :, :, at] = self.eighths(grad).astype(bf16)

        loop(self.d // n, body)

    def attend_back(self, p, last):
        aq, ak, av = self.lanes(p)
        q, k, v = self.qkv[:, aq], self.qkv[:, ak], self.qkv[:, av]
        g = self.gctx[:, aq]

        @pl.when(p + 1 < last)
        def _():
            self.probs_in(p + 1).start()

        self.probs_in(p).wait()
        dq, dk, dv = [], [], []
        for h in range(2):
            probs = self.probs[p % 2, h]
            dv.append(nn(probs, g))
            grad = nt(v, self.half(h, g))
            wide = probs.astype(f32)
            grad = (wide * (grad - total(wide * grad))).astype(bf16)
            dk.append(nn(grad, q))
            dq.append(tn(grad, k))
        dq = (self.pick(*dq) * DH**-0.5).astype(bf16)
        dv = self.pick(*dv).astype(bf16)
        self.qkv[:, aq] = dq
        self.qkv[:, ak] = (self.pick(*dk) * DH**-0.5).astype(bf16)
        self.qkv[:, av] = dv
        self.sums[QB : QB + 1, aq] = total(dq.astype(f32))
        self.sums[VB : VB + 1, aq] = total(dv.astype(f32))

    def grad_h1(self, g, n=256):
        m = self.rows // 2

        def body(i):
            at = ds(i * m, m)
            value = None
            for k in range(3):
                w = self.weight(QKV + k, pl.ds(g * n, n))
                term = nt(self.qkv[at, pl.ds(k * self.d + g * n, n)], w)
                value = term if value is None else value + term
            if g == 0:
                self.wide[at, :] = value
            else:
                self.wide[at, :] += value

        loop(2, body)

    def dw_qkv(self, g, n=256):
        for k in range(3):
            grad = tn(self.h1[...], self.qkv[:, pl.ds(k * self.d + g * n, n)])
            self.w[QKV + k, :, :, :, :, pl.ds(g * n, n)] = self.eighths(grad).astype(bf16)

    def back1(self):
        zero = jnp.zeros((1, self.d), f32)

        def body(i, sums):
            at = ds(i * self.step, self.step)
            inv = self.stats[at, 1:2]
            hat = (self.x[at, :].astype(f32) + self.emb[...] - self.stats[at, 0:1]) * inv
            g = self.wide[at, :]
            value = self.mid[at, :] + norm_backward(g, hat, inv, self.vec(G1))
            self.gx[at, :] = value.astype(bf16)
            return tuple(s + total(t) for s, t in zip(sums, (g * hat, g, value)))

        sums = lax.fori_loop(0, self.rows // self.step, body, (zero,) * 3)
        self.sums[G1 : G1 + 1, :] = sums[0]
        self.sums[B1 : B1 + 1, :] = sums[1]
        self.sums[T0 : T0 + 1, :] = jnp.where(self.sid == 1, 0.0, sums[2])
        self.sums[T1 : T1 + 1, :] = jnp.where(self.sid == 1, sums[2], 0.0)


def pack(r):
    slab = r["s_small"]
    rows = [r[f"vec{i}"][...].astype(f32) for i in range(10)]
    rows = [jnp.pad(v, ((0, 0), (0, 128 - v.shape[1]))) for v in rows]
    slab[...] = jnp.concatenate(rows + [jnp.zeros((5, 128), f32)], axis=0).astype(bf16)


def kernel(outer, groups, names, *refs):
    r = dict(zip(names, refs, strict=True))
    p = Place(outer, groups)
    L = Layer(p, r)
    d, hidden = L.d, L.hidden
    nh = hidden // d
    real = r["patches"].shape[1]
    strips = r["patches"].shape[0]
    per = d // (8 * groups)
    u = d // 8
    n_down = d // 256
    w, w_down, stage = r["w"], r["w_down"], r["stage"]

    gs = []

    def add(shard, block, part, land, settle=None):
        gs.append(
            Gather(p, len(gs), shard, block, part, land, r["g_send"], r["g_recv"], settle)
        )

    add(
        r["s_small"],
        lambda y, x, c: r["small"].at[y * 4 + x * 2 + c],
        lambda ref, h: ref.at[pl.ds(h * (groups // 2), groups // 2)],
        lambda z: r["small"].at[p.y * 4 + p.x * 2 + p.c, z],
    )

    def add_square(i, shard):
        def settle(block):
            block[...] = stage[i].astype(f32).reshape(u, d).astype(bf16)

        add(
            shard,
            lambda y, x, c: w.at[i, y, x, c],
            lambda ref, h: ref.at[pl.ds(h * (u // 2), u // 2)],
            lambda z: stage.at[i, z],
            settle,
        )

    for i in range(3):
        add_square(QKV + i, r["s_qkv"].at[:, pl.ds(i * d, d)])
    add_square(OUT, r["s_out"])
    for i in range(nh):
        add_square(UP + i, r["s_up"].at[:, pl.ds(i * d, d)])
    hu = hidden // 8
    hr = hu // groups
    for i in range(n_down):
        cols = pl.ds(i * 256, 256)
        add(
            r["s_down"].at[:, cols],
            lambda y, x, c, cols=cols: w_down.at[y, x, c, :, cols],
            lambda ref, h: ref.at[pl.ds(h * (hu // 2), hu // 2)],
            lambda z, cols=cols: w_down.at[p.y, p.x, p.c, ds(z * hr, hr), cols],
        )
    xs = Rows(p, r["xp"], r["x"], r["x_send"], r["x_recv"])
    cs = Rows(p, r["cp"], r["cot"], r["c_send"], r["c_recv"])

    ss = []

    def give(part, bufs, out):
        ss.append(Scatter(p, len(ss), part, bufs, out, r["s_send"], r["s_recv"]))

    def bufs(kind, i):
        found = [r[f"{kind}_{name}"].at[i] for name in ("core", "r1", "r2", "q1", "q2")]
        if kind == "flat":
            slot = stage.at[pl.ds(UP + i if i < nh else OUT, 1)]
        elif kind == "head":
            slot = stage.at[pl.ds(QKV, 3), :, :, pl.ds(i * 256, 256)]
        else:
            slot = r["tall_zs"].at[i]
        return found + [slot, r[f"{kind}_zr"].at[i]]

    for i in range(n_down):
        cols = pl.ds(i * 256, 256)
        give(r["p_down"].at[:, :, :, :, :, cols], bufs("tall", i), [r["o_down"].at[:, cols]])
    for i in range(nh):
        give(w.at[pl.ds(UP + i, 1)], bufs("flat", i), [r["o_up"].at[:, pl.ds(i * d, d)]])
    give(w.at[pl.ds(OUT, 1)], bufs("flat", nh), [r["o_out"]])
    for g in range(d // 256):
        cols = pl.ds(g * 256, 256)
        outs = [r["o_qkv"].at[:, pl.ds(k * d + g * 256, 256)] for k in range(3)]
        give(w.at[pl.ds(QKV, 3), :, :, :, :, cols], bufs("head", g), outs)

    ys = Rows(p, r["xp"], r["out"], r["y_send"], r["y_recv"])
    rs = Rows(p, r["cp"], L.gx, r["d_send"], r["d_recv"])
    ts = Tally(p, r["value"], r["got"], r["t_send"], r["t_recv"])

    ends = {X_IN: xs, C_IN: cs, Y_OUT: ys, R_OUT: rs}
    gather = {SMALL: 0, WQ: 1, WK: 2, WV: 3, WO: 4, WU: 5, WD: 5 + nh}
    scatter = {GD: 0, GU: n_down, GO: n_down + nh, GQ: n_down + nh + 1}
    pairs = d // 128

    def prepare():
        for src, dst in ((r["patches"], r["xp"]), (r["cotangent"], r["cp"])):
            dst[...] = jnp.zeros_like(dst)
            for s in range(strips):
                dst[s, :real] = src[s]
        xs.in_local()
        cs.in_local()

    def sent():
        for g in gs:
            g.sent()
        cs.in_sent()

    def context_end():
        for i in (pairs - 2, pairs - 1):
            L.probs_out(i).wait()
        L.mid_norm()

    def rows_done():
        L.back1()
        r["sums"][10:16, :] = jnp.concatenate(
            [L.up_sums[:, j * d : (j + 1) * d] for j in range(nh)]
            + [jnp.zeros((6 - nh, d), f32)]
        )
        r["value"][0] = r["sums"][...]
        ts.start()

    def context_grad():
        L.grad_ctx()
        L.probs_in(0).start()

    once = {
        PREP: prepare, MASK: lambda: L.mask(r["lengths"], r["script_ids"], r["key_mask"]),
        VEC: L.vectors, NORM1: L.norm1, MID: context_end, DOWN: L.mlp_down, BACK2: L.back2,
        GCTX: context_grad, DWOUT: L.dw_out, BACK1: rows_done, SENT: sent,
        SENTX: xs.in_sent,
    }
    counted = {
        PROJ: L.project, UP_: L.mlp_up, GU_: L.grad_h2, DWUP: L.dw_up, GQ_: L.grad_h1,
        DWQKV: L.dw_qkv, T: ts.step,
    }
    looped = {
        ATT: L.attend, DWDOWN: L.dw_down, GPRE: L.grad_pre,
        ATTB: lambda i: L.attend_back(i, pairs),
    }

    def act(step):
        kind, name, i = step
        if kind == ROW:
            ends[name].in_start(i)
        elif kind == IN:
            ends[name].in_finish()
        elif kind == OUT_:
            ends[name].out_start()
        elif name in gather:
            g = gs[gather[name] + i]
            {
                ZS: g.z_start, ZF: g.z_far, ZE: g.z_end, FIN: g.finish,
                MX: lambda: g.pass_on(3, 6, 8), MY: lambda: g.pass_on(4, 5, 9),
                DX: lambda: g.pass_on(6, None, 10), DY: lambda: g.pass_on(5, None, 11),
            }[kind]()
        else:
            s = ss[scatter[name] + i]
            {
                ST: s.start, CA: s.core_add, PX: s.pass_x, PY: s.pass_y, ZT: s.z_start,
                ZP: s.z_pass, FI: s.finish,
            }[kind]()

    pack(r)
    p.greet()
    steps = list(SCHEDULE)
    while steps:
        kind, name, first = steps.pop(0)
        if name:
            act((kind, name, first))
        elif kind in once:
            once[kind]()
        elif kind in counted:
            counted[kind](first)
        else:
            n, between = 1, {}
            while True:
                k = 0
                while k < len(steps) and steps[k][1]:
                    k += 1
                if k == len(steps) or steps[k] != (kind, 0, first + n):
                    break
                between[n - 1] = steps[:k]
                steps = steps[k + 1 :]
                n += 1

            def body(i):
                looped[kind](first + i)
                for at, some in between.items():
                    if some:

                        @pl.when(i == at)
                        def _():
                            for step in some:
                                act(step)

            if n == 1:
                body(0)
            else:
                loop(n, body)

    ys.out_finish()
    for s in range(strips):
        r["o_out_rows"][s] = r["xp"][s, :real]
    r["o_tally"][...] = ts.finish()
    rs.out_finish()
    for s in range(strips):
        r["o_grad_rows"][s] = r["cp"][s, :real]
    for s in ss:
        s.drain()


def on_device(outer, groups, *args):
    (patches, cotangent, lengths, script_ids, key_mask, norm1_gain, norm1_bias, w_qkv, q_bias,
     v_bias, w_attn_out, attn_out_bias, norm2_gain, norm2_bias, w_up, up_bias, w_down, down_bias,
     script_table) = args
    strips, part_rows, d = patches.shape
    hidden = w_up.shape[1]
    parts = 8 * groups
    pad_rows = round_up(part_rows, 16)
    rows = groups * pad_rows
    vectors = [norm1_gain, norm1_bias, q_bias, v_bias, attn_out_bias, norm2_gain, norm2_bias,
               down_bias]
    weights = [w_qkv, w_attn_out, w_up, w_down]
    if outer > 1:
        mates = [[g * outer + i for i in range(outer)] for g in range(8)]
        seq = lax.axis_index("seq")

        def widen(a):
            a = lax.all_gather(a, ("seq",), axis=0, tiled=True)
            a = lax.all_gather(a, "dp", axis=0, tiled=True, axis_index_groups=mates)
            n = a.shape[0] // groups
            return lax.dynamic_slice_in_dim(a, seq * n, n, axis=0)

        vectors = [widen(a) for a in vectors]
        script_table = widen(script_table.T).T
        up_bias = widen(up_bias)
        weights = [widen(a) for a in weights]
    vectors = [v[None] for v in vectors] + [script_table, up_bias[None]]
    vm = pl.BlockSpec(memory_space=pltpu.VMEM)
    sm = pl.BlockSpec(memory_space=pltpu.SMEM)
    anywhere = pl.BlockSpec(memory_space=pl.ANY)
    sems = pltpu.SemaphoreType.DMA
    nh = hidden // d
    u, r, nd, ng = d // 8, d // parts, d // 256, d // 256
    ins = [f"vec{i}" for i in range(10)] + ["s_qkv", "s_out", "s_up", "s_down", "patches", "cotangent", "key_mask",
           "lengths", "script_ids"]
    outs = {
        "o_qkv": ((r, 3 * d), f32),
        "o_out": ((r, d), f32),
        "o_up": ((r, hidden), f32),
        "o_down": ((hidden // parts, d), f32),
        "o_tally": ((16, d), f32),
        "o_out_rows": (patches.shape, bf16),
        "o_grad_rows": (patches.shape, bf16),
        "kept": ((d // 128, 2, rows, rows), bf16),
    }
    scratch = {
        "small": ((8, groups, 16, 128), bf16),
        "s_small": ((16, 128), bf16),
        "stage": ((4 + nh, groups, r, d), bf16),
        "w": ((4 + nh, 2, 2, 2, u, d), bf16),
        "w_down": ((2, 2, 2, hidden // 8, d), bf16),
        "p_down": ((1, 2, 2, 2, hidden // 8, d), bf16),
        "xp": ((strips, pad_rows, d), bf16),
        "cp": ((strips, pad_rows, d), bf16),
        "x": ((rows, d), bf16),
        "cot": ((rows, d), bf16),
        "valid": ((rows, 1), f32),
        "vecs": ((16, d), f32),
        "b_up": ((1, hidden), f32),
        "up_sums": ((1, hidden), f32),
        "sums": ((16, d), f32),
        "emb": ((1, d), f32),
        "stats": ((rows, 4), f32),
        "h1": ((rows, d), bf16),
        "qkv": ((rows, 3 * d), bf16),
        "probs": ((2, 2, rows, rows), bf16),
        "ctx": ((rows, d), bf16),
        "mid": ((rows, d), f32),
        "wide": ((rows, d), f32),
        "h2": ((rows, d), bf16),
        "act": ((rows, hidden), bf16),
        "slope": ((rows, hidden), bf16),
        "value": ((4, 16, d), f32),
        "got": ((2 + groups, 16, d), f32),
    }
    for kind, count, k, uu, n in (
        ("tall", nd, 1, hidden // 8, 256),
        ("flat", nh + 1, 1, u, d),
        ("head", ng, 3, u, 256),
    ):
        rr = uu // groups
        scratch[f"{kind}_core"] = ((count, k, 2, 2, uu, n), bf16)
        scratch[f"{kind}_r1"] = ((count, k, 2, uu // 2, n), bf16)
        scratch[f"{kind}_r2"] = ((count, k, 2, uu // 2, n), bf16)
        scratch[f"{kind}_q1"] = ((count, k, uu // 2, n), bf16)
        scratch[f"{kind}_q2"] = ((count, k, uu // 2, n), bf16)
        if kind == "tall":
            scratch["tall_zs"] = ((count, k, groups, rr, n), bf16)
        scratch[f"{kind}_zr"] = ((count, groups, k, rr, n), bf16)
    n_gather = 5 + nh + nd
    n_scatter = nd + nh + 1 + ng
    semaphores = {
        "g_send": (n_gather, WIRE), "g_recv": (n_gather, WIRE),
        "s_send": (n_scatter, HOPS), "s_recv": (n_scatter, HOPS),
        "t_send": (2 + groups,), "t_recv": (2 + groups,),
        "out_sem": (2,), "in_sem": (2,),
    }
    for name in "xcyd":
        shape = (groups - 1,) if name in "yd" else (d // 256, groups - 1)
        semaphores[f"{name}_send"] = shape
        semaphores[f"{name}_recv"] = shape
    names = ins + list(outs) + list(scratch) + list(semaphores)

    def body(*refs):
        refs = dict(zip(names, refs, strict=True))
        act = refs["act"]
        for k, name in enumerate(("out", "gb", "gctx", "gx")):
            refs[name] = act.at[:, pl.ds(k * d, d)]
        kernel(outer, groups, list(refs), *refs.values())

    res = pl.pallas_call(
        body,
        out_shape=[jax.ShapeDtypeStruct(*s) for s in outs.values()],
        in_specs=[vm] * 17 + [sm] * 2,
        out_specs=[vm] * 7 + [anywhere],
        scratch_shapes=[pltpu.VMEM(*s) for s in scratch.values()]
        + [sems(s) for s in semaphores.values()],
        compiler_params=pltpu.CompilerParams(
            collective_id=0, has_side_effects=True, vmem_limit_bytes=63 * 2**20
        ),
    )(*vectors, *weights, patches, cotangent, key_mask, lengths, script_ids)
    shards = list(res[:4])
    tally = res[4]
    if outer > 1:

        def narrow(a):
            a = lax.psum(a, "dp", axis_index_groups=mates)
            a = lax.all_gather(a, ("seq",), axis=0, tiled=True)
            at = (lax.axis_index("dp") % outer) * groups + lax.axis_index("seq")
            n = a.shape[0] // groups // outer
            return lax.dynamic_slice_in_dim(a, at * n, n, axis=0)

        shards = [narrow(a) for a in shards]
        tally = lax.psum(tally, "dp", axis_index_groups=mates)
    n = d // (parts * outer)
    m = hidden // (parts * outer)
    passed = [res[5], res[6]] + (shards if outer == 1 else [])
    closed = pl.pallas_call(
        functools.partial(close, groups, nh),
        out_shape=[jax.ShapeDtypeStruct((1, n), f32)] * 8
        + [jax.ShapeDtypeStruct((2, n), f32), jax.ShapeDtypeStruct((1, m), f32)]
        + [jax.ShapeDtypeStruct(a.shape, a.dtype) for a in passed],
        in_specs=[vm] * (1 + len(passed)),
        out_specs=[vm] * (10 + len(passed)),
    )(tally, *passed)
    vec = [v.reshape(n) for v in closed[:8]]
    table, vup = closed[8], closed[9].reshape(m)
    if outer == 1:
        shards = closed[12:]
    return (
        closed[10], closed[11], vec[G1], vec[B1], shards[0], vec[QB], vec[VB], shards[1], vec[OB],
        vec[G2], vec[B2], shards[2], vup, shards[3], vec[DB], table,
    )


def close(groups, nh, tally, *refs):
    n_passed = (len(refs) - 10) // 2
    passed, outs = refs[:n_passed], refs[n_passed:]
    for src, dst in zip(passed, outs[10:], strict=True):
        dst[...] = src[...]
    me = lax.axis_index("dp") * groups + lax.axis_index("seq")
    d = tally.shape[1]
    n, m = outs[0].shape[1], outs[9].shape[1]
    mine = pltpu.roll(tally[...], lax.rem(d - me * n, d), 1)
    for i in range(8):
        outs[i][...] = mine[i : i + 1, :n]
    outs[8][...] = mine[T0 : T1 + 1, :n]
    row = jnp.zeros((8, d), f32)
    for i in range(nh):
        line = jnp.broadcast_to(tally[10 + i : 11 + i, :], (8, d))
        row = jnp.where(me * m // d == i, line, row)
    outs[9][...] = pltpu.roll(row, lax.rem(d - lax.rem(me * m, d), d), 1)[0:1, :m]


def solution(mesh):
    dp, seq = mesh.shape["dp"], mesh.shape["seq"]
    both = ("dp", "seq")
    one, two = P(both), P(both, None)
    rows = P("dp", "seq", None)
    return jax.shard_map(
        functools.partial(on_device, dp // 8, seq),
        mesh=mesh,
        in_specs=(
            rows, rows, P("dp"), P("dp"), P("dp", None), one, one, two, one, one, two, one, one,
            one, two, one, two, one, P(None, both),
        ),
        out_specs=(
            rows, rows, one, one, two, one, one, two, one, one, one, two, one, two, one,
            P(None, both),
        ),
        check_vma=False,
    )
```

```python
import functools

import jax
import jax.numpy as jnp
from jax import lax
from jax.experimental import pallas as pl
from jax.experimental.pallas import tpu as pltpu
from jax.sharding import PartitionSpec as P

DH = 64
MESH = pl.DeviceIdType.MESH
f32 = jnp.float32
bf16 = jnp.bfloat16
epsilon = 1e-06
WIRE = 13
FAR = 12
DIRECT = 2
HOPS = 9
QKV, OUT, UP = 0, 3, 4
G1, B1, QB, VB, OB, G2, B2, DB, T0, T1 = range(10)


def round_up(n, m):
    return (n + m - 1) // m * m


def ds(start, size, align=16):
    return pl.ds(pl.multiple_of(start, align), size)


def nn(a, b):
    return lax.dot_general(a, b, (((1,), (0,)), ((), ())), preferred_element_type=f32)


def nt(a, b):
    return lax.dot_general(a, b, (((1,), (1,)), ((), ())), preferred_element_type=f32)


def tn(a, b):
    return lax.dot_general(a, b, (((0,), (0,)), ((), ())), preferred_element_type=f32)


def loop(n, body):
    def step(i, carry):
        body(i)
        return carry

    lax.fori_loop(0, n, step, 0)


def total(v):
    return jnp.sum(v, axis=0, keepdims=True)


def remote(src, dst, send, recv, to):
    return pltpu.make_async_remote_copy(
        src_ref=src, dst_ref=dst, send_sem=send, recv_sem=recv, device_id=to, device_id_type=MESH
    )


(ZS, ZE, MX, MY, DX, DY, FIN, ST, CA, PX, PY, ZT, FI, ROW, IN, OUT_, ZF, ZP) = range(18)
(SMALL, WQ, WK, WV, WO, WU, WD, GD, GU, GO, GQ, X_IN, C_IN, Y_OUT, R_OUT) = range(1, 16)
(PREP, MASK, VEC, NORM1, PROJ, ATT, MID, UP_, DWDOWN, GPRE, DOWN, GU_, BACK2, GCTX, DWUP, ATTB,
 GQ_, DWQKV, BACK1, DWOUT, SENT, SENTX, T) = range(100, 123)
SCHEDULE = (
    (ZS, SMALL, 0), (ZS, WK, 0), (PREP, 0, 0), (ZS, WV, 0), (MASK, 0, 0), (ZS, WQ, 0),
    (ZE, SMALL, 0), (ZF, WK, 0), (ROW, X_IN, 0), (MX, SMALL, 0), (MY, SMALL, 0), (ZF, WV, 0),
    (DX, SMALL, 0), (DY, SMALL, 0), (ZE, WQ, 0), (ZE, WK, 0), (ZS, WU, 2), (FIN, SMALL, 0),
    (VEC, 0, 0), (ZS, WO, 0), (ROW, X_IN, 1), (ZE, WV, 0), (MX, WQ, 0), (MY, WQ, 0), (ZF, WU, 2),
    (MX, WK, 0), (ZS, WU, 0), (MY, WK, 0), (ZF, WO, 0), (ROW, X_IN, 2), (MX, WV, 0), (MY, WV, 0),
    (DX, WQ, 0), (DY, WQ, 0), (ZE, WU, 2), (DX, WK, 0), (DY, WK, 0), (ZF, WU, 0), (ZE, WO, 0),
    (ZS, WU, 1), (DX, WV, 0), (DY, WV, 0), (ZS, WU, 3), (MX, WU, 2), (ZS, WD, 0), (MY, WU, 2),
    (IN, X_IN, 0), (NORM1, 0, 0), (ZE, WU, 0), (FIN, WQ, 0), (PROJ, 0, 0), (ZS, WD, 2),
    (MX, WO, 0), (MY, WO, 0), (ZF, WU, 1), (FIN, WK, 0), (PROJ, 0, 1), (DX, WU, 2), (DY, WU, 2),
    (ZF, WU, 3), (FIN, WV, 0), (PROJ, 0, 2), (ROW, C_IN, 0), (ATT, 0, 0), (MX, WU, 0),
    (MY, WU, 0), (ZF, WD, 0), (ATT, 0, 1), (DX, WO, 0), (DY, WO, 0), (ZE, WU, 1), (ZE, WU, 3),
    (ZS, WD, 1), (ZF, WD, 2), (ATT, 0, 2), (DX, WU, 0), (DY, WU, 0), (ATT, 0, 3), (ROW, C_IN, 1),
    (ATT, 0, 4), (MX, WU, 1), (MY, WU, 1), (ZE, WD, 0), (ATT, 0, 5), (SENTX, 0, 0),
    (ROW, C_IN, 2), (MX, WU, 3), (MY, WU, 3), (ZF, WD, 1), (ZE, WD, 2), (FIN, WO, 0), (MID, 0, 0),
    (DX, WU, 1), (DY, WU, 1), (FIN, WU, 0), (UP_, 0, 0), (FIN, WU, 1), (UP_, 0, 1), (MX, WD, 0),
    (MY, WD, 0), (FIN, WU, 2), (UP_, 0, 2), (DX, WU, 3), (DY, WU, 3), (ZE, WD, 1), (FIN, WU, 3),
    (UP_, 0, 3), (IN, C_IN, 0), (DWDOWN, 0, 0), (MX, WD, 2), (MY, WD, 2), (DWDOWN, 0, 1),
    (DWDOWN, 0, 2), (DWDOWN, 0, 3), (DX, WD, 0), (DY, WD, 0), (DWDOWN, 0, 4), (DWDOWN, 0, 5),
    (DWDOWN, 0, 6), (DWDOWN, 0, 7), (ST, GD, 0), (ST, GD, 1), (ST, GD, 2), (MX, WD, 1),
    (MY, WD, 1), (CA, GD, 0), (DX, WD, 2), (DY, WD, 2), (CA, GD, 1), (CA, GD, 2), (DX, WD, 1),
    (DY, WD, 1), (FIN, WD, 0), (FIN, WD, 1), (FIN, WD, 2), (GPRE, 0, 0), (GPRE, 0, 1),
    (GPRE, 0, 2), (GPRE, 0, 3), (PX, GD, 0), (PY, GD, 0), (GPRE, 0, 4), (GPRE, 0, 5),
    (GPRE, 0, 6), (DOWN, 0, 0), (OUT_, Y_OUT, 0), (PX, GD, 1), (PY, GD, 1), (GPRE, 0, 7),
    (GU_, 0, 0), (SENT, 0, 0), (DWUP, 0, 0), (ST, GU, 0), (PX, GD, 2), (PY, GD, 2), (GU_, 0, 1),
    (GU_, 0, 2), (ZT, GD, 0), (DWUP, 0, 2), (ST, GU, 2), (ZT, GD, 1), (CA, GU, 0), (GU_, 0, 3),
    (BACK2, 0, 0), (ZT, GD, 2), (CA, GU, 2), (DWUP, 0, 1), (ST, GU, 1), (GCTX, 0, 0),
    (ATTB, 0, 0), (PX, GU, 0), (PY, GU, 0), (CA, GU, 1), (ATTB, 0, 1), (PX, GU, 2), (PY, GU, 2),
    (DWUP, 0, 3), (ST, GU, 3), (ZP, GD, 0), (GQ_, 0, 0), (ZT, GU, 0), (DWQKV, 0, 0), (ST, GQ, 0),
    (ZP, GD, 1), (CA, GU, 3), (ATTB, 0, 2), (FI, GD, 0), (ZP, GD, 2), (PX, GU, 1), (PY, GU, 1),
    (ZT, GU, 2), (CA, GQ, 0), (ATTB, 0, 3), (FI, GD, 1), (ZP, GU, 0), (ATTB, 0, 4), (FI, GD, 2),
    (PX, GU, 3), (PY, GU, 3), (ZT, GU, 1), (ATTB, 0, 5), (FI, GU, 0), (ZP, GU, 2), (GQ_, 0, 1),
    (PX, GQ, 0), (PY, GQ, 0), (DWQKV, 0, 1), (ST, GQ, 1), (ZP, GU, 1), (ZT, GU, 3), (GQ_, 0, 2),
    (BACK1, 0, 0), (OUT_, R_OUT, 0), (FI, GU, 2), (CA, GQ, 1), (T, 0, 0), (ZT, GQ, 0),
    (DWQKV, 0, 2), (ST, GQ, 2), (FI, GU, 1), (DWOUT, 0, 0), (T, 0, 1), (ST, GO, 0), (ZP, GU, 3),
    (CA, GQ, 2), (CA, GO, 0), (PX, GQ, 1), (PY, GQ, 1), (PX, GQ, 2), (T, 0, 2), (PY, GQ, 2),
    (PX, GO, 0), (PY, GO, 0), (ZT, GQ, 1), (ZT, GQ, 2), (ZT, GO, 0), (ZP, GQ, 0), (FI, GU, 3),
    (ZP, GQ, 1), (ZP, GQ, 2), (ZP, GO, 0), (FI, GQ, 0), (FI, GQ, 1), (FI, GQ, 2), (FI, GO, 0),
)


class Place:
    def __init__(self, outer, groups):
        self.dp = lax.axis_index("dp")
        self.z = lax.axis_index("seq")
        assert groups == 4
        self.groups = groups
        b = self.dp // outer
        self.c = b % 2
        self.x = (b // 2) % 2
        self.y = b // 4
        self.inner = (self.z == 1) | (self.z == 2)
        self.to_c = (self.dp + outer * (1 - 2 * self.c), self.z)
        self.to_x = (self.dp + outer * (2 - 4 * self.x), self.z)
        self.to_y = (self.dp + outer * (4 - 8 * self.y), self.z)

    def ahead(self, j):
        return (self.z + j) % self.groups

    def behind(self, j):
        return (self.z + self.groups - j) % self.groups

    def to_z(self, z):
        return (self.dp, z)

    def greet(self):
        barrier = pltpu.get_barrier_semaphore()
        peers = [self.to_c, self.to_x, self.to_y]
        peers += [self.to_z(self.ahead(j)) for j in range(1, self.groups)]
        for peer in peers:
            pl.semaphore_signal(barrier, inc=1, device_id=peer, device_id_type=MESH)
        pl.semaphore_wait(barrier, len(peers))


class Gather:
    def __init__(self, place, index, shard, block, part, land, send, recv, here, settle=None):
        self.p, self.i, self.shard = place, index, shard
        self.block, self.part, self.land, self.settle = block, part, land, settle
        self.send, self.recv, self.here = send, recv, here

    def copy(self, k, ref, to):
        return remote(ref, ref, self.send.at[self.i, k], self.recv.at[self.i, k], to)

    def z_wire(self, k):
        p, z = self.p, self.p.z
        if k < 3:
            src, owner, to = self.shard, z, ((z + 1) % 4, (z + 2) % 4, (z + 3) % 4)[k]
        elif self.i < DIRECT:
            src, owner, to = self.shard, z, 3 - z
        else:
            owner = (z + 2) % 4
            src, to = self.land(owner), (z + 1) % 4 * (z // 2)
        return remote(
            src, self.land(owner), self.send.at[self.i, k], self.recv.at[self.i, k], p.to_z(to)
        )

    def own(self):
        return pltpu.make_async_copy(self.shard, self.land(self.p.z), self.here.at[self.i])

    def z_got(self, k):
        z = self.p.z
        owner = ((z + 3) % 4, (z + 2) % 4, (z + 1) % 4)[k] if k < 3 else 3 - z
        ref = self.land(owner)
        remote(
            ref, ref, self.send.at[self.i, k], self.recv.at[self.i, k], self.p.to_z((z + 1) % 4)
        ).wait_recv()

    def z_start(self):
        p = self.p
        pl.when(p.z < 3)(lambda: self.z_wire(0).start())
        self.z_wire(1).start()
        pl.when(p.z > 0)(lambda: self.z_wire(2).start())
        if self.i < DIRECT:
            pl.when(jnp.logical_not(p.inner))(lambda: self.z_wire(FAR).start())
        self.own().start()

    def z_far(self):
        if self.i < DIRECT:
            return

        @pl.when(self.p.inner)
        def _():
            self.z_got(1)
            self.z_wire(FAR).start()

    def xy(self, k):
        p = self.p
        mx, my = 1 - p.x, 1 - p.y
        own = lambda: self.block(p.y, p.x, p.c)
        bx = lambda: self.block(p.y, mx, p.c)
        by = lambda: self.block(my, p.x, p.c)
        bd = lambda: self.block(my, mx, p.c)
        if k == 3:
            return self.copy(3, own(), p.to_x)
        if k == 4:
            return self.copy(4, own(), p.to_y)
        if k == 5:
            return self.copy(5, self.part(by(), 1), p.to_x)
        if k == 6:
            return self.copy(6, self.part(bx(), 0), p.to_y)
        if k == 7:
            return self.copy(7, own(), p.to_c)
        if k == 8:
            return self.copy(8, bx(), p.to_c)
        if k == 9:
            return self.copy(9, by(), p.to_c)
        return self.copy(k, self.part(bd(), k - 10), p.to_c)

    def z_end(self):
        p = self.p
        self.own().wait()
        pl.when(p.z > 0)(lambda: self.z_got(0))
        pl.when(p.z < 3)(lambda: self.z_got(2))

        @pl.when(jnp.logical_not(p.inner))
        def _():
            self.z_got(1)
            self.z_got(FAR)

        if self.i < DIRECT:
            pl.when(p.inner)(lambda: self.z_got(1))
        if self.settle is not None:
            self.settle(self.block(p.y, p.x, p.c))
        for k in (3, 4, 7):
            self.xy(k).start()

    def pass_on(self, came, on, core):
        self.xy(came).wait_recv()
        for k in (on, core):
            if k is not None:
                self.xy(k).start()

    def finish(self):
        for k in (7, 8, 9, 10, 11):
            self.xy(k).wait_recv()

    def sent(self):
        p = self.p
        pl.when(p.z < 3)(lambda: self.z_wire(0).wait_send())
        self.z_wire(1).wait_send()
        pl.when(p.z > 0)(lambda: self.z_wire(2).wait_send())
        far = jnp.logical_not(p.inner) if self.i < DIRECT else p.inner
        pl.when(far)(lambda: self.z_wire(FAR).wait_send())
        for k in range(3, FAR):
            self.xy(k).wait_send()


class Rows:
    def __init__(self, place, parts, strip, send, recv):
        self.p, self.parts, self.strip, self.send, self.recv = place, parts, strip, send, recv
        self.strips, self.rows = parts.shape[0], parts.shape[1]
        self.pieces = parts.shape[2] // 256
        self.home = place.z - place.c
        self.is_home = (self.home >= 0) & (self.home < self.strips)

    def clip(self, s):
        return jnp.clip(s, 0, self.strips - 1)

    def at(self, z):
        return self.strip.at[ds(z * self.rows, self.rows)]

    def inward(self, k, j, owner, s):
        cols = pl.ds(k * 256, 256)
        return remote(
            self.parts.at[s, :, cols], self.strip.at[ds(owner * self.rows, self.rows), cols],
            self.send.at[k, j - 1], self.recv.at[k, j - 1], self.p.to_z(self.p.ahead(j)),
        )

    def in_start(self, k):
        p = self.p
        for j in range(1, p.groups):
            s = p.ahead(j) - p.c

            @pl.when((s >= 0) & (s < self.strips))
            def _():
                self.inward(k, j, p.z, self.clip(s)).start()

    def in_local(self):
        p = self.p

        @pl.when(self.is_home)
        def _():
            self.strip[ds(p.z * self.rows, self.rows), :] = self.parts[self.clip(self.home)]

        @pl.when(jnp.logical_not(self.is_home))
        def _():
            self.strip[...] = jnp.zeros_like(self.strip)

    def in_finish(self):
        p = self.p

        @pl.when(self.is_home)
        def _():
            for k in range(self.pieces):
                for j in range(1, p.groups):
                    self.inward(k, j, p.behind(j), 0).wait_recv()

    def in_sent(self):
        p = self.p
        for j in range(1, p.groups):
            s = p.ahead(j) - p.c

            @pl.when((s >= 0) & (s < self.strips))
            def _():
                for k in range(self.pieces):
                    self.inward(k, j, p.z, self.clip(s)).wait_send()

    def outward(self, j, s):
        z = self.p.ahead(j)
        return remote(
            self.at(z), self.parts.at[s], self.send.at[j - 1], self.recv.at[j - 1], self.p.to_z(z)
        )

    def stay(self, home):
        return pltpu.make_async_copy(
            self.at(self.p.z), self.parts.at[home], self.send.at[self.p.groups - 1]
        )

    def out_start(self):
        p = self.p

        @pl.when(self.is_home)
        def _():
            home = self.clip(self.home)
            for j in range(1, p.groups):
                self.outward(j, home).start()
            self.stay(home).start()

    def out_finish(self):
        p = self.p
        for j in range(1, p.groups):
            s = p.behind(j) - p.c

            @pl.when((s >= 0) & (s < self.strips))
            def _():
                self.outward(j, self.clip(s)).wait_recv()

        @pl.when(self.is_home)
        def _():
            for j in range(1, p.groups):
                self.outward(j, self.clip(self.home)).wait_send()
            self.stay(self.clip(self.home)).wait()


class Scatter:
    def __init__(self, place, index, part, bufs, out, send, recv):
        self.p, self.i, self.part = place, index, part
        self.core, self.r1, self.r2, self.q1, self.q2, self.zs, self.zr = bufs
        self.out, self.send, self.recv = out, send, recv
        self.k, self.u, self.n = self.q1.shape[0], self.core.shape[3], self.q1.shape[2]
        self.r = self.u // place.groups
        self.first, self.second = pl.ds(0, self.u // 2), pl.ds(self.u // 2, self.u // 2)

    def wire(self, k):
        p, i = self.p, self.i
        if k == 0:
            src, dst, to = self.part.at[:, :, :, 1 - p.c], self.core, p.to_c
        elif k == 1:
            src, dst, to = self.core.at[:, :, 1 - p.x, self.first], self.r1, p.to_x
        elif k == 2:
            src, dst, to = self.core.at[:, 1 - p.y, :, self.second], self.r2, p.to_y
        elif k == 3:
            src, dst, to = self.r1.at[:, 1 - p.y], self.q1, p.to_y
        elif k == 4:
            src, dst, to = self.r2.at[:, 1 - p.x], self.q2, p.to_x
        elif k < 8:
            z = (p.z + k - 4) % 4
            src, dst, to = self.zs.at[:, z], self.zr.at[k - 5], p.to_z(z)
        else:
            z = 1 + p.z // 3
            src, dst, to = self.zs.at[:, 3 - p.z], self.zr.at[3], p.to_z(z)
        return remote(src, dst, self.send.at[i, k], self.recv.at[i, k], to)

    def start(self):
        self.wire(0).start()

    def core_add(self):
        p = self.p
        self.wire(0).wait_recv()
        for k in range(self.k):
            for y in range(2):
                for x in range(2):
                    here = self.core.at[k, y, x]
                    here[...] = here[...] + self.part[k, y, x, p.c]
        self.wire(1).start()
        self.wire(2).start()

    def pass_x(self):
        p = self.p
        self.wire(1).wait_recv()
        for k in range(self.k):
            here = self.r1.at[k, 1 - p.y]
            here[...] = here[...] + self.core[k, 1 - p.y, p.x, self.first, :]
        self.wire(3).start()

    def pass_y(self):
        p = self.p
        self.wire(2).wait_recv()
        for k in range(self.k):
            here = self.r2.at[k, 1 - p.x]
            here[...] = here[...] + self.core[k, p.y, 1 - p.x, self.second, :]
        self.wire(4).start()

    def z_start(self):
        p, r = self.p, self.r
        half = self.u // 2
        self.wire(3).wait_recv()
        self.wire(4).wait_recv()
        per = p.groups // 2
        for k in range(self.k):
            for h in range(2):
                mine = self.r1.at[k, p.y] if h == 0 else self.r2.at[k, p.x]
                got = self.q1.at[k] if h == 0 else self.q2.at[k]
                value = self.core[k, p.y, p.x, pl.ds(h * half, half), :].astype(f32)
                value += mine[...].astype(f32) + got[...].astype(f32)
                slabs = value.reshape(per, r, self.n)
                self.zs[k, pl.ds(h * per, per)] = slabs.astype(bf16)
        pl.when(p.z < 3)(lambda: self.wire(5).start())
        pl.when(p.z > 0)(lambda: self.wire(7).start())

        @pl.when(jnp.logical_not(p.inner))
        def _():
            self.wire(6).start()
            self.wire(8).start()

    def z_pass(self):
        @pl.when(self.p.inner)
        def _():
            self.wire(8).wait_recv()
            z = (self.p.z + 2) % 4
            for k in range(self.k):
                self.zs[k, z] = self.zs[k, z] + self.zr[3, k]
            self.wire(6).start()

    def finish(self):
        p = self.p
        self.wire(6).wait_recv()
        for k in range(self.k):
            self.out[k][...] = self.zs[k, p.z].astype(f32) + self.zr[1, k].astype(f32)

        def more(wire, slot):
            self.wire(wire).wait_recv()
            for k in range(self.k):
                self.out[k][...] += self.zr[slot, k].astype(f32)

        pl.when(p.z > 0)(lambda: more(5, 0))
        pl.when(p.z < 3)(lambda: more(7, 2))

    def drain(self):
        p = self.p
        for k in (0, 1, 2, 3, 4, 6):
            self.wire(k).wait_send()
        pl.when(p.z < 3)(lambda: self.wire(5).wait_send())
        pl.when(p.z > 0)(lambda: self.wire(7).wait_send())
        pl.when(jnp.logical_not(p.inner))(lambda: self.wire(8).wait_send())


class Tally:
    def __init__(self, place, value, got, send, recv):
        self.p, self.value, self.got, self.send, self.recv = place, value, got, send, recv

    def copy(self, k):
        p = self.p
        to = (p.to_c, p.to_x, p.to_y)[k] if k < 3 else p.to_z(p.ahead(k - 2))
        return remote(
            self.value.at[min(k, 3)], self.got.at[k], self.send.at[k], self.recv.at[k], to
        )

    def start(self):
        self.copy(0).start()

    def step(self, k):
        self.copy(k).wait_recv()
        self.value[k + 1] = self.value[k] + self.got[k]
        if k < 2:
            self.copy(k + 1).start()
        else:
            for j in range(1, self.p.groups):
                self.copy(2 + j).start()

    def finish(self):
        value = self.value[3]
        for j in range(1, self.p.groups):
            self.copy(2 + j).wait_recv()
            value += self.got[2 + j]
        for k in range(2 + self.p.groups):
            self.copy(k).wait_send()
        return value


def normalize(v):
    mean = jnp.mean(v, axis=1, keepdims=True)
    centred = v - mean
    inv = lax.rsqrt(jnp.mean(centred * centred, axis=1, keepdims=True) + epsilon)
    return centred * inv, mean, inv


def norm_backward(grad, hat, inv, gain):
    t = grad * gain
    mean_t = jnp.mean(t, axis=1, keepdims=True)
    mean_th = jnp.mean(t * hat, axis=1, keepdims=True)
    return inv * (t - mean_t - hat * mean_th)


class Layer:
    def __init__(self, place, refs):
        self.__dict__.update(refs)
        self.p = place
        self.rows, self.d = self.x.shape
        self.hidden = self.act.shape[1]
        self.step = 96

    def vec(self, i):
        return self.vecs[i : i + 1, :]

    def weight(self, i, cols=slice(None)):
        value = self.w[i, :, :, :, :, cols]
        return value.reshape(self.d, value.shape[-1])

    def eighths(self, value):
        return value.reshape(2, 2, 2, value.shape[0] // 8, value.shape[1])

    def vectors(self):
        d, groups = self.d, self.p.groups
        per = d // (8 * groups)
        wide = self.hidden // (8 * groups)

        def spread(lanes, cols, width):
            lane = lax.broadcasted_iota(jnp.int32, (lanes, cols), 0)
            col = lax.broadcasted_iota(jnp.int32, (lanes, cols), 1)
            hit = (col == lane // 128 * width + lane % 128) & (lane % 128 < width)
            return jnp.where(hit, 1.0, 0.0).astype(bf16)

        half = spread(4 * groups * 128, d // 2, per)
        for h in range(2):
            slabs = [self.small[4 * h + b, z] for b in range(4) for z in range(groups)]
            self.vecs[:, h * (d // 2) : (h + 1) * (d // 2)] = nn(jnp.concatenate(slabs, 1), half)
        one = spread(groups * 128, groups * wide, wide)
        for b in range(8):
            slabs = [self.small[b, z] for z in range(groups)]
            row = nn(jnp.concatenate(slabs, 1), one)[10:11, :]
            self.b_up[:, b * groups * wide : (b + 1) * groups * wide] = row

    def mask(self, lengths, script_ids, key_mask):
        strips, length = key_mask.shape
        home = jnp.clip(self.p.z - self.p.c, 0, strips - 1)
        keys = jnp.zeros((1, length), jnp.int32)
        for s in range(strips):
            keys = jnp.where(home == s, key_mask[s : s + 1, :], keys)
        pos = lax.broadcasted_iota(jnp.int32, (1, length), 1)
        good = (pos == 0) | ((pos < lengths[home]) & (keys == 1))
        good = jnp.broadcast_to(jnp.where(good, 1.0, 0.0), (8, length)).astype(bf16)
        real = length // self.p.groups
        padded = self.rows // self.p.groups
        row = lax.broadcasted_iota(jnp.int32, (self.rows, length), 0)
        col = lax.broadcasted_iota(jnp.int32, (self.rows, length), 1)
        hit = (col == row // padded * real + row % padded) & (row % padded < real)
        self.valid[...] = nt(jnp.where(hit, 1.0, 0.0).astype(bf16), good)[:, 0:1]
        self.sid = script_ids[home]

    def norm1(self):
        self.emb[...] = jnp.where(self.sid == 1, self.vec(T1), self.vec(T0))

        def body(i):
            at = ds(i * self.step, self.step)
            hat, mean, inv = normalize(self.x[at, :].astype(f32) + self.emb[...])
            self.stats[at, 0:1] = mean
            self.stats[at, 1:2] = inv
            self.h1[at, :] = (hat * self.vec(G1) + self.vec(B1)).astype(bf16)

        loop(self.rows // self.step, body)

    def project(self, i, n=256):
        d = self.d

        def body(k):
            at = ds(k * n, n, 128)
            value = nn(self.h1[...], self.weight(QKV + i, at))
            if i != 1:
                value = value + self.vecs[QB if i == 0 else VB : (QB if i == 0 else VB) + 1, at]
            self.qkv[:, ds(i * d + k * n, n, 128)] = value.astype(bf16)

        loop(d // n, body)

    def half(self, h, value):
        lane = lax.broadcasted_iota(jnp.int32, value.shape, 1)
        return jnp.where(lane // DH == h, value, jnp.zeros_like(value))

    def pick(self, a, b):
        lane = lax.broadcasted_iota(jnp.int32, a.shape, 1)
        return jnp.where(lane < DH, a, b)

    def lanes(self, p):
        return [ds(i * self.d + p * 128, 128, 128) for i in range(3)]

    def probs_out(self, p):
        slot = p % 2
        return pltpu.make_async_copy(self.probs.at[slot], self.kept.at[p], self.out_sem.at[slot])

    def probs_in(self, p):
        slot = p % 2
        return pltpu.make_async_copy(self.kept.at[p], self.probs.at[slot], self.in_sem.at[slot])

    def attend(self, p):
        aq, ak, av = self.lanes(p)
        q = self.qkv[:, aq] * jnp.asarray(DH**-0.5, bf16)
        k, v = self.qkv[:, ak], self.qkv[:, av]
        valid = self.valid[...] > 0

        @pl.when(p >= 2)
        def _():
            self.probs_out(p - 2).wait()

        contexts = []
        for h in range(2):
            s = nt(k, self.half(h, q))
            s = jnp.where(valid, s, -1e9)
            e = jnp.exp(s - jnp.max(s, axis=0, keepdims=True))
            probs = (e * (1.0 / total(e))).astype(bf16)
            self.probs[p % 2, h] = probs
            contexts.append(tn(probs, v))
        self.ctx[:, ds(p * 128, 128, 128)] = self.pick(*contexts).astype(bf16)
        self.probs_out(p).start()

    def mid_norm(self, n=256):
        def body(k):
            at = ds(k * n, n, 128)
            self.mid[:, at] = nn(self.ctx[...], self.weight(OUT, at))

        loop(self.d // n, body)

        def norm(i):
            at = ds(i * self.step, self.step)
            v = self.x[at, :].astype(f32) + self.emb[...] + (self.mid[at, :] + self.vec(OB))
            self.mid[at, :] = v
            hat, mean, inv = normalize(v)
            self.stats[at, 2:3] = mean
            self.stats[at, 3:4] = inv
            self.h2[at, :] = (hat * self.vec(G2) + self.vec(B2)).astype(bf16)

        loop(self.rows // self.step, norm)

    def mlp_up(self, j, n=256):
        def body(k):
            at = ds(j * self.d + k * n, n, 128)
            pre = nn(self.h2[...], self.weight(UP + j, ds(k * n, n, 128))) + self.b_up[:, at]
            cum = 0.5 * (1.0 + lax.erf(pre * 2.0**-0.5))
            den = jnp.exp(-0.5 * pre * pre) * (2.0 * jnp.pi) ** -0.5
            self.act[:, at] = (pre * cum).astype(bf16)
            self.slope[:, at] = (cum + pre * den).astype(bf16)

        loop(self.d // n, body)

    def down(self, b):
        return self.w_down.at[b // 4, (b // 2) % 2, b % 2]

    def dw_down(self, b):
        u = self.hidden // 8
        grad = tn(self.act[:, ds(b * u, u, 128)], self.cot[...])
        self.p_down[0, b // 4, (b // 2) % 2, b % 2] = grad.astype(bf16)

    def grad_pre(self, b):
        u = self.hidden // 8
        at = ds(b * u, u, 128)
        g = (nt(self.cot[...], self.down(b)[...]) * self.slope[:, at].astype(f32)).astype(bf16)
        self.slope[:, at] = g
        self.up_sums[:, at] = total(g.astype(f32))

    def mlp_down(self):
        m = self.rows // 2

        def body(i):
            at = ds(i * m, m)
            value = self.mid[at, :] + self.vec(DB)
            for k in range(self.hidden // self.d):
                w = self.w_down[k // 2, k % 2].reshape(self.d, self.d)
                value = value + nn(self.act[at, pl.ds(k * self.d, self.d)], w)
            self.out[at, :] = value.astype(bf16)

        loop(2, body)

    def grad_h2(self, j):
        m = self.rows // 2

        def body(i):
            at = ds(i * m, m)
            value = nt(self.slope[at, ds(j * self.d, self.d, 128)], self.weight(UP + j))
            if j == 0:
                self.wide[at, :] = value
            else:
                self.wide[at, :] += value

        loop(2, body)

    def dw_up(self, j, n=256):
        def body(k):
            grad = tn(self.h2[...], self.slope[:, ds(j * self.d + k * n, n, 128)])
            self.w[UP + j, :, :, :, :, ds(k * n, n, 128)] = self.eighths(grad).astype(bf16)

        loop(self.d // n, body)

    def back2(self):
        zero = jnp.zeros((1, self.d), f32)

        def body(i, sums):
            at = ds(i * self.step, self.step)
            inv = self.stats[at, 3:4]
            hat = (self.mid[at, :] - self.stats[at, 2:3]) * inv
            g = self.wide[at, :]
            cot = self.cot[at, :].astype(f32)
            value = cot + norm_backward(g, hat, inv, self.vec(G2))
            self.mid[at, :] = value
            low = value.astype(bf16)
            self.gb[at, :] = low
            terms = (g * hat, g, cot, low.astype(f32))
            return tuple(s + total(t) for s, t in zip(sums, terms))

        sums = lax.fori_loop(0, self.rows // self.step, body, (zero,) * 4)
        for row, s in zip((G2, B2, DB, OB), sums):
            self.sums[row : row + 1, :] = s

    def grad_ctx(self):
        m = self.rows // 2

        def body(i):
            at = ds(i * m, m)
            self.gctx[at, :] = nt(self.gb[at, :], self.weight(OUT)).astype(bf16)

        loop(2, body)

    def dw_out(self, n=256):
        def body(k):
            at = ds(k * n, n, 128)
            grad = tn(self.ctx[...], self.gb[:, at])
            self.w[OUT, :, :, :, :, at] = self.eighths(grad).astype(bf16)

        loop(self.d // n, body)

    def attend_back(self, p, last):
        aq, ak, av = self.lanes(p)
        q, k, v = self.qkv[:, aq], self.qkv[:, ak], self.qkv[:, av]
        g = self.gctx[:, aq]

        @pl.when(p + 1 < last)
        def _():
            self.probs_in(p + 1).start()

        self.probs_in(p).wait()
        dq, dk, dv = [], [], []
        for h in range(2):
            probs = self.probs[p % 2, h]
            dv.append(nn(probs, g))
            grad = nt(v, self.half(h, g))
            wide = probs.astype(f32)
            grad = (wide * (grad - total(wide * grad))).astype(bf16)
            dk.append(nn(grad, q))
            dq.append(tn(grad, k))
        dq = (self.pick(*dq) * DH**-0.5).astype(bf16)
        dv = self.pick(*dv).astype(bf16)
        self.qkv[:, aq] = dq
        self.qkv[:, ak] = (self.pick(*dk) * DH**-0.5).astype(bf16)
        self.qkv[:, av] = dv
        self.sums[QB : QB + 1, aq] = total(dq.astype(f32))
        self.sums[VB : VB + 1, aq] = total(dv.astype(f32))

    def grad_h1(self, g, n=256):
        m = self.rows // 2

        def body(i):
            at = ds(i * m, m)
            value = None
            for k in range(3):
                w = self.weight(QKV + k, pl.ds(g * n, n))
                term = nt(self.qkv[at, pl.ds(k * self.d + g * n, n)], w)
                value = term if value is None else value + term
            if g == 0:
                self.wide[at, :] = value
            else:
                self.wide[at, :] += value

        loop(2, body)

    def dw_qkv(self, g, n=256):
        for k in range(3):
            grad = tn(self.h1[...], self.qkv[:, pl.ds(k * self.d + g * n, n)])
            self.w[QKV + k, :, :, :, :, pl.ds(g * n, n)] = self.eighths(grad).astype(bf16)

    def back1(self):
        zero = jnp.zeros((1, self.d), f32)

        def body(i, sums):
            at = ds(i * self.step, self.step)
            inv = self.stats[at, 1:2]
            hat = (self.x[at, :].astype(f32) + self.emb[...] - self.stats[at, 0:1]) * inv
            g = self.wide[at, :]
            value = self.mid[at, :] + norm_backward(g, hat, inv, self.vec(G1))
            self.gx[at, :] = value.astype(bf16)
            return tuple(s + total(t) for s, t in zip(sums, (g * hat, g, value)))

        sums = lax.fori_loop(0, self.rows // self.step, body, (zero,) * 3)
        self.sums[G1 : G1 + 1, :] = sums[0]
        self.sums[B1 : B1 + 1, :] = sums[1]
        self.sums[T0 : T0 + 1, :] = jnp.where(self.sid == 1, 0.0, sums[2])
        self.sums[T1 : T1 + 1, :] = jnp.where(self.sid == 1, sums[2], 0.0)


def pack(r):
    slab = r["s_small"]
    rows = [r[f"vec{i}"][...].astype(f32) for i in range(10)]
    rows = [jnp.pad(v, ((0, 0), (0, 128 - v.shape[1]))) for v in rows]
    slab[...] = jnp.concatenate(rows + [jnp.zeros((5, 128), f32)], axis=0).astype(bf16)


def kernel(outer, groups, names, *refs):
    r = dict(zip(names, refs, strict=True))
    p = Place(outer, groups)
    L = Layer(p, r)
    d, hidden = L.d, L.hidden
    nh = hidden // d
    real = r["patches"].shape[1]
    strips = r["patches"].shape[0]
    per = d // (8 * groups)
    u = d // 8
    n_down = d // 256
    w, w_down, stage = r["w"], r["w_down"], r["stage"]

    gs = []

    def add(shard, block, part, land, settle=None):
        gs.append(
            Gather(
                p, len(gs), shard, block, part, land, r["g_send"], r["g_recv"], r["g_here"], settle
            )
        )

    add(
        r["s_small"],
        lambda y, x, c: r["small"].at[y * 4 + x * 2 + c],
        lambda ref, h: ref.at[pl.ds(h * (groups // 2), groups // 2)],
        lambda z: r["small"].at[p.y * 4 + p.x * 2 + p.c, z],
    )

    def add_square(i, shard):
        def settle(block):
            block[...] = stage[i].astype(f32).reshape(u, d).astype(bf16)

        add(
            shard,
            lambda y, x, c: w.at[i, y, x, c],
            lambda ref, h: ref.at[pl.ds(h * (u // 2), u // 2)],
            lambda z: stage.at[i, z],
            settle,
        )

    for i in range(3):
        add_square(QKV + i, r["s_qkv"].at[:, pl.ds(i * d, d)])
    add_square(OUT, r["s_out"])
    for i in range(nh):
        add_square(UP + i, r["s_up"].at[:, pl.ds(i * d, d)])
    hu = hidden // 8
    hr = hu // groups
    for i in range(n_down):
        cols = pl.ds(i * 256, 256)
        add(
            r["s_down"].at[:, cols],
            lambda y, x, c, cols=cols: w_down.at[y, x, c, :, cols],
            lambda ref, h: ref.at[pl.ds(h * (hu // 2), hu // 2)],
            lambda z, cols=cols: w_down.at[p.y, p.x, p.c, ds(z * hr, hr), cols],
        )
    xs = Rows(p, r["xp"], r["x"], r["x_send"], r["x_recv"])
    cs = Rows(p, r["cp"], r["cot"], r["c_send"], r["c_recv"])

    ss = []

    def give(part, bufs, out):
        ss.append(Scatter(p, len(ss), part, bufs, out, r["s_send"], r["s_recv"]))

    def bufs(kind, i):
        found = [r[f"{kind}_{name}"].at[i] for name in ("core", "r1", "r2", "q1", "q2")]
        if kind == "flat":
            slot = stage.at[pl.ds(UP + i if i < nh else OUT, 1)]
        elif kind == "head":
            slot = stage.at[pl.ds(QKV, 3), :, :, pl.ds(i * 256, 256)]
        else:
            slot = r["tall_zs"].at[i]
        return found + [slot, r[f"{kind}_zr"].at[i]]

    for i in range(n_down):
        cols = pl.ds(i * 256, 256)
        give(r["p_down"].at[:, :, :, :, :, cols], bufs("tall", i), [r["o_down"].at[:, cols]])
    for i in range(nh):
        give(w.at[pl.ds(UP + i, 1)], bufs("flat", i), [r["o_up"].at[:, pl.ds(i * d, d)]])
    give(w.at[pl.ds(OUT, 1)], bufs("flat", nh), [r["o_out"]])
    for g in range(d // 256):
        cols = pl.ds(g * 256, 256)
        outs = [r["o_qkv"].at[:, pl.ds(k * d + g * 256, 256)] for k in range(3)]
        give(w.at[pl.ds(QKV, 3), :, :, :, :, cols], bufs("head", g), outs)

    ys = Rows(p, r["o_out_rows"], r["out"], r["y_send"], r["y_recv"])
    rs = Rows(p, r["o_grad_rows"], L.gx, r["d_send"], r["d_recv"])
    ts = Tally(p, r["value"], r["got"], r["t_send"], r["t_recv"])

    ends = {X_IN: xs, C_IN: cs, Y_OUT: ys, R_OUT: rs}
    gather = {SMALL: 0, WQ: 1, WK: 2, WV: 3, WO: 4, WU: 5, WD: 5 + nh}
    scatter = {GD: 0, GU: n_down, GO: n_down + nh, GQ: n_down + nh + 1}
    pairs = d // 128

    fetch = [
        pltpu.make_async_copy(r[a], r[b], r["arg_sem"].at[i])
        for i, (a, b) in enumerate((("patches", "pin"), ("cotangent", "cin")))
    ]
    for copy in fetch:
        copy.start()

    def prepare():
        for copy, src, dst in zip(fetch, (r["pin"], r["cin"]), (r["xp"], r["cp"]), strict=True):
            copy.wait()
            dst[...] = jnp.zeros_like(dst)
            for s in range(strips):
                dst[s, :real] = src[s]
        xs.in_local()
        cs.in_local()

    def sent():
        for g in gs:
            g.sent()
        cs.in_sent()

    def context_end():
        for i in (pairs - 2, pairs - 1):
            L.probs_out(i).wait()
        L.mid_norm()

    def rows_done():
        L.back1()
        r["sums"][10:16, :] = jnp.concatenate(
            [L.up_sums[:, j * d : (j + 1) * d] for j in range(nh)]
            + [jnp.zeros((6 - nh, d), f32)]
        )
        r["value"][0] = r["sums"][...]
        ts.start()

    def context_grad():
        L.grad_ctx()
        L.probs_in(0).start()

    once = {
        PREP: prepare, MASK: lambda: L.mask(r["lengths"], r["script_ids"], r["key_mask"]),
        VEC: L.vectors, NORM1: L.norm1, MID: context_end, DOWN: L.mlp_down, BACK2: L.back2,
        GCTX: context_grad, DWOUT: L.dw_out, BACK1: rows_done, SENT: sent,
        SENTX: xs.in_sent,
    }
    counted = {
        PROJ: L.project, UP_: L.mlp_up, GU_: L.grad_h2, DWUP: L.dw_up, GQ_: L.grad_h1,
        DWQKV: L.dw_qkv, T: ts.step,
    }
    looped = {
        ATT: L.attend, DWDOWN: L.dw_down, GPRE: L.grad_pre,
        ATTB: lambda i: L.attend_back(i, pairs),
    }

    def act(step):
        kind, name, i = step
        if kind == ROW:
            ends[name].in_start(i)
        elif kind == IN:
            ends[name].in_finish()
        elif kind == OUT_:
            ends[name].out_start()
        elif name in gather:
            g = gs[gather[name] + i]
            {
                ZS: g.z_start, ZF: g.z_far, ZE: g.z_end, FIN: g.finish,
                MX: lambda: g.pass_on(3, 6, 8), MY: lambda: g.pass_on(4, 5, 9),
                DX: lambda: g.pass_on(6, None, 10), DY: lambda: g.pass_on(5, None, 11),
            }[kind]()
        else:
            s = ss[scatter[name] + i]
            {
                ST: s.start, CA: s.core_add, PX: s.pass_x, PY: s.pass_y, ZT: s.z_start,
                ZP: s.z_pass, FI: s.finish,
            }[kind]()

    pack(r)
    p.greet()
    steps = list(SCHEDULE)
    while steps:
        kind, name, first = steps.pop(0)
        if name:
            act((kind, name, first))
        elif kind in once:
            once[kind]()
        elif kind in counted:
            counted[kind](first)
        else:
            n, between = 1, {}
            while True:
                k = 0
                while k < len(steps) and steps[k][1]:
                    k += 1
                if k == len(steps) or steps[k] != (kind, 0, first + n):
                    break
                between[n - 1] = steps[:k]
                steps = steps[k + 1 :]
                n += 1

            def body(i):
                looped[kind](first + i)
                for at, some in between.items():
                    if some:

                        @pl.when(i == at)
                        def _():
                            for step in some:
                                act(step)

            if n == 1:
                body(0)
            else:
                loop(n, body)

    ys.out_finish()
    r["o_tally"][...] = ts.finish()
    rs.out_finish()
    for s in ss:
        s.drain()


def on_device(outer, groups, *args):
    (patches, cotangent, lengths, script_ids, key_mask, norm1_gain, norm1_bias, w_qkv, q_bias,
     v_bias, w_attn_out, attn_out_bias, norm2_gain, norm2_bias, w_up, up_bias, w_down, down_bias,
     script_table) = args
    strips, part_rows, d = patches.shape
    hidden = w_up.shape[1]
    parts = 8 * groups
    pad_rows = round_up(part_rows, 16)
    rows = groups * pad_rows
    vectors = [norm1_gain, norm1_bias, q_bias, v_bias, attn_out_bias, norm2_gain, norm2_bias,
               down_bias]
    weights = [w_qkv, w_attn_out, w_up, w_down]
    if outer > 1:
        mates = [[g * outer + i for i in range(outer)] for g in range(8)]
        seq = lax.axis_index("seq")

        def widen(a):
            a = lax.all_gather(a, ("seq",), axis=0, tiled=True)
            a = lax.all_gather(a, "dp", axis=0, tiled=True, axis_index_groups=mates)
            n = a.shape[0] // groups
            return lax.dynamic_slice_in_dim(a, seq * n, n, axis=0)

        vectors = [widen(a) for a in vectors]
        script_table = widen(script_table.T).T
        up_bias = widen(up_bias)
        weights = [widen(a) for a in weights]
    vectors = [v[None] for v in vectors] + [script_table, up_bias[None]]
    vm = pl.BlockSpec(memory_space=pltpu.VMEM)
    sm = pl.BlockSpec(memory_space=pltpu.SMEM)
    anywhere = pl.BlockSpec(memory_space=pl.ANY)
    sems = pltpu.SemaphoreType.DMA
    nh = hidden // d
    u, r, nd, ng = d // 8, d // parts, d // 256, d // 256
    ins = [f"vec{i}" for i in range(10)] + ["s_qkv", "s_out", "s_up", "s_down", "patches", "cotangent", "key_mask",
           "lengths", "script_ids"]
    outs = {
        "o_qkv": ((r, 3 * d), f32),
        "o_out": ((r, d), f32),
        "o_up": ((r, hidden), f32),
        "o_down": ((hidden // parts, d), f32),
        "o_tally": ((16, d), f32),
        "o_out_rows": ((strips, pad_rows, d), bf16),
        "o_grad_rows": ((strips, pad_rows, d), bf16),
        "kept": ((d // 128, 2, rows, rows), bf16),
    }
    scratch = {
        "small": ((8, groups, 16, 128), bf16),
        "s_small": ((16, 128), bf16),
        "stage": ((4 + nh, groups, r, d), bf16),
        "w": ((4 + nh, 2, 2, 2, u, d), bf16),
        "w_down": ((2, 2, 2, hidden // 8, d), bf16),
        "p_down": ((1, 2, 2, 2, hidden // 8, d), bf16),
        "pin": (patches.shape, bf16),
        "cin": (patches.shape, bf16),
        "xp": ((strips, pad_rows, d), bf16),
        "cp": ((strips, pad_rows, d), bf16),
        "x": ((rows, d), bf16),
        "cot": ((rows, d), bf16),
        "valid": ((rows, 1), f32),
        "vecs": ((16, d), f32),
        "b_up": ((1, hidden), f32),
        "up_sums": ((1, hidden), f32),
        "sums": ((16, d), f32),
        "emb": ((1, d), f32),
        "stats": ((rows, 4), f32),
        "h1": ((rows, d), bf16),
        "qkv": ((rows, 3 * d), bf16),
        "probs": ((2, 2, rows, rows), bf16),
        "ctx": ((rows, d), bf16),
        "mid": ((rows, d), f32),
        "wide": ((rows, d), f32),
        "h2": ((rows, d), bf16),
        "act": ((rows, hidden), bf16),
        "slope": ((rows, hidden), bf16),
        "value": ((4, 16, d), f32),
        "got": ((2 + groups, 16, d), f32),
    }
    for kind, count, k, uu, n in (
        ("tall", nd, 1, hidden // 8, 256),
        ("flat", nh + 1, 1, u, d),
        ("head", ng, 3, u, 256),
    ):
        rr = uu // groups
        scratch[f"{kind}_core"] = ((count, k, 2, 2, uu, n), bf16)
        scratch[f"{kind}_r1"] = ((count, k, 2, uu // 2, n), bf16)
        scratch[f"{kind}_r2"] = ((count, k, 2, uu // 2, n), bf16)
        scratch[f"{kind}_q1"] = ((count, k, uu // 2, n), bf16)
        scratch[f"{kind}_q2"] = ((count, k, uu // 2, n), bf16)
        if kind == "tall":
            scratch["tall_zs"] = ((count, k, groups, rr, n), bf16)
        scratch[f"{kind}_zr"] = ((count, groups, k, rr, n), bf16)
    n_gather = 5 + nh + nd
    n_scatter = nd + nh + 1 + ng
    semaphores = {
        "g_send": (n_gather, WIRE), "g_recv": (n_gather, WIRE),
        "s_send": (n_scatter, HOPS), "s_recv": (n_scatter, HOPS),
        "t_send": (2 + groups,), "t_recv": (2 + groups,),
        "out_sem": (2,), "in_sem": (2,), "g_here": (n_gather,), "arg_sem": (2,),
    }
    for name in "xcyd":
        shape = (groups,) if name in "yd" else (d // 256, groups - 1)
        semaphores[f"{name}_send"] = shape
        semaphores[f"{name}_recv"] = shape
    names = ins + list(outs) + list(scratch) + list(semaphores)

    def body(*refs):
        refs = dict(zip(names, refs, strict=True))
        act = refs["act"]
        for k, name in enumerate(("out", "gb", "gctx", "gx")):
            refs[name] = act.at[:, pl.ds(k * d, d)]
        kernel(outer, groups, list(refs), *refs.values())

    res = pl.pallas_call(
        body,
        out_shape=[jax.ShapeDtypeStruct(*s) for s in outs.values()],
        in_specs=[vm] * 10 + [anywhere] * 6 + [vm] + [sm] * 2,
        out_specs=[vm] * 5 + [anywhere] * 3,
        scratch_shapes=[pltpu.VMEM(*s) for s in scratch.values()]
        + [sems(s) for s in semaphores.values()],
        compiler_params=pltpu.CompilerParams(
            collective_id=0, has_side_effects=True, vmem_limit_bytes=63 * 2**20
        ),
    )(*vectors, *weights, patches, cotangent, key_mask, lengths, script_ids)
    shards = list(res[:4])
    tally = res[4]
    if outer > 1:

        def narrow(a):
            a = lax.psum(a, "dp", axis_index_groups=mates)
            a = lax.all_gather(a, ("seq",), axis=0, tiled=True)
            at = (lax.axis_index("dp") % outer) * groups + lax.axis_index("seq")
            n = a.shape[0] // groups // outer
            return lax.dynamic_slice_in_dim(a, at * n, n, axis=0)

        shards = [narrow(a) for a in shards]
        tally = lax.psum(tally, "dp", axis_index_groups=mates)
    n = d // (parts * outer)
    m = hidden // (parts * outer)
    passed = [res[5], res[6]] + (shards if outer == 1 else [])
    shapes = [patches.shape] * 2 + [a.shape for a in passed[2:]]
    closed = pl.pallas_call(
        functools.partial(close, groups, nh),
        out_shape=[jax.ShapeDtypeStruct((1, n), f32)] * 8
        + [jax.ShapeDtypeStruct((2, n), f32), jax.ShapeDtypeStruct((1, m), f32)]
        + [jax.ShapeDtypeStruct(n, a.dtype) for n, a in zip(shapes, passed, strict=True)],
        in_specs=[vm] * (1 + len(passed)),
        out_specs=[vm] * (10 + len(passed)),
    )(tally, *passed)
    vec = [v.reshape(n) for v in closed[:8]]
    table, vup = closed[8], closed[9].reshape(m)
    if outer == 1:
        shards = closed[12:]
    return (
        closed[10], closed[11], vec[G1], vec[B1], shards[0], vec[QB], vec[VB], shards[1], vec[OB],
        vec[G2], vec[B2], shards[2], vup, shards[3], vec[DB], table,
    )


def close(groups, nh, tally, *refs):
    n_passed = (len(refs) - 10) // 2
    passed, outs = refs[:n_passed], refs[n_passed:]
    for src, dst in zip(passed, outs[10:], strict=True):
        if len(src.shape) == 3:
            for s in range(src.shape[0]):
                dst[s] = src[s, : dst.shape[1]]
        else:
            dst[...] = src[...]
    me = lax.axis_index("dp") * groups + lax.axis_index("seq")
    d = tally.shape[1]
    n, m = outs[0].shape[1], outs[9].shape[1]
    mine = pltpu.roll(tally[...], lax.rem(d - me * n, d), 1)
    for i in range(8):
        outs[i][...] = mine[i : i + 1, :n]
    outs[8][...] = mine[T0 : T1 + 1, :n]
    row = jnp.zeros((8, d), f32)
    for i in range(nh):
        line = jnp.broadcast_to(tally[10 + i : 11 + i, :], (8, d))
        row = jnp.where(me * m // d == i, line, row)
    outs[9][...] = pltpu.roll(row, lax.rem(d - lax.rem(me * m, d), d), 1)[0:1, :m]


def solution(mesh):
    dp, seq = mesh.shape["dp"], mesh.shape["seq"]
    both = ("dp", "seq")
    one, two = P(both), P(both, None)
    rows = P("dp", "seq", None)
    return jax.shard_map(
        functools.partial(on_device, dp // 8, seq),
        mesh=mesh,
        in_specs=(
            rows, rows, P("dp"), P("dp"), P("dp", None), one, one, two, one, one, two, one, one,
            one, two, one, two, one, P(None, both),
        ),
        out_specs=(
            rows, rows, one, one, two, one, one, two, one, one, one, two, one, two, one,
            P(None, both),
        ),
        check_vma=False,
    )
```

```python
import functools

import jax
import jax.numpy as jnp
from jax import lax
from jax.experimental import pallas as pl
from jax.experimental.pallas import tpu as pltpu
from jax.sharding import PartitionSpec as P

DH = 64
MESH = pl.DeviceIdType.MESH
f32 = jnp.float32
bf16 = jnp.bfloat16
epsilon = 1e-06
WIRE = 13
FAR = 12
DIRECT = 2
HOPS = 9
QKV, OUT, UP = 0, 3, 4
G1, B1, QB, VB, OB, G2, B2, DB, T0, T1 = range(10)


def round_up(n, m):
    return (n + m - 1) // m * m


def ds(start, size, align=16):
    return pl.ds(pl.multiple_of(start, align), size)


def nn(a, b):
    return lax.dot_general(a, b, (((1,), (0,)), ((), ())), preferred_element_type=f32)


def nt(a, b):
    return lax.dot_general(a, b, (((1,), (1,)), ((), ())), preferred_element_type=f32)


def tn(a, b):
    return lax.dot_general(a, b, (((0,), (0,)), ((), ())), preferred_element_type=f32)


def loop(n, body):
    def step(i, carry):
        body(i)
        return carry

    lax.fori_loop(0, n, step, 0)


def total(v):
    return jnp.sum(v, axis=0, keepdims=True)


def remote(src, dst, send, recv, to):
    return pltpu.make_async_remote_copy(
        src_ref=src, dst_ref=dst, send_sem=send, recv_sem=recv, device_id=to, device_id_type=MESH
    )


(ZS, ZE, MX, MY, DX, DY, FIN, ST, CA, PX, PY, ZT, FI, ROW, IN, OUT_, ZF, ZP) = range(18)
(SMALL, WQ, WK, WV, WO, WU, WD, GD, GU, GO, GQ, X_IN, C_IN, Y_OUT, R_OUT) = range(1, 16)
(PREP, MASK, VEC, NORM1, PROJ, ATT, MID, UP_, DWDOWN, GPRE, DOWN, GU_, BACK2, GCTX, DWUP, ATTB,
 GQ_, DWQKV, BACK1, DWOUT, SENT, SENTX, T) = range(100, 123)
SCHEDULE = (
    (ZS, SMALL, 0), (ZS, WK, 0), (PREP, 0, 0), (ZS, WV, 0), (MASK, 0, 0), (ZS, WQ, 0),
    (ZE, SMALL, 0), (ZS, WU, 1), (ZF, WK, 0), (ZS, WU, 3), (MX, SMALL, 0), (MY, SMALL, 0),
    (ZF, WV, 0), (ZS, WO, 0), (ZE, WQ, 0), (DX, SMALL, 0), (DY, SMALL, 0), (ROW, X_IN, 0),
    (ZF, WU, 1), (FIN, SMALL, 0), (VEC, 0, 0), (ZE, WK, 0), (ZF, WU, 3), (ZE, WV, 0), (ZS, WU, 0),
    (MX, WQ, 0), (MY, WQ, 0), (ZF, WO, 0), (ROW, X_IN, 1), (MX, WK, 0), (MY, WK, 0), (ZE, WU, 1),
    (ZE, WU, 3), (MX, WV, 0), (MY, WV, 0), (ZS, WU, 2), (ZF, WU, 0), (DX, WQ, 0), (DY, WQ, 0),
    (ZE, WO, 0), (ROW, X_IN, 2), (DX, WK, 0), (DY, WK, 0), (MX, WU, 1), (MY, WU, 1), (ZS, WD, 2),
    (ZF, WU, 2), (ZE, WU, 0), (MX, WU, 3), (MY, WU, 3), (ZS, WD, 1), (DX, WV, 0), (DY, WV, 0),
    (ZS, WD, 0), (IN, X_IN, 0), (NORM1, 0, 0), (MX, WO, 0), (MY, WO, 0), (FIN, WQ, 0),
    (PROJ, 0, 0), (DX, WU, 1), (DY, WU, 1), (ZF, WD, 2), (FIN, WK, 0), (PROJ, 0, 1),
    (ROW, C_IN, 0), (ZE, WU, 2), (FIN, WV, 0), (PROJ, 0, 2), (ATT, 0, 0), (MX, WU, 0),
    (MY, WU, 0), (ZF, WD, 1), (ATT, 0, 1), (ROW, C_IN, 1), (DY, WO, 0), (DX, WO, 0), (DX, WU, 3),
    (DY, WU, 3), (ZF, WD, 0), (ZE, WD, 2), (ATT, 0, 2), (ATT, 0, 3), (MX, WU, 2), (MY, WU, 2),
    (ATT, 0, 4), (SENTX, 0, 0), (ROW, C_IN, 2), (DX, WU, 0), (DY, WU, 0), (ZE, WD, 1),
    (ATT, 0, 5), (FIN, WO, 0), (MID, 0, 0), (DX, WU, 2), (DY, WU, 2), (ZE, WD, 0), (MX, WD, 2),
    (MY, WD, 2), (FIN, WU, 0), (UP_, 0, 0), (FIN, WU, 1), (UP_, 0, 1), (FIN, WU, 2), (UP_, 0, 2),
    (MX, WD, 1), (MY, WD, 1), (FIN, WU, 3), (UP_, 0, 3), (IN, C_IN, 0), (DWDOWN, 0, 0),
    (DWDOWN, 0, 1), (DWDOWN, 0, 2), (MX, WD, 0), (MY, WD, 0), (DWDOWN, 0, 3), (ST, GD, 0),
    (ST, GD, 1), (ST, GD, 2), (DX, WD, 2), (DY, WD, 2), (DX, WD, 1), (DY, WD, 1), (CA, GD, 0),
    (DX, WD, 0), (DY, WD, 0), (CA, GD, 1), (CA, GD, 2), (FIN, WD, 0), (FIN, WD, 1), (FIN, WD, 2),
    (GPRE, 0, 0), (GPRE, 0, 1), (GPRE, 0, 2), (DOWN, 0, 0), (OUT_, Y_OUT, 0), (PX, GD, 0),
    (PY, GD, 0), (GPRE, 0, 3), (PX, GD, 1), (PY, GD, 1), (GU_, 0, 0), (GU_, 0, 1), (GU_, 0, 2),
    (SENT, 0, 0), (DWUP, 0, 2), (ST, GU, 2), (GU_, 0, 3), (PX, GD, 2), (PY, GD, 2), (DWUP, 0, 0),
    (ST, GU, 0), (BACK2, 0, 0), (ZT, GD, 0), (CA, GU, 2), (GCTX, 0, 0), (ZT, GD, 1), (CA, GU, 0),
    (DWUP, 0, 3), (ST, GU, 3), (ATTB, 0, 0), (ZT, GD, 2), (DWUP, 0, 1), (ST, GU, 1), (CA, GU, 3),
    (ATTB, 0, 1), (PX, GU, 2), (PY, GU, 2), (ATTB, 0, 2), (PX, GU, 0), (PY, GU, 0), (CA, GU, 1),
    (GQ_, 0, 0), (ZP, GD, 0), (DWQKV, 0, 0), (ST, GQ, 0), (ZP, GD, 1), (PX, GU, 3), (PY, GU, 3),
    (ATTB, 0, 3), (ZP, GD, 2), (ZT, GU, 2), (ATTB, 0, 4), (FI, GD, 0), (ZT, GU, 0), (CA, GQ, 0),
    (GQ_, 0, 1), (FI, GD, 1), (ATTB, 0, 5), (FI, GD, 2), (PX, GU, 1), (PY, GU, 1), (ZT, GU, 3),
    (GQ_, 0, 2), (ZP, GU, 2), (DWQKV, 0, 2), (ST, GQ, 2), (ZP, GU, 0), (BACK1, 0, 0),
    (OUT_, R_OUT, 0), (PX, GQ, 0), (PY, GQ, 0), (T, 0, 0), (DWOUT, 0, 0), (ST, GO, 0), (ZT, GU, 1),
    (ZP, GU, 3), (CA, GQ, 2), (T, 0, 1), (DWQKV, 0, 1), (ST, GQ, 1), (FI, GU, 0), (FI, GU, 2),
    (CA, GO, 0), (ZT, GQ, 0), (CA, GQ, 1), (T, 0, 2), (PX, GQ, 2), (PY, GQ, 2), (PX, GO, 0),
    (PY, GO, 0), (PX, GQ, 1), (PY, GQ, 1), (ZT, GQ, 2), (ZT, GO, 0), (ZP, GU, 1), (ZT, GQ, 1),
    (FI, GU, 3), (ZP, GQ, 0), (ZP, GQ, 2), (ZP, GO, 0), (FI, GU, 1), (ZP, GQ, 1), (FI, GQ, 0),
    (FI, GQ, 2), (FI, GO, 0), (FI, GQ, 1),
)


class Place:
    def __init__(self, outer, groups):
        self.dp = lax.axis_index("dp")
        self.z = lax.axis_index("seq")
        assert groups == 4
        self.groups = groups
        b = self.dp // outer
        self.c = b % 2
        self.x = (b // 2) % 2
        self.y = b // 4
        self.inner = (self.z == 1) | (self.z == 2)
        self.to_c = (self.dp + outer * (1 - 2 * self.c), self.z)
        self.to_x = (self.dp + outer * (2 - 4 * self.x), self.z)
        self.to_y = (self.dp + outer * (4 - 8 * self.y), self.z)

    def ahead(self, j):
        return (self.z + j) % self.groups

    def behind(self, j):
        return (self.z + self.groups - j) % self.groups

    def to_z(self, z):
        return (self.dp, z)

    def greet(self):
        barrier = pltpu.get_barrier_semaphore()
        peers = [self.to_c, self.to_x, self.to_y]
        peers += [self.to_z(self.ahead(j)) for j in range(1, self.groups)]
        for peer in peers:
            pl.semaphore_signal(barrier, inc=1, device_id=peer, device_id_type=MESH)
        pl.semaphore_wait(barrier, len(peers))


class Gather:
    def __init__(self, place, index, shard, block, part, land, send, recv, here, settle=None):
        self.p, self.i, self.shard = place, index, shard
        self.block, self.part, self.land, self.settle = block, part, land, settle
        self.send, self.recv, self.here = send, recv, here

    def copy(self, k, ref, to):
        return remote(ref, ref, self.send.at[self.i, k], self.recv.at[self.i, k], to)

    def z_wire(self, k):
        p, z = self.p, self.p.z
        if k < 3:
            src, owner, to = self.shard, z, ((z + 1) % 4, (z + 2) % 4, (z + 3) % 4)[k]
        elif self.i < DIRECT:
            src, owner, to = self.shard, z, 3 - z
        else:
            owner = (z + 2) % 4
            src, to = self.land(owner), (z + 1) % 4 * (z // 2)
        return remote(
            src, self.land(owner), self.send.at[self.i, k], self.recv.at[self.i, k], p.to_z(to)
        )

    def own(self):
        return pltpu.make_async_copy(self.shard, self.land(self.p.z), self.here.at[self.i])

    def z_got(self, k):
        z = self.p.z
        owner = ((z + 3) % 4, (z + 2) % 4, (z + 1) % 4)[k] if k < 3 else 3 - z
        ref = self.land(owner)
        remote(
            ref, ref, self.send.at[self.i, k], self.recv.at[self.i, k], self.p.to_z((z + 1) % 4)
        ).wait_recv()

    def z_start(self):
        p = self.p
        pl.when(p.z < 3)(lambda: self.z_wire(0).start())
        self.z_wire(1).start()
        pl.when(p.z > 0)(lambda: self.z_wire(2).start())
        if self.i < DIRECT:
            pl.when(jnp.logical_not(p.inner))(lambda: self.z_wire(FAR).start())
        self.own().start()

    def z_far(self):
        if self.i < DIRECT:
            return

        @pl.when(self.p.inner)
        def _():
            self.z_got(1)
            self.z_wire(FAR).start()

    def xy(self, k):
        p = self.p
        mx, my = 1 - p.x, 1 - p.y
        own = lambda: self.block(p.y, p.x, p.c)
        bx = lambda: self.block(p.y, mx, p.c)
        by = lambda: self.block(my, p.x, p.c)
        bd = lambda: self.block(my, mx, p.c)
        if k == 3:
            return self.copy(3, own(), p.to_x)
        if k == 4:
            return self.copy(4, own(), p.to_y)
        if k == 5:
            return self.copy(5, self.part(by(), 1), p.to_x)
        if k == 6:
            return self.copy(6, self.part(bx(), 0), p.to_y)
        if k == 7:
            return self.copy(7, own(), p.to_c)
        if k == 8:
            return self.copy(8, bx(), p.to_c)
        if k == 9:
            return self.copy(9, by(), p.to_c)
        return self.copy(k, self.part(bd(), k - 10), p.to_c)

    def z_end(self):
        p = self.p
        self.own().wait()
        pl.when(p.z > 0)(lambda: self.z_got(0))
        pl.when(p.z < 3)(lambda: self.z_got(2))

        @pl.when(jnp.logical_not(p.inner))
        def _():
            self.z_got(1)
            self.z_got(FAR)

        if self.i < DIRECT:
            pl.when(p.inner)(lambda: self.z_got(1))
        if self.settle is not None:
            self.settle(self.block(p.y, p.x, p.c))
        for k in (3, 4, 7):
            self.xy(k).start()

    def pass_on(self, came, on, core):
        self.xy(came).wait_recv()
        for k in (on, core):
            if k is not None:
                self.xy(k).start()

    def finish(self):
        for k in (7, 8, 9, 10, 11):
            self.xy(k).wait_recv()

    def sent(self):
        p = self.p
        pl.when(p.z < 3)(lambda: self.z_wire(0).wait_send())
        self.z_wire(1).wait_send()
        pl.when(p.z > 0)(lambda: self.z_wire(2).wait_send())
        far = jnp.logical_not(p.inner) if self.i < DIRECT else p.inner
        pl.when(far)(lambda: self.z_wire(FAR).wait_send())
        for k in range(3, FAR):
            self.xy(k).wait_send()


class Rows:
    def __init__(self, place, parts, strip, send, recv):
        self.p, self.parts, self.strip, self.send, self.recv = place, parts, strip, send, recv
        self.strips, self.rows = parts.shape[0], parts.shape[1]
        self.pieces = parts.shape[2] // 256
        self.home = place.z - place.c
        self.is_home = (self.home >= 0) & (self.home < self.strips)

    def clip(self, s):
        return jnp.clip(s, 0, self.strips - 1)

    def at(self, z):
        return self.strip.at[ds(z * self.rows, self.rows)]

    def inward(self, k, j, owner, s):
        cols = pl.ds(k * 256, 256)
        return remote(
            self.parts.at[s, :, cols], self.strip.at[ds(owner * self.rows, self.rows), cols],
            self.send.at[k, j - 1], self.recv.at[k, j - 1], self.p.to_z(self.p.ahead(j)),
        )

    def in_start(self, k):
        p = self.p
        for j in range(1, p.groups):
            s = p.ahead(j) - p.c

            @pl.when((s >= 0) & (s < self.strips))
            def _():
                self.inward(k, j, p.z, self.clip(s)).start()

    def in_local(self):
        p = self.p

        @pl.when(self.is_home)
        def _():
            self.strip[ds(p.z * self.rows, self.rows), :] = self.parts[self.clip(self.home)]

        @pl.when(jnp.logical_not(self.is_home))
        def _():
            self.strip[...] = jnp.zeros_like(self.strip)

    def in_finish(self):
        p = self.p

        @pl.when(self.is_home)
        def _():
            for k in range(self.pieces):
                for j in range(1, p.groups):
                    self.inward(k, j, p.behind(j), 0).wait_recv()

    def in_sent(self):
        p = self.p
        for j in range(1, p.groups):
            s = p.ahead(j) - p.c

            @pl.when((s >= 0) & (s < self.strips))
            def _():
                for k in range(self.pieces):
                    self.inward(k, j, p.z, self.clip(s)).wait_send()

    def outward(self, j, s):
        z = self.p.ahead(j)
        return remote(
            self.at(z), self.parts.at[s], self.send.at[j - 1], self.recv.at[j - 1], self.p.to_z(z)
        )

    def stay(self, home):
        return pltpu.make_async_copy(
            self.at(self.p.z), self.parts.at[home], self.send.at[self.p.groups - 1]
        )

    def out_start(self):
        p = self.p

        @pl.when(self.is_home)
        def _():
            home = self.clip(self.home)
            for j in range(1, p.groups):
                self.outward(j, home).start()
            self.stay(home).start()

    def out_finish(self):
        p = self.p
        for j in range(1, p.groups):
            s = p.behind(j) - p.c

            @pl.when((s >= 0) & (s < self.strips))
            def _():
                self.outward(j, self.clip(s)).wait_recv()

        @pl.when(self.is_home)
        def _():
            for j in range(1, p.groups):
                self.outward(j, self.clip(self.home)).wait_send()
            self.stay(self.clip(self.home)).wait()


class Scatter:
    def __init__(self, place, index, part, bufs, out, send, recv):
        self.p, self.i, self.part = place, index, part
        self.core, self.r1, self.r2, self.q1, self.q2, self.zs, self.zr = bufs
        self.out, self.send, self.recv = out, send, recv
        self.k, self.u, self.n = self.q1.shape[0], self.core.shape[3], self.q1.shape[2]
        self.r = self.u // place.groups
        self.first, self.second = pl.ds(0, self.u // 2), pl.ds(self.u // 2, self.u // 2)

    def wire(self, k):
        p, i = self.p, self.i
        if k == 0:
            src, dst, to = self.part.at[:, :, :, 1 - p.c], self.core, p.to_c
        elif k == 1:
            src, dst, to = self.core.at[:, :, 1 - p.x, self.first], self.r1, p.to_x
        elif k == 2:
            src, dst, to = self.core.at[:, 1 - p.y, :, self.second], self.r2, p.to_y
        elif k == 3:
            src, dst, to = self.r1.at[:, 1 - p.y], self.q1, p.to_y
        elif k == 4:
            src, dst, to = self.r2.at[:, 1 - p.x], self.q2, p.to_x
        elif k < 8:
            z = (p.z + k - 4) % 4
            src, dst, to = self.zs.at[:, z], self.zr.at[k - 5], p.to_z(z)
        else:
            z = 1 + p.z // 3
            src, dst, to = self.zs.at[:, 3 - p.z], self.zr.at[3], p.to_z(z)
        return remote(src, dst, self.send.at[i, k], self.recv.at[i, k], to)

    def start(self):
        self.wire(0).start()

    def core_add(self):
        p = self.p
        self.wire(0).wait_recv()
        for k in range(self.k):
            for y in range(2):
                for x in range(2):
                    here = self.core.at[k, y, x]
                    here[...] = here[...] + self.part[k, y, x, p.c]
        self.wire(1).start()
        self.wire(2).start()

    def pass_x(self):
        p = self.p
        self.wire(1).wait_recv()
        for k in range(self.k):
            here = self.r1.at[k, 1 - p.y]
            here[...] = here[...] + self.core[k, 1 - p.y, p.x, self.first, :]
        self.wire(3).start()

    def pass_y(self):
        p = self.p
        self.wire(2).wait_recv()
        for k in range(self.k):
            here = self.r2.at[k, 1 - p.x]
            here[...] = here[...] + self.core[k, p.y, 1 - p.x, self.second, :]
        self.wire(4).start()

    def z_start(self):
        p, r = self.p, self.r
        half = self.u // 2
        self.wire(3).wait_recv()
        self.wire(4).wait_recv()
        per = p.groups // 2
        for k in range(self.k):
            for h in range(2):
                mine = self.r1.at[k, p.y] if h == 0 else self.r2.at[k, p.x]
                got = self.q1.at[k] if h == 0 else self.q2.at[k]
                value = self.core[k, p.y, p.x, pl.ds(h * half, half), :].astype(f32)
                value += mine[...].astype(f32) + got[...].astype(f32)
                slabs = value.reshape(per, r, self.n)
                self.zs[k, pl.ds(h * per, per)] = slabs.astype(bf16)
        pl.when(p.z < 3)(lambda: self.wire(5).start())
        pl.when(p.z > 0)(lambda: self.wire(7).start())

        @pl.when(jnp.logical_not(p.inner))
        def _():
            self.wire(6).start()
            self.wire(8).start()

    def z_pass(self):
        @pl.when(self.p.inner)
        def _():
            self.wire(8).wait_recv()
            z = (self.p.z + 2) % 4
            for k in range(self.k):
                self.zs[k, z] = self.zs[k, z] + self.zr[3, k]
            self.wire(6).start()

    def finish(self):
        p = self.p
        self.wire(6).wait_recv()
        for k in range(self.k):
            self.out[k][...] = self.zs[k, p.z].astype(f32) + self.zr[1, k].astype(f32)

        def more(wire, slot):
            self.wire(wire).wait_recv()
            for k in range(self.k):
                self.out[k][...] += self.zr[slot, k].astype(f32)

        pl.when(p.z > 0)(lambda: more(5, 0))
        pl.when(p.z < 3)(lambda: more(7, 2))

    def drain(self):
        p = self.p
        for k in (0, 1, 2, 3, 4, 6):
            self.wire(k).wait_send()
        pl.when(p.z < 3)(lambda: self.wire(5).wait_send())
        pl.when(p.z > 0)(lambda: self.wire(7).wait_send())
        pl.when(jnp.logical_not(p.inner))(lambda: self.wire(8).wait_send())


class Tally:
    def __init__(self, place, value, got, send, recv):
        self.p, self.value, self.got, self.send, self.recv = place, value, got, send, recv

    def copy(self, k):
        p = self.p
        to = (p.to_c, p.to_x, p.to_y)[k] if k < 3 else p.to_z(p.ahead(k - 2))
        return remote(
            self.value.at[min(k, 3)], self.got.at[k], self.send.at[k], self.recv.at[k], to
        )

    def start(self):
        self.copy(0).start()

    def step(self, k):
        self.copy(k).wait_recv()
        self.value[k + 1] = self.value[k] + self.got[k]
        if k < 2:
            self.copy(k + 1).start()
        else:
            for j in range(1, self.p.groups):
                self.copy(2 + j).start()

    def finish(self):
        value = self.value[3]
        for j in range(1, self.p.groups):
            self.copy(2 + j).wait_recv()
            value += self.got[2 + j]
        for k in range(2 + self.p.groups):
            self.copy(k).wait_send()
        return value


def normalize(v):
    mean = jnp.mean(v, axis=1, keepdims=True)
    centred = v - mean
    inv = lax.rsqrt(jnp.mean(centred * centred, axis=1, keepdims=True) + epsilon)
    return centred * inv, mean, inv


def norm_backward(grad, hat, inv, gain):
    t = grad * gain
    mean_t = jnp.mean(t, axis=1, keepdims=True)
    mean_th = jnp.mean(t * hat, axis=1, keepdims=True)
    return inv * (t - mean_t - hat * mean_th)


class Layer:
    def __init__(self, place, refs):
        self.__dict__.update(refs)
        self.p = place
        self.rows, self.d = self.x.shape
        self.hidden = self.act.shape[1]
        self.step = 96

    def vec(self, i):
        return self.vecs[i : i + 1, :]

    def weight(self, i, cols=slice(None)):
        value = self.w[i, :, :, :, :, cols]
        return value.reshape(self.d, value.shape[-1])

    def eighths(self, value):
        return value.reshape(2, 2, 2, value.shape[0] // 8, value.shape[1])

    def vectors(self):
        d, groups = self.d, self.p.groups
        per = d // (8 * groups)
        wide = self.hidden // (8 * groups)

        def spread(lanes, cols, width):
            lane = lax.broadcasted_iota(jnp.int32, (lanes, cols), 0)
            col = lax.broadcasted_iota(jnp.int32, (lanes, cols), 1)
            hit = (col == lane // 128 * width + lane % 128) & (lane % 128 < width)
            return jnp.where(hit, 1.0, 0.0).astype(bf16)

        half = spread(4 * groups * 128, d // 2, per)
        for h in range(2):
            slabs = [self.small[4 * h + b, z] for b in range(4) for z in range(groups)]
            self.vecs[:, h * (d // 2) : (h + 1) * (d // 2)] = nn(jnp.concatenate(slabs, 1), half)
        one = spread(groups * 128, groups * wide, wide)
        for b in range(8):
            slabs = [self.small[b, z] for z in range(groups)]
            row = nn(jnp.concatenate(slabs, 1), one)[10:11, :]
            self.b_up[:, b * groups * wide : (b + 1) * groups * wide] = row

    def mask(self, lengths, script_ids, key_mask):
        strips, length = key_mask.shape
        home = jnp.clip(self.p.z - self.p.c, 0, strips - 1)
        keys = jnp.zeros((1, length), jnp.int32)
        for s in range(strips):
            keys = jnp.where(home == s, key_mask[s : s + 1, :], keys)
        pos = lax.broadcasted_iota(jnp.int32, (1, length), 1)
        good = (pos == 0) | ((pos < lengths[home]) & (keys == 1))
        good = jnp.broadcast_to(jnp.where(good, 1.0, 0.0), (8, length)).astype(bf16)
        real = length // self.p.groups
        padded = self.rows // self.p.groups
        row = lax.broadcasted_iota(jnp.int32, (self.rows, length), 0)
        col = lax.broadcasted_iota(jnp.int32, (self.rows, length), 1)
        hit = (col == row // padded * real + row % padded) & (row % padded < real)
        self.valid[...] = nt(jnp.where(hit, 1.0, 0.0).astype(bf16), good)[:, 0:1]
        self.sid = script_ids[home]

    def norm1(self):
        self.emb[...] = jnp.where(self.sid == 1, self.vec(T1), self.vec(T0))

        def body(i):
            at = ds(i * self.step, self.step)
            hat, mean, inv = normalize(self.x[at, :].astype(f32) + self.emb[...])
            self.stats[at, 0:1] = mean
            self.stats[at, 1:2] = inv
            self.h1[at, :] = (hat * self.vec(G1) + self.vec(B1)).astype(bf16)

        loop(self.rows // self.step, body)

    def project(self, i, n=768):
        d = self.d

        def body(k):
            at = ds(k * n, n, 128)
            value = nn(self.h1[...], self.weight(QKV + i, at))
            if i != 1:
                value = value + self.vecs[QB if i == 0 else VB : (QB if i == 0 else VB) + 1, at]
            self.qkv[:, ds(i * d + k * n, n, 128)] = value.astype(bf16)

        loop(d // n, body)

    def half(self, h, value):
        lane = lax.broadcasted_iota(jnp.int32, value.shape, 1)
        return jnp.where(lane // DH == h, value, jnp.zeros_like(value))

    def pick(self, a, b):
        lane = lax.broadcasted_iota(jnp.int32, a.shape, 1)
        return jnp.where(lane < DH, a, b)

    def lanes(self, p):
        return [ds(i * self.d + p * 128, 128, 128) for i in range(3)]

    def probs_out(self, p):
        slot = p % 2
        return pltpu.make_async_copy(self.probs.at[slot], self.kept.at[p], self.out_sem.at[slot])

    def probs_in(self, p):
        slot = p % 2
        return pltpu.make_async_copy(self.kept.at[p], self.probs.at[slot], self.in_sem.at[slot])

    def attend(self, p):
        aq, ak, av = self.lanes(p)
        q = self.qkv[:, aq] * jnp.asarray(DH**-0.5, bf16)
        k, v = self.qkv[:, ak], self.qkv[:, av]
        valid = self.valid[...] > 0
        turned = v.T

        @pl.when(p >= 2)
        def _():
            self.probs_out(p - 2).wait()

        contexts = []
        for h in range(2):
            s = nt(k, self.half(h, q))
            s = jnp.where(valid, s, -1e9)
            e = jnp.exp(s - jnp.max(s, axis=0, keepdims=True))
            probs = (e * (1.0 / total(e))).astype(bf16)
            self.probs[p % 2, h] = probs
            contexts.append(nn(turned[h * DH : (h + 1) * DH], probs))
        self.ctx[:, ds(p * 128, 128, 128)] = jnp.concatenate(contexts, axis=0).T.astype(bf16)
        self.probs_out(p).start()

    def mid_norm(self, n=768):
        def body(k):
            at = ds(k * n, n, 128)
            self.mid[:, at] = nn(self.ctx[...], self.weight(OUT, at))

        loop(self.d // n, body)

        def norm(i):
            at = ds(i * self.step, self.step)
            v = self.x[at, :].astype(f32) + self.emb[...] + (self.mid[at, :] + self.vec(OB))
            self.mid[at, :] = v
            hat, mean, inv = normalize(v)
            self.stats[at, 2:3] = mean
            self.stats[at, 3:4] = inv
            self.h2[at, :] = (hat * self.vec(G2) + self.vec(B2)).astype(bf16)

        loop(self.rows // self.step, norm)

    def mlp_up(self, j, n=768):
        def body(k):
            at = ds(j * self.d + k * n, n, 128)
            pre = nn(self.h2[...], self.weight(UP + j, ds(k * n, n, 128))) + self.b_up[:, at]
            cum = 0.5 * (1.0 + lax.erf(pre * 2.0**-0.5))
            den = jnp.exp(-0.5 * pre * pre) * (2.0 * jnp.pi) ** -0.5
            self.act[:, at] = (pre * cum).astype(bf16)
            self.slope[:, at] = (cum + pre * den).astype(bf16)

        loop(self.d // n, body)

    def dw_down(self, b):
        u = self.hidden // 4
        grad = tn(self.act[:, ds(b * u, u, 128)], self.cot[...])
        self.p_down[0, b // 2, b % 2] = grad.reshape(2, u // 2, self.d).astype(bf16)

    def grad_pre(self, b):
        u = self.hidden // 4
        at = ds(b * u, u, 128)
        w = self.w_down[b // 2, b % 2].reshape(u, self.d)
        g = (nt(self.cot[...], w) * self.slope[:, at].astype(f32)).astype(bf16)
        self.slope[:, at] = g
        self.up_sums[:, at] = total(g.astype(f32))

    def mlp_down(self):
        m = self.rows // 2

        def body(i):
            at = ds(i * m, m)
            value = self.mid[at, :] + self.vec(DB)
            for k in range(self.hidden // self.d):
                w = self.w_down[k // 2, k % 2].reshape(self.d, self.d)
                value = value + nn(self.act[at, pl.ds(k * self.d, self.d)], w)
            self.out[at, :] = value.astype(bf16)

        loop(2, body)

    def grad_h2(self, j):
        m = self.rows // 2

        def body(i):
            at = ds(i * m, m)
            value = nt(self.slope[at, ds(j * self.d, self.d, 128)], self.weight(UP + j))
            if j == 0:
                self.wide[at, :] = value
            else:
                self.wide[at, :] += value

        loop(2, body)

    def dw_up(self, j, n=768):
        def body(k):
            grad = tn(self.h2[...], self.slope[:, ds(j * self.d + k * n, n, 128)])
            self.w[UP + j, :, :, :, :, ds(k * n, n, 128)] = self.eighths(grad).astype(bf16)

        loop(self.d // n, body)

    def back2(self):
        zero = jnp.zeros((1, self.d), f32)

        def body(i, sums):
            at = ds(i * self.step, self.step)
            inv = self.stats[at, 3:4]
            hat = (self.mid[at, :] - self.stats[at, 2:3]) * inv
            g = self.wide[at, :]
            cot = self.cot[at, :].astype(f32)
            value = cot + norm_backward(g, hat, inv, self.vec(G2))
            self.mid[at, :] = value
            low = value.astype(bf16)
            self.gb[at, :] = low
            terms = (g * hat, g, cot, low.astype(f32))
            return tuple(s + total(t) for s, t in zip(sums, terms))

        sums = lax.fori_loop(0, self.rows // self.step, body, (zero,) * 4)
        for row, s in zip((G2, B2, DB, OB), sums):
            self.sums[row : row + 1, :] = s

    def grad_ctx(self):
        m = self.rows // 2

        def body(i):
            at = ds(i * m, m)
            self.gctx[at, :] = nt(self.gb[at, :], self.weight(OUT)).astype(bf16)

        loop(2, body)

    def dw_out(self, n=768):
        def body(k):
            at = ds(k * n, n, 128)
            grad = tn(self.ctx[...], self.gb[:, at])
            self.w[OUT, :, :, :, :, at] = self.eighths(grad).astype(bf16)

        loop(self.d // n, body)

    def attend_back(self, p, last):
        aq, ak, av = self.lanes(p)
        q, k, v = self.qkv[:, aq], self.qkv[:, ak], self.qkv[:, av]
        g = self.gctx[:, aq]

        @pl.when(p + 1 < last)
        def _():
            self.probs_in(p + 1).start()

        self.probs_in(p).wait()
        turned = k.T
        dq, dk, dv = [], [], []
        for h in range(2):
            probs = self.probs[p % 2, h]
            dv.append(nn(probs, g))
            grad = nt(v, self.half(h, g))
            wide = probs.astype(f32)
            grad = (wide * (grad - total(wide * grad))).astype(bf16)
            dk.append(nn(grad, q))
            dq.append(nn(turned[h * DH : (h + 1) * DH], grad))
        dq = (jnp.concatenate(dq, axis=0).T * DH**-0.5).astype(bf16)
        dv = self.pick(*dv).astype(bf16)
        self.qkv[:, aq] = dq
        self.qkv[:, ak] = (self.pick(*dk) * DH**-0.5).astype(bf16)
        self.qkv[:, av] = dv
        self.sums[QB : QB + 1, aq] = total(dq.astype(f32))
        self.sums[VB : VB + 1, aq] = total(dv.astype(f32))

    def grad_h1(self, g, n=256):
        m = self.rows // 2

        def body(i):
            at = ds(i * m, m)
            value = None
            for k in range(3):
                w = self.weight(QKV + k, pl.ds(g * n, n))
                term = nt(self.qkv[at, pl.ds(k * self.d + g * n, n)], w)
                value = term if value is None else value + term
            if g == 0:
                self.wide[at, :] = value
            else:
                self.wide[at, :] += value

        loop(2, body)

    def dw_qkv(self, g, n=256):
        for k in range(3):
            grad = tn(self.h1[...], self.qkv[:, pl.ds(k * self.d + g * n, n)])
            self.w[QKV + k, :, :, :, :, pl.ds(g * n, n)] = self.eighths(grad).astype(bf16)

    def back1(self):
        zero = jnp.zeros((1, self.d), f32)

        def body(i, sums):
            at = ds(i * self.step, self.step)
            inv = self.stats[at, 1:2]
            hat = (self.x[at, :].astype(f32) + self.emb[...] - self.stats[at, 0:1]) * inv
            g = self.wide[at, :]
            value = self.mid[at, :] + norm_backward(g, hat, inv, self.vec(G1))
            self.gx[at, :] = value.astype(bf16)
            return tuple(s + total(t) for s, t in zip(sums, (g * hat, g, value)))

        sums = lax.fori_loop(0, self.rows // self.step, body, (zero,) * 3)
        self.sums[G1 : G1 + 1, :] = sums[0]
        self.sums[B1 : B1 + 1, :] = sums[1]
        self.sums[T0 : T0 + 1, :] = jnp.where(self.sid == 1, 0.0, sums[2])
        self.sums[T1 : T1 + 1, :] = jnp.where(self.sid == 1, sums[2], 0.0)


def pack(r):
    slab = r["s_small"]
    rows = [r[f"vec{i}"][...].astype(f32) for i in range(10)]
    rows = [jnp.pad(v, ((0, 0), (0, 128 - v.shape[1]))) for v in rows]
    slab[...] = jnp.concatenate(rows + [jnp.zeros((5, 128), f32)], axis=0).astype(bf16)


def kernel(outer, groups, names, *refs):
    r = dict(zip(names, refs, strict=True))
    p = Place(outer, groups)
    L = Layer(p, r)
    d, hidden = L.d, L.hidden
    nh = hidden // d
    real = r["patches"].shape[1]
    strips = r["patches"].shape[0]
    per = d // (8 * groups)
    u = d // 8
    n_down = d // 256
    w, w_down, stage = r["w"], r["w_down"], r["stage"]

    gs = []

    def add(shard, block, part, land, settle=None):
        gs.append(
            Gather(
                p, len(gs), shard, block, part, land, r["g_send"], r["g_recv"], r["g_here"], settle
            )
        )

    add(
        r["s_small"],
        lambda y, x, c: r["small"].at[y * 4 + x * 2 + c],
        lambda ref, h: ref.at[pl.ds(h * (groups // 2), groups // 2)],
        lambda z: r["small"].at[p.y * 4 + p.x * 2 + p.c, z],
    )

    def add_square(i, shard):
        def settle(block):
            block[...] = stage[i].astype(f32).reshape(u, d).astype(bf16)

        add(
            shard,
            lambda y, x, c: w.at[i, y, x, c],
            lambda ref, h: ref.at[pl.ds(h * (u // 2), u // 2)],
            lambda z: stage.at[i, z],
            settle,
        )

    for i in range(3):
        add_square(QKV + i, r["s_qkv"].at[:, pl.ds(i * d, d)])
    add_square(OUT, r["s_out"])
    for i in range(nh):
        add_square(UP + i, r["s_up"].at[:, pl.ds(i * d, d)])
    hu = hidden // 8
    hr = hu // groups
    for i in range(n_down):
        cols = pl.ds(i * 256, 256)
        add(
            r["s_down"].at[:, cols],
            lambda y, x, c, cols=cols: w_down.at[y, x, c, :, cols],
            lambda ref, h: ref.at[pl.ds(h * (hu // 2), hu // 2)],
            lambda z, cols=cols: w_down.at[p.y, p.x, p.c, ds(z * hr, hr), cols],
        )
    xs = Rows(p, r["xp"], r["x"], r["x_send"], r["x_recv"])
    cs = Rows(p, r["cp"], r["cot"], r["c_send"], r["c_recv"])

    ss = []

    def give(part, bufs, out):
        ss.append(Scatter(p, len(ss), part, bufs, out, r["s_send"], r["s_recv"]))

    def bufs(kind, i):
        found = [r[f"{kind}_{name}"].at[i] for name in ("core", "r1", "r2", "q1", "q2")]
        if kind == "flat":
            slot = stage.at[pl.ds(UP + i if i < nh else OUT, 1)]
        elif kind == "head":
            slot = stage.at[pl.ds(QKV, 3), :, :, pl.ds(i * 256, 256)]
        else:
            slot = r["tall_zs"].at[i]
        return found + [slot, r[f"{kind}_zr"].at[i]]

    for i in range(n_down):
        cols = pl.ds(i * 256, 256)
        give(r["p_down"].at[:, :, :, :, :, cols], bufs("tall", i), [r["o_down"].at[:, cols]])
    for i in range(nh):
        give(w.at[pl.ds(UP + i, 1)], bufs("flat", i), [r["o_up"].at[:, pl.ds(i * d, d)]])
    give(w.at[pl.ds(OUT, 1)], bufs("flat", nh), [r["o_out"]])
    for g in range(d // 256):
        cols = pl.ds(g * 256, 256)
        outs = [r["o_qkv"].at[:, pl.ds(k * d + g * 256, 256)] for k in range(3)]
        give(w.at[pl.ds(QKV, 3), :, :, :, :, cols], bufs("head", g), outs)

    ys = Rows(p, r["o_out_rows"], r["out"], r["y_send"], r["y_recv"])
    rs = Rows(p, r["o_grad_rows"], L.gx, r["d_send"], r["d_recv"])
    ts = Tally(p, r["value"], r["got"], r["t_send"], r["t_recv"])

    ends = {X_IN: xs, C_IN: cs, Y_OUT: ys, R_OUT: rs}
    gather = {SMALL: 0, WQ: 1, WK: 2, WV: 3, WO: 4, WU: 5, WD: 5 + nh}
    scatter = {GD: 0, GU: n_down, GO: n_down + nh, GQ: n_down + nh + 1}
    pairs = d // 128

    fetch = [
        pltpu.make_async_copy(r[a], r["pin"], r["arg_sem"].at[i])
        for i, a in enumerate(("patches", "cotangent"))
    ]
    fetch[0].start()

    def lay(dst):
        dst[...] = jnp.zeros_like(dst)
        for s in range(strips):
            dst[s, :real] = r["pin"][s]

    def prepare():
        fetch[0].wait()
        lay(r["xp"])
        fetch[1].start()
        xs.in_local()

    def mask():
        L.mask(r["lengths"], r["script_ids"], r["key_mask"])
        fetch[1].wait()
        lay(r["cp"])
        cs.in_local()

    def sent():
        for g in gs:
            g.sent()
        cs.in_sent()

    def context_end():
        for i in (pairs - 2, pairs - 1):
            L.probs_out(i).wait()
        L.mid_norm()

    def rows_done():
        L.back1()
        r["sums"][10:16, :] = jnp.concatenate(
            [L.up_sums[:, j * d : (j + 1) * d] for j in range(nh)]
            + [jnp.zeros((6 - nh, d), f32)]
        )
        r["value"][0] = r["sums"][...]
        ts.start()

    def context_grad():
        L.grad_ctx()
        L.probs_in(0).start()

    once = {
        PREP: prepare, MASK: mask,
        VEC: L.vectors, NORM1: L.norm1, MID: context_end, DOWN: L.mlp_down, BACK2: L.back2,
        GCTX: context_grad, DWOUT: L.dw_out, BACK1: rows_done, SENT: sent,
        SENTX: xs.in_sent,
    }
    counted = {
        PROJ: L.project, UP_: L.mlp_up, GU_: L.grad_h2, DWUP: L.dw_up, GQ_: L.grad_h1,
        DWQKV: L.dw_qkv, T: ts.step,
    }
    looped = {
        ATT: L.attend, DWDOWN: L.dw_down, GPRE: L.grad_pre,
        ATTB: lambda i: L.attend_back(i, pairs),
    }

    def act(step):
        kind, name, i = step
        if kind == ROW:
            ends[name].in_start(i)
        elif kind == IN:
            ends[name].in_finish()
        elif kind == OUT_:
            ends[name].out_start()
        elif name in gather:
            g = gs[gather[name] + i]
            {
                ZS: g.z_start, ZF: g.z_far, ZE: g.z_end, FIN: g.finish,
                MX: lambda: g.pass_on(3, 6, 8), MY: lambda: g.pass_on(4, 5, 9),
                DX: lambda: g.pass_on(6, None, 10), DY: lambda: g.pass_on(5, None, 11),
            }[kind]()
        else:
            s = ss[scatter[name] + i]
            {
                ST: s.start, CA: s.core_add, PX: s.pass_x, PY: s.pass_y, ZT: s.z_start,
                ZP: s.z_pass, FI: s.finish,
            }[kind]()

    pack(r)
    p.greet()
    steps = list(SCHEDULE)
    while steps:
        kind, name, first = steps.pop(0)
        if name:
            act((kind, name, first))
        elif kind in once:
            once[kind]()
        elif kind in counted:
            counted[kind](first)
        else:
            n, between = 1, {}
            while True:
                k = 0
                while k < len(steps) and steps[k][1]:
                    k += 1
                if k == len(steps) or steps[k] != (kind, 0, first + n):
                    break
                between[n - 1] = steps[:k]
                steps = steps[k + 1 :]
                n += 1

            def body(i):
                looped[kind](first + i)
                for at, some in between.items():
                    if some:

                        @pl.when(i == at)
                        def _():
                            for step in some:
                                act(step)

            if n == 1:
                body(0)
            else:
                loop(n, body)

    ys.out_finish()
    r["o_tally"][...] = ts.finish()
    rs.out_finish()
    for s in ss:
        s.drain()


def on_device(outer, groups, *args):
    (patches, cotangent, lengths, script_ids, key_mask, norm1_gain, norm1_bias, w_qkv, q_bias,
     v_bias, w_attn_out, attn_out_bias, norm2_gain, norm2_bias, w_up, up_bias, w_down, down_bias,
     script_table) = args
    strips, part_rows, d = patches.shape
    hidden = w_up.shape[1]
    parts = 8 * groups
    pad_rows = round_up(part_rows, 16)
    rows = groups * pad_rows
    vectors = [norm1_gain, norm1_bias, q_bias, v_bias, attn_out_bias, norm2_gain, norm2_bias,
               down_bias]
    weights = [w_qkv, w_attn_out, w_up, w_down]
    if outer > 1:
        mates = [[g * outer + i for i in range(outer)] for g in range(8)]
        seq = lax.axis_index("seq")

        def widen(a):
            a = lax.all_gather(a, ("seq",), axis=0, tiled=True)
            a = lax.all_gather(a, "dp", axis=0, tiled=True, axis_index_groups=mates)
            n = a.shape[0] // groups
            return lax.dynamic_slice_in_dim(a, seq * n, n, axis=0)

        vectors = [widen(a) for a in vectors]
        script_table = widen(script_table.T).T
        up_bias = widen(up_bias)
        weights = [widen(a) for a in weights]
    vectors = [v[None] for v in vectors] + [script_table, up_bias[None]]
    vm = pl.BlockSpec(memory_space=pltpu.VMEM)
    sm = pl.BlockSpec(memory_space=pltpu.SMEM)
    anywhere = pl.BlockSpec(memory_space=pl.ANY)
    sems = pltpu.SemaphoreType.DMA
    nh = hidden // d
    u, r, nd, ng = d // 8, d // parts, d // 256, d // 256
    ins = [f"vec{i}" for i in range(10)] + ["s_qkv", "s_out", "s_up", "s_down", "patches", "cotangent", "key_mask",
           "lengths", "script_ids"]
    outs = {
        "o_qkv": ((r, 3 * d), f32),
        "o_out": ((r, d), f32),
        "o_up": ((r, hidden), f32),
        "o_down": ((hidden // parts, d), f32),
        "o_tally": ((16, d), f32),
        "o_out_rows": ((strips, pad_rows, d), bf16),
        "o_grad_rows": ((strips, pad_rows, d), bf16),
        "kept": ((d // 128, 2, rows, rows), bf16),
    }
    scratch = {
        "small": ((8, groups, 16, 128), bf16),
        "s_small": ((16, 128), bf16),
        "stage": ((4 + nh, groups, r, d), bf16),
        "w": ((4 + nh, 2, 2, 2, u, d), bf16),
        "w_down": ((2, 2, 2, hidden // 8, d), bf16),
        "p_down": ((1, 2, 2, 2, hidden // 8, d), bf16),
        "pin": (patches.shape, bf16),
        "xp": ((strips, pad_rows, d), bf16),
        "cp": ((strips, pad_rows, d), bf16),
        "x": ((rows, d), bf16),
        "cot": ((rows, d), bf16),
        "valid": ((rows, 1), f32),
        "vecs": ((16, d), f32),
        "b_up": ((1, hidden), f32),
        "up_sums": ((1, hidden), f32),
        "sums": ((16, d), f32),
        "emb": ((1, d), f32),
        "stats": ((rows, 4), f32),
        "h1": ((rows, d), bf16),
        "qkv": ((rows, 3 * d), bf16),
        "probs": ((2, 2, rows, rows), bf16),
        "ctx": ((rows, d), bf16),
        "mid": ((rows, d), f32),
        "wide": ((rows, d), f32),
        "h2": ((rows, d), bf16),
        "act": ((rows, hidden), bf16),
        "slope": ((rows, hidden), bf16),
        "value": ((4, 16, d), f32),
        "got": ((2 + groups, 16, d), f32),
    }
    for kind, count, k, uu, n in (
        ("tall", nd, 1, hidden // 8, 256),
        ("flat", nh + 1, 1, u, d),
        ("head", ng, 3, u, 256),
    ):
        rr = uu // groups
        scratch[f"{kind}_core"] = ((count, k, 2, 2, uu, n), bf16)
        scratch[f"{kind}_r1"] = ((count, k, 2, uu // 2, n), bf16)
        scratch[f"{kind}_r2"] = ((count, k, 2, uu // 2, n), bf16)
        scratch[f"{kind}_q1"] = ((count, k, uu // 2, n), bf16)
        scratch[f"{kind}_q2"] = ((count, k, uu // 2, n), bf16)
        if kind == "tall":
            scratch["tall_zs"] = ((count, k, groups, rr, n), bf16)
        scratch[f"{kind}_zr"] = ((count, groups, k, rr, n), bf16)
    n_gather = 5 + nh + nd
    n_scatter = nd + nh + 1 + ng
    semaphores = {
        "g_send": (n_gather, WIRE), "g_recv": (n_gather, WIRE),
        "s_send": (n_scatter, HOPS), "s_recv": (n_scatter, HOPS),
        "t_send": (2 + groups,), "t_recv": (2 + groups,),
        "out_sem": (2,), "in_sem": (2,), "g_here": (n_gather,), "arg_sem": (2,),
    }
    for name in "xcyd":
        shape = (groups,) if name in "yd" else (d // 256, groups - 1)
        semaphores[f"{name}_send"] = shape
        semaphores[f"{name}_recv"] = shape
    names = ins + list(outs) + list(scratch) + list(semaphores)

    def body(*refs):
        refs = dict(zip(names, refs, strict=True))
        act = refs["act"]
        for k, name in enumerate(("out", "gb", "gctx", "gx")):
            refs[name] = act.at[:, pl.ds(k * d, d)]
        kernel(outer, groups, list(refs), *refs.values())

    res = pl.pallas_call(
        body,
        out_shape=[jax.ShapeDtypeStruct(*s) for s in outs.values()],
        in_specs=[vm] * 10 + [anywhere] * 6 + [vm] + [sm] * 2,
        out_specs=[vm] * 5 + [anywhere] * 3,
        scratch_shapes=[pltpu.VMEM(*s) for s in scratch.values()]
        + [sems(s) for s in semaphores.values()],
        compiler_params=pltpu.CompilerParams(
            collective_id=0, has_side_effects=True, vmem_limit_bytes=63 * 2**20
        ),
    )(*vectors, *weights, patches, cotangent, key_mask, lengths, script_ids)
    shards = list(res[:4])
    tally = res[4]
    if outer > 1:

        def narrow(a):
            a = lax.psum(a, "dp", axis_index_groups=mates)
            a = lax.all_gather(a, ("seq",), axis=0, tiled=True)
            at = (lax.axis_index("dp") % outer) * groups + lax.axis_index("seq")
            n = a.shape[0] // groups // outer
            return lax.dynamic_slice_in_dim(a, at * n, n, axis=0)

        shards = [narrow(a) for a in shards]
        tally = lax.psum(tally, "dp", axis_index_groups=mates)
    n = d // (parts * outer)
    m = hidden // (parts * outer)
    passed = [res[5], res[6]] + (shards if outer == 1 else [])
    shapes = [patches.shape] * 2 + [a.shape for a in passed[2:]]
    closed = pl.pallas_call(
        functools.partial(close, groups, nh),
        out_shape=[jax.ShapeDtypeStruct((1, n), f32)] * 8
        + [jax.ShapeDtypeStruct((2, n), f32), jax.ShapeDtypeStruct((1, m), f32)]
        + [jax.ShapeDtypeStruct(n, a.dtype) for n, a in zip(shapes, passed, strict=True)],
        in_specs=[vm] * (1 + len(passed)),
        out_specs=[vm] * (10 + len(passed)),
    )(tally, *passed)
    vec = [v.reshape(n) for v in closed[:8]]
    table, vup = closed[8], closed[9].reshape(m)
    if outer == 1:
        shards = closed[12:]
    return (
        closed[10], closed[11], vec[G1], vec[B1], shards[0], vec[QB], vec[VB], shards[1], vec[OB],
        vec[G2], vec[B2], shards[2], vup, shards[3], vec[DB], table,
    )


def close(groups, nh, tally, *refs):
    n_passed = (len(refs) - 10) // 2
    passed, outs = refs[:n_passed], refs[n_passed:]
    for src, dst in zip(passed, outs[10:], strict=True):
        if len(src.shape) == 3:
            for s in range(src.shape[0]):
                dst[s] = src[s, : dst.shape[1]]
        else:
            dst[...] = src[...]
    me = lax.axis_index("dp") * groups + lax.axis_index("seq")
    d = tally.shape[1]
    n, m = outs[0].shape[1], outs[9].shape[1]
    mine = pltpu.roll(tally[...], lax.rem(d - me * n, d), 1)
    for i in range(8):
        outs[i][...] = mine[i : i + 1, :n]
    outs[8][...] = mine[T0 : T1 + 1, :n]
    row = jnp.zeros((8, d), f32)
    for i in range(nh):
        line = jnp.broadcast_to(tally[10 + i : 11 + i, :], (8, d))
        row = jnp.where(me * m // d == i, line, row)
    outs[9][...] = pltpu.roll(row, lax.rem(d - lax.rem(me * m, d), d), 1)[0:1, :m]


def solution(mesh):
    dp, seq = mesh.shape["dp"], mesh.shape["seq"]
    both = ("dp", "seq")
    one, two = P(both), P(both, None)
    rows = P("dp", "seq", None)
    return jax.shard_map(
        functools.partial(on_device, dp // 8, seq),
        mesh=mesh,
        in_specs=(
            rows, rows, P("dp"), P("dp"), P("dp", None), one, one, two, one, one, two, one, one,
            one, two, one, two, one, P(None, both),
        ),
        out_specs=(
            rows, rows, one, one, two, one, one, two, one, one, one, two, one, two, one,
            P(None, both),
        ),
        check_vma=False,
    )
```

```python
import functools

import jax
import jax.numpy as jnp
from jax import lax
from jax.experimental import pallas as pl
from jax.experimental.pallas import tpu as pltpu
from jax.sharding import PartitionSpec as P

DH = 64
MESH = pl.DeviceIdType.MESH
f32 = jnp.float32
bf16 = jnp.bfloat16
epsilon = 1e-06
WIRE = 13
FAR = 12
DIRECT = 2
HOPS = 9
QKV, OUT, UP = 0, 3, 4
G1, B1, QB, VB, OB, G2, B2, DB, T0, T1 = range(10)


def round_up(n, m):
    return (n + m - 1) // m * m


def ds(start, size, align=16):
    return pl.ds(pl.multiple_of(start, align), size)


def nn(a, b):
    return lax.dot_general(a, b, (((1,), (0,)), ((), ())), preferred_element_type=f32)


def nt(a, b):
    return lax.dot_general(a, b, (((1,), (1,)), ((), ())), preferred_element_type=f32)


def tn(a, b):
    return lax.dot_general(a, b, (((0,), (0,)), ((), ())), preferred_element_type=f32)


def loop(n, body):
    def step(i, carry):
        body(i)
        return carry

    lax.fori_loop(0, n, step, 0)


def total(v):
    return jnp.sum(v, axis=0, keepdims=True)


def remote(src, dst, send, recv, to):
    return pltpu.make_async_remote_copy(
        src_ref=src, dst_ref=dst, send_sem=send, recv_sem=recv, device_id=to, device_id_type=MESH
    )


(ZS, ZE, MX, MY, DX, DY, FIN, ST, CA, PX, PY, ZT, FI, ROW, IN, OUT_, ZF, ZP) = range(18)
(SMALL, WQ, WK, WV, WO, WU, WD, GD, GU, GO, GQ, X_IN, C_IN, Y_OUT, R_OUT) = range(1, 16)
(PREP, MASK, VEC, NORM1, PROJ, ATT, MID, UP_, DWDOWN, GPRE, DOWN, GU_, BACK2, GCTX, DWUP, ATTB,
 GQ_, DWQKV, BACK1, DWOUT, SENT, SENTX, T) = range(100, 123)
SCHEDULE = (
    (ZS, SMALL, 0), (ZS, WK, 0), (PREP, 0, 0), (ZS, WV, 0), (MASK, 0, 0), (ZS, WQ, 0),
    (ZE, SMALL, 0), (ZS, WU, 1), (ZF, WK, 0), (ZS, WU, 3), (MX, SMALL, 0), (MY, SMALL, 0),
    (ZF, WV, 0), (ZS, WO, 0), (ZE, WQ, 0), (DX, SMALL, 0), (DY, SMALL, 0), (ROW, X_IN, 0),
    (ZF, WU, 1), (FIN, SMALL, 0), (VEC, 0, 0), (ZE, WK, 0), (ZF, WU, 3), (ZE, WV, 0), (ZS, WU, 0),
    (MX, WQ, 0), (MY, WQ, 0), (ZF, WO, 0), (ROW, X_IN, 1), (MX, WK, 0), (MY, WK, 0), (ZE, WU, 1),
    (ZE, WU, 3), (MX, WV, 0), (MY, WV, 0), (ZS, WU, 2), (ZF, WU, 0), (DX, WQ, 0), (DY, WQ, 0),
    (ZE, WO, 0), (ROW, X_IN, 2), (DX, WK, 0), (DY, WK, 0), (MX, WU, 1), (MY, WU, 1), (ZS, WD, 2),
    (ZF, WU, 2), (ZE, WU, 0), (MX, WU, 3), (MY, WU, 3), (ZS, WD, 1), (DX, WV, 0), (DY, WV, 0),
    (ZS, WD, 0), (IN, X_IN, 0), (NORM1, 0, 0), (MX, WO, 0), (MY, WO, 0), (FIN, WQ, 0),
    (PROJ, 0, 0), (DX, WU, 1), (DY, WU, 1), (ZF, WD, 2), (FIN, WK, 0), (PROJ, 0, 1),
    (ROW, C_IN, 0), (ZE, WU, 2), (FIN, WV, 0), (PROJ, 0, 2), (ATT, 0, 0), (MX, WU, 0),
    (MY, WU, 0), (ZF, WD, 1), (ATT, 0, 1), (ROW, C_IN, 1), (DY, WO, 0), (DX, WO, 0), (DX, WU, 3),
    (DY, WU, 3), (ZF, WD, 0), (ZE, WD, 2), (ATT, 0, 2), (ATT, 0, 3), (MX, WU, 2), (MY, WU, 2),
    (ATT, 0, 4), (SENTX, 0, 0), (ROW, C_IN, 2), (DX, WU, 0), (DY, WU, 0), (ZE, WD, 1),
    (ATT, 0, 5), (FIN, WO, 0), (MID, 0, 0), (DX, WU, 2), (DY, WU, 2), (ZE, WD, 0), (MX, WD, 2),
    (MY, WD, 2), (FIN, WU, 0), (UP_, 0, 0), (FIN, WU, 1), (UP_, 0, 1), (FIN, WU, 2), (UP_, 0, 2),
    (MX, WD, 1), (MY, WD, 1), (FIN, WU, 3), (UP_, 0, 3), (IN, C_IN, 0), (DWDOWN, 0, 0),
    (DWDOWN, 0, 1), (DWDOWN, 0, 2), (MX, WD, 0), (MY, WD, 0), (DWDOWN, 0, 3), (ST, GD, 0),
    (ST, GD, 1), (ST, GD, 2), (DX, WD, 2), (DY, WD, 2), (DX, WD, 1), (DY, WD, 1), (CA, GD, 0),
    (DX, WD, 0), (DY, WD, 0), (CA, GD, 1), (CA, GD, 2), (FIN, WD, 0), (FIN, WD, 1), (FIN, WD, 2),
    (GPRE, 0, 0), (GPRE, 0, 1), (GPRE, 0, 2), (DOWN, 0, 0), (OUT_, Y_OUT, 0), (PX, GD, 0),
    (PY, GD, 0), (GPRE, 0, 3), (PX, GD, 1), (PY, GD, 1), (GU_, 0, 0), (GU_, 0, 1), (GU_, 0, 2),
    (SENT, 0, 0), (DWUP, 0, 2), (ST, GU, 2), (GU_, 0, 3), (PX, GD, 2), (PY, GD, 2), (DWUP, 0, 0),
    (ST, GU, 0), (BACK2, 0, 0), (ZT, GD, 0), (CA, GU, 2), (GCTX, 0, 0), (ZT, GD, 1), (CA, GU, 0),
    (DWUP, 0, 3), (ST, GU, 3), (ATTB, 0, 0), (ZT, GD, 2), (DWUP, 0, 1), (ST, GU, 1), (CA, GU, 3),
    (ATTB, 0, 1), (PX, GU, 2), (PY, GU, 2), (ATTB, 0, 2), (PX, GU, 0), (PY, GU, 0), (CA, GU, 1),
    (GQ_, 0, 0), (ZP, GD, 0), (DWQKV, 0, 0), (ST, GQ, 0), (ZP, GD, 1), (PX, GU, 3), (PY, GU, 3),
    (ATTB, 0, 3), (ZP, GD, 2), (ZT, GU, 2), (ATTB, 0, 4), (FI, GD, 0), (ZT, GU, 0), (CA, GQ, 0),
    (GQ_, 0, 1), (FI, GD, 1), (ATTB, 0, 5), (FI, GD, 2), (PX, GU, 1), (PY, GU, 1), (ZT, GU, 3),
    (GQ_, 0, 2), (ZP, GU, 2), (DWQKV, 0, 2), (ST, GQ, 2), (ZP, GU, 0), (BACK1, 0, 0),
    (OUT_, R_OUT, 0), (PX, GQ, 0), (PY, GQ, 0), (T, 0, 0), (DWOUT, 0, 0), (ST, GO, 0), (ZT, GU, 1),
    (ZP, GU, 3), (CA, GQ, 2), (T, 0, 1), (DWQKV, 0, 1), (ST, GQ, 1), (FI, GU, 0), (FI, GU, 2),
    (CA, GO, 0), (ZT, GQ, 0), (CA, GQ, 1), (T, 0, 2), (PX, GQ, 2), (PY, GQ, 2), (PX, GO, 0),
    (PY, GO, 0), (PX, GQ, 1), (PY, GQ, 1), (ZT, GQ, 2), (ZT, GO, 0), (ZP, GU, 1), (ZT, GQ, 1),
    (FI, GU, 3), (ZP, GQ, 0), (ZP, GQ, 2), (ZP, GO, 0), (FI, GU, 1), (ZP, GQ, 1), (FI, GQ, 0),
    (FI, GQ, 2), (FI, GO, 0), (FI, GQ, 1),
)


class Place:
    def __init__(self, outer, groups):
        self.dp = lax.axis_index("dp")
        self.z = lax.axis_index("seq")
        assert groups == 4
        self.groups = groups
        b = self.dp // outer
        self.c = b % 2
        self.x = (b // 2) % 2
        self.y = b // 4
        self.inner = (self.z == 1) | (self.z == 2)
        self.to_c = (self.dp + outer * (1 - 2 * self.c), self.z)
        self.to_x = (self.dp + outer * (2 - 4 * self.x), self.z)
        self.to_y = (self.dp + outer * (4 - 8 * self.y), self.z)

    def ahead(self, j):
        return (self.z + j) % self.groups

    def behind(self, j):
        return (self.z + self.groups - j) % self.groups

    def to_z(self, z):
        return (self.dp, z)

    def greet(self):
        barrier = pltpu.get_barrier_semaphore()
        peers = [self.to_c, self.to_x, self.to_y]
        peers += [self.to_z(self.ahead(j)) for j in range(1, self.groups)]
        for peer in peers:
            pl.semaphore_signal(barrier, inc=1, device_id=peer, device_id_type=MESH)
        pl.semaphore_wait(barrier, len(peers))


class Gather:
    def __init__(self, place, index, shard, block, part, land, send, recv, here, settle=None):
        self.p, self.i, self.shard = place, index, shard
        self.block, self.part, self.land, self.settle = block, part, land, settle
        self.send, self.recv, self.here = send, recv, here

    def copy(self, k, ref, to):
        return remote(ref, ref, self.send.at[self.i, k], self.recv.at[self.i, k], to)

    def z_wire(self, k):
        p, z = self.p, self.p.z
        if k < 3:
            src, owner, to = self.shard, z, ((z + 1) % 4, (z + 2) % 4, (z + 3) % 4)[k]
        elif self.i < DIRECT:
            src, owner, to = self.shard, z, 3 - z
        else:
            owner = (z + 2) % 4
            src, to = self.land(owner), (z + 1) % 4 * (z // 2)
        return remote(
            src, self.land(owner), self.send.at[self.i, k], self.recv.at[self.i, k], p.to_z(to)
        )

    def own(self):
        return pltpu.make_async_copy(self.shard, self.land(self.p.z), self.here.at[self.i])

    def z_got(self, k):
        z = self.p.z
        owner = ((z + 3) % 4, (z + 2) % 4, (z + 1) % 4)[k] if k < 3 else 3 - z
        ref = self.land(owner)
        remote(
            ref, ref, self.send.at[self.i, k], self.recv.at[self.i, k], self.p.to_z((z + 1) % 4)
        ).wait_recv()

    def z_start(self):
        p = self.p
        pl.when(p.z < 3)(lambda: self.z_wire(0).start())
        self.z_wire(1).start()
        pl.when(p.z > 0)(lambda: self.z_wire(2).start())
        if self.i < DIRECT:
            pl.when(jnp.logical_not(p.inner))(lambda: self.z_wire(FAR).start())
        self.own().start()

    def z_far(self):
        if self.i < DIRECT:
            return

        @pl.when(self.p.inner)
        def _():
            self.z_got(1)
            self.z_wire(FAR).start()

    def xy(self, k):
        p = self.p
        mx, my = 1 - p.x, 1 - p.y
        own = lambda: self.block(p.y, p.x, p.c)
        bx = lambda: self.block(p.y, mx, p.c)
        by = lambda: self.block(my, p.x, p.c)
        bd = lambda: self.block(my, mx, p.c)
        if k == 3:
            return self.copy(3, own(), p.to_x)
        if k == 4:
            return self.copy(4, own(), p.to_y)
        if k == 5:
            return self.copy(5, self.part(by(), 1), p.to_x)
        if k == 6:
            return self.copy(6, self.part(bx(), 0), p.to_y)
        if k == 7:
            return self.copy(7, own(), p.to_c)
        if k == 8:
            return self.copy(8, bx(), p.to_c)
        if k == 9:
            return self.copy(9, by(), p.to_c)
        return self.copy(k, self.part(bd(), k - 10), p.to_c)

    def z_end(self):
        p = self.p
        self.own().wait()
        pl.when(p.z > 0)(lambda: self.z_got(0))
        pl.when(p.z < 3)(lambda: self.z_got(2))

        @pl.when(jnp.logical_not(p.inner))
        def _():
            self.z_got(1)
            self.z_got(FAR)

        if self.i < DIRECT:
            pl.when(p.inner)(lambda: self.z_got(1))
        if self.settle is not None:
            self.settle(self.block(p.y, p.x, p.c))
        for k in (3, 4, 7):
            self.xy(k).start()

    def pass_on(self, came, on, core):
        self.xy(came).wait_recv()
        for k in (on, core):
            if k is not None:
                self.xy(k).start()

    def finish(self):
        for k in (7, 8, 9, 10, 11):
            self.xy(k).wait_recv()

    def sent(self):
        p = self.p
        pl.when(p.z < 3)(lambda: self.z_wire(0).wait_send())
        self.z_wire(1).wait_send()
        pl.when(p.z > 0)(lambda: self.z_wire(2).wait_send())
        far = jnp.logical_not(p.inner) if self.i < DIRECT else p.inner
        pl.when(far)(lambda: self.z_wire(FAR).wait_send())
        for k in range(3, FAR):
            self.xy(k).wait_send()


class Rows:
    def __init__(self, place, parts, strip, send, recv):
        self.p, self.parts, self.strip, self.send, self.recv = place, parts, strip, send, recv
        self.strips, self.rows = parts.shape[0], parts.shape[1]
        self.pieces = parts.shape[2] // 256
        self.home = place.z - place.c
        self.is_home = (self.home >= 0) & (self.home < self.strips)

    def clip(self, s):
        return jnp.clip(s, 0, self.strips - 1)

    def at(self, z):
        return self.strip.at[ds(z * self.rows, self.rows)]

    def inward(self, k, j, owner, s):
        cols = pl.ds(k * 256, 256)
        return remote(
            self.parts.at[s, :, cols], self.strip.at[ds(owner * self.rows, self.rows), cols],
            self.send.at[k, j - 1], self.recv.at[k, j - 1], self.p.to_z(self.p.ahead(j)),
        )

    def in_start(self, k):
        p = self.p
        for j in range(1, p.groups):
            s = p.ahead(j) - p.c

            @pl.when((s >= 0) & (s < self.strips))
            def _():
                self.inward(k, j, p.z, self.clip(s)).start()

    def in_local(self):
        p = self.p

        @pl.when(self.is_home)
        def _():
            self.strip[ds(p.z * self.rows, self.rows), :] = self.parts[self.clip(self.home)]

        @pl.when(jnp.logical_not(self.is_home))
        def _():
            self.strip[...] = jnp.zeros_like(self.strip)

    def in_finish(self):
        p = self.p

        @pl.when(self.is_home)
        def _():
            for k in range(self.pieces):
                for j in range(1, p.groups):
                    self.inward(k, j, p.behind(j), 0).wait_recv()

    def in_sent(self):
        p = self.p
        for j in range(1, p.groups):
            s = p.ahead(j) - p.c

            @pl.when((s >= 0) & (s < self.strips))
            def _():
                for k in range(self.pieces):
                    self.inward(k, j, p.z, self.clip(s)).wait_send()

    def outward(self, j, s):
        z = self.p.ahead(j)
        return remote(
            self.at(z), self.parts.at[s], self.send.at[j - 1], self.recv.at[j - 1], self.p.to_z(z)
        )

    def stay(self, home):
        return pltpu.make_async_copy(
            self.at(self.p.z), self.parts.at[home], self.send.at[self.p.groups - 1]
        )

    def out_start(self):
        p = self.p

        @pl.when(self.is_home)
        def _():
            home = self.clip(self.home)
            for j in range(1, p.groups):
                self.outward(j, home).start()
            self.stay(home).start()

    def out_finish(self):
        p = self.p
        for j in range(1, p.groups):
            s = p.behind(j) - p.c

            @pl.when((s >= 0) & (s < self.strips))
            def _():
                self.outward(j, self.clip(s)).wait_recv()

        @pl.when(self.is_home)
        def _():
            for j in range(1, p.groups):
                self.outward(j, self.clip(self.home)).wait_send()
            self.stay(self.clip(self.home)).wait()


class Scatter:
    def __init__(self, place, index, part, bufs, out, send, recv):
        self.p, self.i, self.part = place, index, part
        self.core, self.r1, self.r2, self.q1, self.q2, self.zs, self.zr = bufs
        self.out, self.send, self.recv = out, send, recv
        self.k, self.u, self.n = self.q1.shape[0], self.core.shape[3], self.q1.shape[2]
        self.r = self.u // place.groups
        self.first, self.second = pl.ds(0, self.u // 2), pl.ds(self.u // 2, self.u // 2)

    def wire(self, k):
        p, i = self.p, self.i
        if k == 0:
            src, dst, to = self.part.at[:, :, :, 1 - p.c], self.core, p.to_c
        elif k == 1:
            src, dst, to = self.core.at[:, :, 1 - p.x, self.first], self.r1, p.to_x
        elif k == 2:
            src, dst, to = self.core.at[:, 1 - p.y, :, self.second], self.r2, p.to_y
        elif k == 3:
            src, dst, to = self.r1.at[:, 1 - p.y], self.q1, p.to_y
        elif k == 4:
            src, dst, to = self.r2.at[:, 1 - p.x], self.q2, p.to_x
        elif k < 8:
            z = (p.z + k - 4) % 4
            src, dst, to = self.zs.at[:, z], self.zr.at[k - 5], p.to_z(z)
        else:
            z = 1 + p.z // 3
            src, dst, to = self.zs.at[:, 3 - p.z], self.zr.at[3], p.to_z(z)
        return remote(src, dst, self.send.at[i, k], self.recv.at[i, k], to)

    def start(self):
        self.wire(0).start()

    def core_add(self):
        p = self.p
        self.wire(0).wait_recv()
        for k in range(self.k):
            for y in range(2):
                for x in range(2):
                    here = self.core.at[k, y, x]
                    here[...] = here[...] + self.part[k, y, x, p.c]
        self.wire(1).start()
        self.wire(2).start()

    def pass_x(self):
        p = self.p
        self.wire(1).wait_recv()
        for k in range(self.k):
            here = self.r1.at[k, 1 - p.y]
            here[...] = here[...] + self.core[k, 1 - p.y, p.x, self.first, :]
        self.wire(3).start()

    def pass_y(self):
        p = self.p
        self.wire(2).wait_recv()
        for k in range(self.k):
            here = self.r2.at[k, 1 - p.x]
            here[...] = here[...] + self.core[k, p.y, 1 - p.x, self.second, :]
        self.wire(4).start()

    def z_start(self):
        p, r = self.p, self.r
        half = self.u // 2
        self.wire(3).wait_recv()
        self.wire(4).wait_recv()
        per = p.groups // 2
        for k in range(self.k):
            for h in range(2):
                mine = self.r1.at[k, p.y] if h == 0 else self.r2.at[k, p.x]
                got = self.q1.at[k] if h == 0 else self.q2.at[k]
                value = self.core[k, p.y, p.x, pl.ds(h * half, half), :].astype(f32)
                value += mine[...].astype(f32) + got[...].astype(f32)
                slabs = value.reshape(per, r, self.n)
                self.zs[k, pl.ds(h * per, per)] = slabs.astype(bf16)
        pl.when(p.z < 3)(lambda: self.wire(5).start())
        pl.when(p.z > 0)(lambda: self.wire(7).start())

        @pl.when(jnp.logical_not(p.inner))
        def _():
            self.wire(6).start()
            self.wire(8).start()

    def z_pass(self):
        @pl.when(self.p.inner)
        def _():
            self.wire(8).wait_recv()
            z = (self.p.z + 2) % 4
            for k in range(self.k):
                self.zs[k, z] = self.zs[k, z] + self.zr[3, k]
            self.wire(6).start()

    def finish(self):
        p = self.p
        self.wire(6).wait_recv()
        for k in range(self.k):
            self.out[k][...] = self.zs[k, p.z].astype(f32) + self.zr[1, k].astype(f32)

        def more(wire, slot):
            self.wire(wire).wait_recv()
            for k in range(self.k):
                self.out[k][...] += self.zr[slot, k].astype(f32)

        pl.when(p.z > 0)(lambda: more(5, 0))
        pl.when(p.z < 3)(lambda: more(7, 2))

    def drain(self):
        p = self.p
        for k in (0, 1, 2, 3, 4, 6):
            self.wire(k).wait_send()
        pl.when(p.z < 3)(lambda: self.wire(5).wait_send())
        pl.when(p.z > 0)(lambda: self.wire(7).wait_send())
        pl.when(jnp.logical_not(p.inner))(lambda: self.wire(8).wait_send())


class Tally:
    def __init__(self, place, value, got, send, recv):
        self.p, self.value, self.got, self.send, self.recv = place, value, got, send, recv

    def copy(self, k):
        p = self.p
        to = (p.to_c, p.to_x, p.to_y)[k] if k < 3 else p.to_z(p.ahead(k - 2))
        return remote(
            self.value.at[min(k, 3)], self.got.at[k], self.send.at[k], self.recv.at[k], to
        )

    def start(self):
        self.copy(0).start()

    def step(self, k):
        self.copy(k).wait_recv()
        self.value[k + 1] = self.value[k] + self.got[k]
        if k < 2:
            self.copy(k + 1).start()
        else:
            for j in range(1, self.p.groups):
                self.copy(2 + j).start()

    def finish(self):
        value = self.value[3]
        for j in range(1, self.p.groups):
            self.copy(2 + j).wait_recv()
            value += self.got[2 + j]
        for k in range(2 + self.p.groups):
            self.copy(k).wait_send()
        return value


def normalize(v):
    mean = jnp.mean(v, axis=1, keepdims=True)
    centred = v - mean
    inv = lax.rsqrt(jnp.mean(centred * centred, axis=1, keepdims=True) + epsilon)
    return centred * inv, mean, inv


def norm_backward(grad, hat, inv, gain):
    t = grad * gain
    mean_t = jnp.mean(t, axis=1, keepdims=True)
    mean_th = jnp.mean(t * hat, axis=1, keepdims=True)
    return inv * (t - mean_t - hat * mean_th)


class Layer:
    def __init__(self, place, refs):
        self.__dict__.update(refs)
        self.p = place
        self.rows, self.d = self.x.shape
        self.hidden = self.act.shape[1]
        self.step = 96

    def vec(self, i):
        return self.vecs[i : i + 1, :]

    def weight(self, i, cols=slice(None)):
        value = self.w[i, :, :, :, :, cols]
        return value.reshape(self.d, value.shape[-1])

    def eighths(self, value):
        return value.reshape(2, 2, 2, value.shape[0] // 8, value.shape[1])

    def vectors(self):
        d, groups = self.d, self.p.groups
        per = d // (8 * groups)
        wide = self.hidden // (8 * groups)

        def spread(lanes, cols, width):
            lane = lax.broadcasted_iota(jnp.int32, (lanes, cols), 0)
            col = lax.broadcasted_iota(jnp.int32, (lanes, cols), 1)
            hit = (col == lane // 128 * width + lane % 128) & (lane % 128 < width)
            return jnp.where(hit, 1.0, 0.0).astype(bf16)

        half = spread(4 * groups * 128, d // 2, per)
        for h in range(2):
            slabs = [self.small[4 * h + b, z] for b in range(4) for z in range(groups)]
            self.vecs[:, h * (d // 2) : (h + 1) * (d // 2)] = nn(jnp.concatenate(slabs, 1), half)
        one = spread(groups * 128, groups * wide, wide)
        for b in range(8):
            slabs = [self.small[b, z] for z in range(groups)]
            row = nn(jnp.concatenate(slabs, 1), one)[10:11, :]
            self.b_up[:, b * groups * wide : (b + 1) * groups * wide] = row

    def mask(self, lengths, script_ids, key_mask):
        strips, length = key_mask.shape
        home = jnp.clip(self.p.z - self.p.c, 0, strips - 1)
        keys = jnp.zeros((1, length), jnp.int32)
        for s in range(strips):
            keys = jnp.where(home == s, key_mask[s : s + 1, :], keys)
        pos = lax.broadcasted_iota(jnp.int32, (1, length), 1)
        good = (pos == 0) | ((pos < lengths[home]) & (keys == 1))
        good = jnp.broadcast_to(jnp.where(good, 1.0, 0.0), (8, length)).astype(bf16)
        real = length // self.p.groups
        padded = self.rows // self.p.groups
        row = lax.broadcasted_iota(jnp.int32, (self.rows, length), 0)
        col = lax.broadcasted_iota(jnp.int32, (self.rows, length), 1)
        hit = (col == row // padded * real + row % padded) & (row % padded < real)
        self.valid[...] = nt(jnp.where(hit, 1.0, 0.0).astype(bf16), good)[:, 0:1]
        self.sid = script_ids[home]

    def norm1(self):
        self.emb[...] = jnp.where(self.sid == 1, self.vec(T1), self.vec(T0))

        def body(i):
            at = ds(i * self.step, self.step)
            hat, mean, inv = normalize(self.x[at, :].astype(f32) + self.emb[...])
            self.stats[at, 0:1] = mean
            self.stats[at, 1:2] = inv
            self.h1[at, :] = (hat * self.vec(G1) + self.vec(B1)).astype(bf16)

        loop(self.rows // self.step, body)

    def project(self, i, n=768):
        d = self.d

        def body(k):
            at = ds(k * n, n, 128)
            value = nn(self.h1[...], self.weight(QKV + i, at))
            if i != 1:
                value = value + self.vecs[QB if i == 0 else VB : (QB if i == 0 else VB) + 1, at]
            self.qkv[:, ds(i * d + k * n, n, 128)] = value.astype(bf16)

        loop(d // n, body)

    def half(self, h, value):
        lane = lax.broadcasted_iota(jnp.int32, value.shape, 1)
        return jnp.where(lane // DH == h, value, jnp.zeros_like(value))

    def pick(self, a, b):
        lane = lax.broadcasted_iota(jnp.int32, a.shape, 1)
        return jnp.where(lane < DH, a, b)

    def lanes(self, p):
        return [ds(i * self.d + p * 128, 128, 128) for i in range(3)]

    def probs_out(self, p):
        slot = p % 2
        return pltpu.make_async_copy(self.probs.at[slot], self.kept.at[p], self.out_sem.at[slot])

    def probs_in(self, p):
        slot = p % 2
        return pltpu.make_async_copy(self.kept.at[p], self.probs.at[slot], self.in_sem.at[slot])

    def attend(self, p):
        aq, ak, av = self.lanes(p)
        q = self.qkv[:, aq] * jnp.asarray(DH**-0.5, bf16)
        k, v = self.qkv[:, ak], self.qkv[:, av]
        valid = self.valid[...] > 0
        turned = v.T

        @pl.when(p >= 2)
        def _():
            self.probs_out(p - 2).wait()

        contexts = []
        for h in range(2):
            s = nt(k, self.half(h, q))
            s = jnp.where(valid, s, -1e9)
            e = jnp.exp(s - jnp.max(s, axis=0, keepdims=True))
            probs = (e * (1.0 / total(e))).astype(bf16)
            self.probs[p % 2, h] = probs
            contexts.append(nn(turned[h * DH : (h + 1) * DH], probs))
        self.ctx[:, ds(p * 128, 128, 128)] = jnp.concatenate(contexts, axis=0).T.astype(bf16)
        self.probs_out(p).start()

    def mid_norm(self, n=768):
        def body(k):
            at = ds(k * n, n, 128)
            self.mid[:, at] = nn(self.ctx[...], self.weight(OUT, at))

        loop(self.d // n, body)

        def norm(i):
            at = ds(i * self.step, self.step)
            v = self.x[at, :].astype(f32) + self.emb[...] + (self.mid[at, :] + self.vec(OB))
            self.mid[at, :] = v
            hat, mean, inv = normalize(v)
            self.stats[at, 2:3] = mean
            self.stats[at, 3:4] = inv
            self.h2[at, :] = (hat * self.vec(G2) + self.vec(B2)).astype(bf16)

        loop(self.rows // self.step, norm)

    def mlp_up(self, j, n=768):
        def body(k):
            at = ds(j * self.d + k * n, n, 128)
            pre = nn(self.h2[...], self.weight(UP + j, ds(k * n, n, 128))) + self.b_up[:, at]
            cum = 0.5 * (1.0 + lax.erf(pre * 2.0**-0.5))
            den = jnp.exp(-0.5 * pre * pre) * (2.0 * jnp.pi) ** -0.5
            self.act[:, at] = (pre * cum).astype(bf16)
            self.slope[:, at] = (cum + pre * den).astype(bf16)

        loop(self.d // n, body)

    def dw_down(self, b):
        u = self.hidden // 4
        grad = tn(self.act[:, ds(b * u, u, 128)], self.cot[...])
        self.p_down[0, b // 2, b % 2] = grad.reshape(2, u // 2, self.d).astype(bf16)

    def grad_pre(self, b):
        u = self.hidden // 4
        at = ds(b * u, u, 128)
        w = self.w_down[b // 2, b % 2].reshape(u, self.d)
        g = (nt(self.cot[...], w) * self.slope[:, at].astype(f32)).astype(bf16)
        self.slope[:, at] = g
        self.up_sums[:, at] = total(g.astype(f32))

    def mlp_down(self):
        m = self.rows // 2

        def body(i):
            at = ds(i * m, m)
            value = self.mid[at, :] + self.vec(DB)
            for k in range(self.hidden // self.d):
                w = self.w_down[k // 2, k % 2].reshape(self.d, self.d)
                value = value + nn(self.act[at, pl.ds(k * self.d, self.d)], w)
            self.out[at, :] = value.astype(bf16)

        loop(2, body)

    def grad_h2(self, j):
        m = self.rows

        def body(i):
            at = ds(i * m, m)
            value = nt(self.slope[at, ds(j * self.d, self.d, 128)], self.weight(UP + j))
            if j == 0:
                self.wide[at, :] = value
            else:
                self.wide[at, :] += value

        loop(1, body)

    def dw_up(self, j, n=768):
        def body(k):
            grad = tn(self.h2[...], self.slope[:, ds(j * self.d + k * n, n, 128)])
            self.w[UP + j, :, :, :, :, ds(k * n, n, 128)] = self.eighths(grad).astype(bf16)

        loop(self.d // n, body)

    def back2(self):
        zero = jnp.zeros((1, self.d), f32)

        def body(i, sums):
            at = ds(i * self.step, self.step)
            inv = self.stats[at, 3:4]
            hat = (self.mid[at, :] - self.stats[at, 2:3]) * inv
            g = self.wide[at, :]
            cot = self.cot[at, :].astype(f32)
            value = cot + norm_backward(g, hat, inv, self.vec(G2))
            self.mid[at, :] = value
            low = value.astype(bf16)
            self.gb[at, :] = low
            terms = (g * hat, g, cot, low.astype(f32))
            return tuple(s + total(t) for s, t in zip(sums, terms))

        sums = lax.fori_loop(0, self.rows // self.step, body, (zero,) * 4)
        for row, s in zip((G2, B2, DB, OB), sums):
            self.sums[row : row + 1, :] = s

    def grad_ctx(self):
        m = self.rows

        def body(i):
            at = ds(i * m, m)
            self.gctx[at, :] = nt(self.gb[at, :], self.weight(OUT)).astype(bf16)

        loop(1, body)

    def dw_out(self, n=768):
        def body(k):
            at = ds(k * n, n, 128)
            grad = tn(self.ctx[...], self.gb[:, at])
            self.w[OUT, :, :, :, :, at] = self.eighths(grad).astype(bf16)

        loop(self.d // n, body)

    def attend_back(self, p, last):
        aq, ak, av = self.lanes(p)
        q, k, v = self.qkv[:, aq], self.qkv[:, ak], self.qkv[:, av]
        g = self.gctx[:, aq]

        @pl.when(p + 1 < last)
        def _():
            self.probs_in(p + 1).start()

        self.probs_in(p).wait()
        turned = k.T
        dq, dk, dv = [], [], []
        for h in range(2):
            probs = self.probs[p % 2, h]
            dv.append(nn(probs, g))
            grad = nt(v, self.half(h, g))
            wide = probs.astype(f32)
            grad = (wide * (grad - total(wide * grad))).astype(bf16)
            dk.append(nn(grad, q))
            dq.append(nn(turned[h * DH : (h + 1) * DH], grad))
        dq = (jnp.concatenate(dq, axis=0).T * DH**-0.5).astype(bf16)
        dv = self.pick(*dv).astype(bf16)
        self.qkv[:, aq] = dq
        self.qkv[:, ak] = (self.pick(*dk) * DH**-0.5).astype(bf16)
        self.qkv[:, av] = dv
        self.sums[QB : QB + 1, aq] = total(dq.astype(f32))
        self.sums[VB : VB + 1, aq] = total(dv.astype(f32))

    def grad_h1(self, g, n=256):
        m = self.rows // 2

        def body(i):
            at = ds(i * m, m)
            value = None
            for k in range(3):
                w = self.weight(QKV + k, pl.ds(g * n, n))
                term = nt(self.qkv[at, pl.ds(k * self.d + g * n, n)], w)
                value = term if value is None else value + term
            if g == 0:
                self.wide[at, :] = value
            else:
                self.wide[at, :] += value

        loop(2, body)

    def dw_qkv(self, g, n=256):
        for k in range(3):
            grad = tn(self.h1[...], self.qkv[:, pl.ds(k * self.d + g * n, n)])
            self.w[QKV + k, :, :, :, :, pl.ds(g * n, n)] = self.eighths(grad).astype(bf16)

    def back1(self):
        zero = jnp.zeros((1, self.d), f32)

        def body(i, sums):
            at = ds(i * self.step, self.step)
            inv = self.stats[at, 1:2]
            hat = (self.x[at, :].astype(f32) + self.emb[...] - self.stats[at, 0:1]) * inv
            g = self.wide[at, :]
            value = self.mid[at, :] + norm_backward(g, hat, inv, self.vec(G1))
            self.gx[at, :] = value.astype(bf16)
            return tuple(s + total(t) for s, t in zip(sums, (g * hat, g, value)))

        sums = lax.fori_loop(0, self.rows // self.step, body, (zero,) * 3)
        self.sums[G1 : G1 + 1, :] = sums[0]
        self.sums[B1 : B1 + 1, :] = sums[1]
        self.sums[T0 : T0 + 1, :] = jnp.where(self.sid == 1, 0.0, sums[2])
        self.sums[T1 : T1 + 1, :] = jnp.where(self.sid == 1, sums[2], 0.0)


def pack(r):
    slab = r["s_small"]
    rows = [r[f"vec{i}"][...].astype(f32) for i in range(10)]
    rows = [jnp.pad(v, ((0, 0), (0, 128 - v.shape[1]))) for v in rows]
    slab[...] = jnp.concatenate(rows + [jnp.zeros((5, 128), f32)], axis=0).astype(bf16)


def kernel(outer, groups, names, *refs):
    r = dict(zip(names, refs, strict=True))
    p = Place(outer, groups)
    L = Layer(p, r)
    d, hidden = L.d, L.hidden
    nh = hidden // d
    real = r["patches"].shape[1]
    strips = r["patches"].shape[0]
    per = d // (8 * groups)
    u = d // 8
    n_down = d // 256
    w, w_down, stage = r["w"], r["w_down"], r["stage"]

    gs = []

    def add(shard, block, part, land, settle=None):
        gs.append(
            Gather(
                p, len(gs), shard, block, part, land, r["g_send"], r["g_recv"], r["g_here"], settle
            )
        )

    add(
        r["s_small"],
        lambda y, x, c: r["small"].at[y * 4 + x * 2 + c],
        lambda ref, h: ref.at[pl.ds(h * (groups // 2), groups // 2)],
        lambda z: r["small"].at[p.y * 4 + p.x * 2 + p.c, z],
    )

    def add_square(i, shard):
        def settle(block):
            block[...] = stage[i].astype(f32).reshape(u, d).astype(bf16)

        add(
            shard,
            lambda y, x, c: w.at[i, y, x, c],
            lambda ref, h: ref.at[pl.ds(h * (u // 2), u // 2)],
            lambda z: stage.at[i, z],
            settle,
        )

    for i in range(3):
        add_square(QKV + i, r["s_qkv"].at[:, pl.ds(i * d, d)])
    add_square(OUT, r["s_out"])
    for i in range(nh):
        add_square(UP + i, r["s_up"].at[:, pl.ds(i * d, d)])
    hu = hidden // 8
    hr = hu // groups
    for i in range(n_down):
        cols = pl.ds(i * 256, 256)
        add(
            r["s_down"].at[:, cols],
            lambda y, x, c, cols=cols: w_down.at[y, x, c, :, cols],
            lambda ref, h: ref.at[pl.ds(h * (hu // 2), hu // 2)],
            lambda z, cols=cols: w_down.at[p.y, p.x, p.c, ds(z * hr, hr), cols],
        )
    xs = Rows(p, r["xp"], r["x"], r["x_send"], r["x_recv"])
    cs = Rows(p, r["cp"], r["cot"], r["c_send"], r["c_recv"])

    ss = []

    def give(part, bufs, out):
        ss.append(Scatter(p, len(ss), part, bufs, out, r["s_send"], r["s_recv"]))

    def bufs(kind, i):
        found = [r[f"{kind}_{name}"].at[i] for name in ("core", "r1", "r2", "q1", "q2")]
        if kind == "flat":
            slot = stage.at[pl.ds(UP + i if i < nh else OUT, 1)]
        elif kind == "head":
            slot = stage.at[pl.ds(QKV, 3), :, :, pl.ds(i * 256, 256)]
        else:
            slot = r["tall_zs"].at[i]
        return found + [slot, r[f"{kind}_zr"].at[i]]

    for i in range(n_down):
        cols = pl.ds(i * 256, 256)
        give(r["p_down"].at[:, :, :, :, :, cols], bufs("tall", i), [r["o_down"].at[:, cols]])
    for i in range(nh):
        give(w.at[pl.ds(UP + i, 1)], bufs("flat", i), [r["o_up"].at[:, pl.ds(i * d, d)]])
    give(w.at[pl.ds(OUT, 1)], bufs("flat", nh), [r["o_out"]])
    for g in range(d // 256):
        cols = pl.ds(g * 256, 256)
        outs = [r["o_qkv"].at[:, pl.ds(k * d + g * 256, 256)] for k in range(3)]
        give(w.at[pl.ds(QKV, 3), :, :, :, :, cols], bufs("head", g), outs)

    ys = Rows(p, r["o_out_rows"], r["out"], r["y_send"], r["y_recv"])
    rs = Rows(p, r["o_grad_rows"], L.gx, r["d_send"], r["d_recv"])
    ts = Tally(p, r["value"], r["got"], r["t_send"], r["t_recv"])

    ends = {X_IN: xs, C_IN: cs, Y_OUT: ys, R_OUT: rs}
    gather = {SMALL: 0, WQ: 1, WK: 2, WV: 3, WO: 4, WU: 5, WD: 5 + nh}
    scatter = {GD: 0, GU: n_down, GO: n_down + nh, GQ: n_down + nh + 1}
    pairs = d // 128

    fetch = [
        pltpu.make_async_copy(r[a], r["pin"], r["arg_sem"].at[i])
        for i, a in enumerate(("patches", "cotangent"))
    ]
    fetch[0].start()

    def lay(dst):
        dst[...] = jnp.zeros_like(dst)
        for s in range(strips):
            dst[s, :real] = r["pin"][s]

    def prepare():
        fetch[0].wait()
        lay(r["xp"])
        fetch[1].start()
        xs.in_local()

    def mask():
        L.mask(r["lengths"], r["script_ids"], r["key_mask"])
        fetch[1].wait()
        lay(r["cp"])
        cs.in_local()

    def sent():
        for g in gs:
            g.sent()
        cs.in_sent()

    def context_end():
        for i in (pairs - 2, pairs - 1):
            L.probs_out(i).wait()
        L.mid_norm()

    def rows_done():
        L.back1()
        r["sums"][10:16, :] = jnp.concatenate(
            [L.up_sums[:, j * d : (j + 1) * d] for j in range(nh)]
            + [jnp.zeros((6 - nh, d), f32)]
        )
        r["value"][0] = r["sums"][...]
        ts.start()

    def context_grad():
        L.grad_ctx()
        L.probs_in(0).start()

    once = {
        PREP: prepare, MASK: mask,
        VEC: L.vectors, NORM1: L.norm1, MID: context_end, DOWN: L.mlp_down, BACK2: L.back2,
        GCTX: context_grad, DWOUT: L.dw_out, BACK1: rows_done, SENT: sent,
        SENTX: xs.in_sent,
    }
    counted = {
        PROJ: L.project, UP_: L.mlp_up, GU_: L.grad_h2, DWUP: L.dw_up, GQ_: L.grad_h1,
        DWQKV: L.dw_qkv, T: ts.step,
    }
    looped = {
        ATT: L.attend, DWDOWN: L.dw_down, GPRE: L.grad_pre,
        ATTB: lambda i: L.attend_back(i, pairs),
    }

    def act(step):
        kind, name, i = step
        if kind == ROW:
            ends[name].in_start(i)
        elif kind == IN:
            ends[name].in_finish()
        elif kind == OUT_:
            ends[name].out_start()
        elif name in gather:
            g = gs[gather[name] + i]
            {
                ZS: g.z_start, ZF: g.z_far, ZE: g.z_end, FIN: g.finish,
                MX: lambda: g.pass_on(3, 6, 8), MY: lambda: g.pass_on(4, 5, 9),
                DX: lambda: g.pass_on(6, None, 10), DY: lambda: g.pass_on(5, None, 11),
            }[kind]()
        else:
            s = ss[scatter[name] + i]
            {
                ST: s.start, CA: s.core_add, PX: s.pass_x, PY: s.pass_y, ZT: s.z_start,
                ZP: s.z_pass, FI: s.finish,
            }[kind]()

    pack(r)
    p.greet()
    steps = list(SCHEDULE)
    while steps:
        kind, name, first = steps.pop(0)
        if name:
            act((kind, name, first))
        elif kind in once:
            once[kind]()
        elif kind in counted:
            counted[kind](first)
        else:
            n, between = 1, {}
            while True:
                k = 0
                while k < len(steps) and steps[k][1]:
                    k += 1
                if k == len(steps) or steps[k] != (kind, 0, first + n):
                    break
                between[n - 1] = steps[:k]
                steps = steps[k + 1 :]
                n += 1

            def body(i):
                looped[kind](first + i)
                for at, some in between.items():
                    if some:

                        @pl.when(i == at)
                        def _():
                            for step in some:
                                act(step)

            if n == 1:
                body(0)
            else:
                loop(n, body)

    ys.out_finish()
    r["o_tally"][...] = ts.finish()
    rs.out_finish()
    for s in ss:
        s.drain()


def on_device(outer, groups, *args):
    (patches, cotangent, lengths, script_ids, key_mask, norm1_gain, norm1_bias, w_qkv, q_bias,
     v_bias, w_attn_out, attn_out_bias, norm2_gain, norm2_bias, w_up, up_bias, w_down, down_bias,
     script_table) = args
    strips, part_rows, d = patches.shape
    hidden = w_up.shape[1]
    parts = 8 * groups
    pad_rows = round_up(part_rows, 16)
    rows = groups * pad_rows
    vectors = [norm1_gain, norm1_bias, q_bias, v_bias, attn_out_bias, norm2_gain, norm2_bias,
               down_bias]
    weights = [w_qkv, w_attn_out, w_up, w_down]
    if outer > 1:
        mates = [[g * outer + i for i in range(outer)] for g in range(8)]
        seq = lax.axis_index("seq")

        def widen(a):
            a = lax.all_gather(a, ("seq",), axis=0, tiled=True)
            a = lax.all_gather(a, "dp", axis=0, tiled=True, axis_index_groups=mates)
            n = a.shape[0] // groups
            return lax.dynamic_slice_in_dim(a, seq * n, n, axis=0)

        vectors = [widen(a) for a in vectors]
        script_table = widen(script_table.T).T
        up_bias = widen(up_bias)
        weights = [widen(a) for a in weights]
    vectors = [v[None] for v in vectors] + [script_table, up_bias[None]]
    vm = pl.BlockSpec(memory_space=pltpu.VMEM)
    sm = pl.BlockSpec(memory_space=pltpu.SMEM)
    anywhere = pl.BlockSpec(memory_space=pl.ANY)
    sems = pltpu.SemaphoreType.DMA
    nh = hidden // d
    u, r, nd, ng = d // 8, d // parts, d // 256, d // 256
    ins = [f"vec{i}" for i in range(10)] + ["s_qkv", "s_out", "s_up", "s_down", "patches", "cotangent", "key_mask",
           "lengths", "script_ids"]
    outs = {
        "o_qkv": ((r, 3 * d), f32),
        "o_out": ((r, d), f32),
        "o_up": ((r, hidden), f32),
        "o_down": ((hidden // parts, d), f32),
        "o_tally": ((16, d), f32),
        "o_out_rows": ((strips, pad_rows, d), bf16),
        "o_grad_rows": ((strips, pad_rows, d), bf16),
        "kept": ((d // 128, 2, rows, rows), bf16),
    }
    scratch = {
        "small": ((8, groups, 16, 128), bf16),
        "s_small": ((16, 128), bf16),
        "stage": ((4 + nh, groups, r, d), bf16),
        "w": ((4 + nh, 2, 2, 2, u, d), bf16),
        "w_down": ((2, 2, 2, hidden // 8, d), bf16),
        "p_down": ((1, 2, 2, 2, hidden // 8, d), bf16),
        "pin": (patches.shape, bf16),
        "xp": ((strips, pad_rows, d), bf16),
        "cp": ((strips, pad_rows, d), bf16),
        "x": ((rows, d), bf16),
        "cot": ((rows, d), bf16),
        "valid": ((rows, 1), f32),
        "vecs": ((16, d), f32),
        "b_up": ((1, hidden), f32),
        "up_sums": ((1, hidden), f32),
        "sums": ((16, d), f32),
        "emb": ((1, d), f32),
        "stats": ((rows, 4), f32),
        "h1": ((rows, d), bf16),
        "qkv": ((rows, 3 * d), bf16),
        "probs": ((2, 2, rows, rows), bf16),
        "ctx": ((rows, d), bf16),
        "mid": ((rows, d), f32),
        "wide": ((rows, d), f32),
        "h2": ((rows, d), bf16),
        "act": ((rows, hidden), bf16),
        "slope": ((rows, hidden), bf16),
        "value": ((4, 16, d), f32),
        "got": ((2 + groups, 16, d), f32),
    }
    for kind, count, k, uu, n in (
        ("tall", nd, 1, hidden // 8, 256),
        ("flat", nh + 1, 1, u, d),
        ("head", ng, 3, u, 256),
    ):
        rr = uu // groups
        scratch[f"{kind}_core"] = ((count, k, 2, 2, uu, n), bf16)
        scratch[f"{kind}_r1"] = ((count, k, 2, uu // 2, n), bf16)
        scratch[f"{kind}_r2"] = ((count, k, 2, uu // 2, n), bf16)
        scratch[f"{kind}_q1"] = ((count, k, uu // 2, n), bf16)
        scratch[f"{kind}_q2"] = ((count, k, uu // 2, n), bf16)
        if kind == "tall":
            scratch["tall_zs"] = ((count, k, groups, rr, n), bf16)
        scratch[f"{kind}_zr"] = ((count, groups, k, rr, n), bf16)
    n_gather = 5 + nh + nd
    n_scatter = nd + nh + 1 + ng
    semaphores = {
        "g_send": (n_gather, WIRE), "g_recv": (n_gather, WIRE),
        "s_send": (n_scatter, HOPS), "s_recv": (n_scatter, HOPS),
        "t_send": (2 + groups,), "t_recv": (2 + groups,),
        "out_sem": (2,), "in_sem": (2,), "g_here": (n_gather,), "arg_sem": (2,),
    }
    for name in "xcyd":
        shape = (groups,) if name in "yd" else (d // 256, groups - 1)
        semaphores[f"{name}_send"] = shape
        semaphores[f"{name}_recv"] = shape
    names = ins + list(outs) + list(scratch) + list(semaphores)

    def body(*refs):
        refs = dict(zip(names, refs, strict=True))
        act = refs["act"]
        for k, name in enumerate(("out", "gb", "gctx", "gx")):
            refs[name] = act.at[:, pl.ds(k * d, d)]
        kernel(outer, groups, list(refs), *refs.values())

    res = pl.pallas_call(
        body,
        out_shape=[jax.ShapeDtypeStruct(*s) for s in outs.values()],
        in_specs=[vm] * 10 + [anywhere] * 6 + [vm] + [sm] * 2,
        out_specs=[vm] * 5 + [anywhere] * 3,
        scratch_shapes=[pltpu.VMEM(*s) for s in scratch.values()]
        + [sems(s) for s in semaphores.values()],
        compiler_params=pltpu.CompilerParams(
            collective_id=0, has_side_effects=True, vmem_limit_bytes=63 * 2**20
        ),
    )(*vectors, *weights, patches, cotangent, key_mask, lengths, script_ids)
    shards = list(res[:4])
    tally = res[4]
    if outer > 1:

        def narrow(a):
            a = lax.psum(a, "dp", axis_index_groups=mates)
            a = lax.all_gather(a, ("seq",), axis=0, tiled=True)
            at = (lax.axis_index("dp") % outer) * groups + lax.axis_index("seq")
            n = a.shape[0] // groups // outer
            return lax.dynamic_slice_in_dim(a, at * n, n, axis=0)

        shards = [narrow(a) for a in shards]
        tally = lax.psum(tally, "dp", axis_index_groups=mates)
    n = d // (parts * outer)
    m = hidden // (parts * outer)
    passed = [res[5], res[6]] + (shards if outer == 1 else [])
    shapes = [patches.shape] * 2 + [a.shape for a in passed[2:]]
    closed = pl.pallas_call(
        functools.partial(close, groups, nh),
        out_shape=[jax.ShapeDtypeStruct((1, n), f32)] * 8
        + [jax.ShapeDtypeStruct((2, n), f32), jax.ShapeDtypeStruct((1, m), f32)]
        + [jax.ShapeDtypeStruct(n, a.dtype) for n, a in zip(shapes, passed, strict=True)],
        in_specs=[vm] * (1 + len(passed)),
        out_specs=[vm] * (10 + len(passed)),
    )(tally, *passed)
    vec = [v.reshape(n) for v in closed[:8]]
    table, vup = closed[8], closed[9].reshape(m)
    if outer == 1:
        shards = closed[12:]
    return (
        closed[10], closed[11], vec[G1], vec[B1], shards[0], vec[QB], vec[VB], shards[1], vec[OB],
        vec[G2], vec[B2], shards[2], vup, shards[3], vec[DB], table,
    )


def close(groups, nh, tally, *refs):
    n_passed = (len(refs) - 10) // 2
    passed, outs = refs[:n_passed], refs[n_passed:]
    for src, dst in zip(passed, outs[10:], strict=True):
        if len(src.shape) == 3:
            for s in range(src.shape[0]):
                dst[s] = src[s, : dst.shape[1]]
        else:
            dst[...] = src[...]
    me = lax.axis_index("dp") * groups + lax.axis_index("seq")
    d = tally.shape[1]
    n, m = outs[0].shape[1], outs[9].shape[1]
    mine = pltpu.roll(tally[...], lax.rem(d - me * n, d), 1)
    for i in range(8):
        outs[i][...] = mine[i : i + 1, :n]
    outs[8][...] = mine[T0 : T1 + 1, :n]
    row = jnp.zeros((8, d), f32)
    for i in range(nh):
        line = jnp.broadcast_to(tally[10 + i : 11 + i, :], (8, d))
        row = jnp.where(me * m // d == i, line, row)
    outs[9][...] = pltpu.roll(row, lax.rem(d - lax.rem(me * m, d), d), 1)[0:1, :m]


def solution(mesh):
    dp, seq = mesh.shape["dp"], mesh.shape["seq"]
    both = ("dp", "seq")
    one, two = P(both), P(both, None)
    rows = P("dp", "seq", None)
    return jax.shard_map(
        functools.partial(on_device, dp // 8, seq),
        mesh=mesh,
        in_specs=(
            rows, rows, P("dp"), P("dp"), P("dp", None), one, one, two, one, one, two, one, one,
            one, two, one, two, one, P(None, both),
        ),
        out_specs=(
            rows, rows, one, one, two, one, one, two, one, one, one, two, one, two, one,
            P(None, both),
        ),
        check_vma=False,
    )
```
